32 devices in a mesh: clip: 8 (over y, x, core), head: 4 (over z).
Axes of the slice: x: 2, y: 2, z: 4, core: 2. Of those that a mesh axis runs over, the one named last changes fastest.
Arguments:
- inputs: bfloat16 [6272, 768], P(('clip', 'head')), may hold values from -6 to 6
- ln1_gain: float32 [768], replicated, may hold values from 0.5 to 1.5
- ln1_bias: float32 [768], replicated, may hold values from -1.2 to 1.2
- w_qkv: bfloat16 [768, 2304], P(None, 'head'), may hold values from -0.21875 to 0.21875
- pool_kernel: float32 [8, 3, 27, 96], P('head'), may hold values from -1.75 to 1.75
- rel_table: float32 [8, 41, 96], P('head'), may hold values from -0.24 to 0.24
- comp_kernel: float32 [8, 2, 8, 96], P('head'), may hold values from -3.6 to 3.6
- memory_bank: bfloat16 [64, 2, 392, 768], P('clip', None, None, 'head'), may hold values from -6 to 6
- mem_index: int32 [16, 2], P('clip'), may hold values from 0 to 7
- clip_group: int32 [16], P('clip'), may hold values from 0 to 2
- w_proj: bfloat16 [768, 768], P('head'), may hold values from -0.21875 to 0.21875
- proj_bias: float32 [768], replicated, may hold values from -1.2 to 1.2
- ln2_gain: float32 [768], replicated, may hold values from 0.5 to 1.5
- ln2_bias: float32 [768], replicated, may hold values from -1.2 to 1.2
- w_up: bfloat16 [768, 3072], P(None, 'head'), may hold values from -0.21875 to 0.21875
- up_bias: float32 [3072], P('head'), may hold values from -1.2 to 1.2
- w_down: bfloat16 [3072, 768], P('head'), may hold values from -0.109375 to 0.109375
- down_bias: float32 [768], replicated, may hold values from -1.2 to 1.2
- cotangent: bfloat16 [6272, 768], P(('clip', 'head')), may hold values from -6 to 6
Outputs:
- output: bfloat16 [6272, 768], P(('clip', 'head'))
- grad_inputs: float32 [6272, 768], P(('clip', 'head'))
- grad_ln1_gain: float32 [768], replicated
- grad_ln1_bias: float32 [768], replicated
- grad_w_qkv: float32 [768, 2304], P(None, 'head')
- grad_pool_kernel: float32 [8, 3, 27, 96], P('head')
- grad_rel_table: float32 [8, 41, 96], P('head')
- grad_comp_kernel: float32 [8, 2, 8, 96], P('head')
- grad_w_proj: float32 [768, 768], P('head')
- grad_proj_bias: float32 [768], replicated
- grad_ln2_gain: float32 [768], replicated
- grad_ln2_bias: float32 [768], replicated
- grad_w_up: float32 [768, 3072], P(None, 'head')
- grad_up_bias: float32 [3072], P('head')
- grad_w_down: float32 [3072, 768], P('head')
- grad_down_bias: float32 [768], replicated
The draws below stay inside these ranges and needn't reach their ends.
Inputs may be any that keep to these rules, and one draw needn't show every extreme that they name: mem_index names rows of the memory bank held by the clip's own index of the clip axis. clip_group 0, 1, 2 selects memory stride 2, 4, 8.
All inputs are finite; a program needn't handle non-finite values.
Results may differ from the reference program's by a relative error of at most 0.02.
The reference program's roundings to bfloat16 on the way count: a program that leaves them out, or rounds other values in their place, can miss the bound.
Values may be sent and summed in bfloat16 or wider, within the bound.
No kernel may reach another device: no remote copies, remote signals or barrier semaphores. Data moves between devices by JAX's collectives and lax.ppermute only.
A program may use at most 256 MiB of HBM per device.

```python
import jax
import jax.numpy as jnp
from jax import lax

D = 768
HEADS = 8
FF = 3072
HEAD_DIM = 96
CLIP_DEV = 2
MEM_DEV = 8
CLIPS = 16
MEMS = 64
TOKENS = 6272
N_CLIP = 8


def with_ends(values, stream_key, smallest, high):
    index_at = [jax.random.randint(jax.random.fold_in(stream_key, axis), (), 0, length) for axis, length in enumerate(values.shape)]
    longest = values.shape.index(max(values.shape))
    beside = index_at[:longest] + [(index_at[longest] + 1) % values.shape[longest]] + index_at[longest + 1:]
    return values.at[tuple(index_at)].set(smallest).at[tuple(beside)].set(high)


def levels(stream_key, shape, pieces, low, high):
    factor_of = 1.0
    for axis_at, parts in pieces:
        heights = jax.random.uniform(jax.random.fold_in(jax.random.fold_in(stream_key, 6), axis_at), (parts,), jnp.float32, low / len(pieces), high / len(pieces))
        factor_of = factor_of * jnp.repeat(jnp.exp(heights), shape[axis_at] // parts).reshape((-1,) + (1,) * (len(shape) - 1 - axis_at))
    return factor_of


def centred(stream_key, extent, width, bound, pieces=(), kind=jnp.bfloat16):
    level = levels(stream_key, extent, pieces, -0.22, 0.18) if pieces else 1.0
    values = jax.random.normal(stream_key, extent, jnp.float32) * width * level
    return jnp.minimum(jnp.maximum(values, -bound), bound).astype(kind)


def setup_inputs(seed: int = 0) -> dict:
    key_of = jax.random.split(jax.random.key(seed), 20)
    inputs = centred(key_of[0], (TOKENS, D), 1.0, 6.0, ((0, 32),))
    ln1_gain = jnp.clip(1.0 + 0.1 * jax.random.normal(key_of[1], (D,), jnp.float32), 0.5, 1.5)
    ln1_bias = centred(key_of[2], (D,), 0.2, 1.2, (), jnp.float32)
    w_qkv = centred(key_of[3], (D, 3 * D), D ** -0.5, 0.21875, ((1, 4),))
    pool_kernel = centred(key_of[4], (HEADS, 3, 27, HEAD_DIM), 11 ** -0.5, 1.75, ((0, 4),), jnp.float32)
    rel_table = centred(key_of[5], (HEADS, 41, HEAD_DIM), 0.04, 0.24, ((0, 4),), jnp.float32)
    comp_kernel = centred(key_of[6], (HEADS, 2, 8, HEAD_DIM), 0.6, 3.6, ((0, 4),), jnp.float32)
    memory_bank = centred(key_of[7], (MEMS, 2, 392, D), 1.0, 6.0, ((0, 8), (3, 4)))
    mem_index = with_ends(jax.random.randint(key_of[8], (CLIPS, 2), 0, MEM_DEV), jax.random.fold_in(key_of[8], 1), 0, MEM_DEV - 1).astype(jnp.int32)
    clip_group = with_ends(jax.random.randint(key_of[9], (CLIPS,), 0, 3), jax.random.fold_in(key_of[9], 1), 0, 2).astype(jnp.int32)
    w_proj = centred(key_of[10], (D, D), D ** -0.5, 0.21875, ((0, 4),))
    proj_bias = centred(key_of[11], (D,), 0.2, 1.2, (), jnp.float32)
    ln2_gain = jnp.clip(1.0 + 0.1 * jax.random.normal(key_of[12], (D,), jnp.float32), 0.5, 1.5)
    ln2_bias = centred(key_of[13], (D,), 0.2, 1.2, (), jnp.float32)
    w_up = centred(key_of[14], (D, FF), D ** -0.5, 0.21875, ((1, 4),))
    up_bias = centred(key_of[15], (FF,), 0.2, 1.2, ((0, 4),), jnp.float32)
    w_down = centred(key_of[16], (FF, D), FF ** -0.5, 0.109375, ((0, 4),))
    down_bias = centred(key_of[17], (D,), 0.2, 1.2, (), jnp.float32)
    cotangent = centred(key_of[18], (TOKENS, D), 1.0, 6.0, ((0, 32),))
    return dict(inputs=inputs, ln1_gain=ln1_gain, ln1_bias=ln1_bias, w_qkv=w_qkv, pool_kernel=pool_kernel, rel_table=rel_table, comp_kernel=comp_kernel, memory_bank=memory_bank, mem_index=mem_index, clip_group=clip_group, w_proj=w_proj, proj_bias=proj_bias, ln2_gain=ln2_gain, ln2_bias=ln2_bias, w_up=w_up, up_bias=up_bias, w_down=w_down, down_bias=down_bias, cotangent=cotangent)


highest = lax.Precision.HIGHEST
eps_norm = 1e-06
neg_large = -1000000000.0

@jax.custom_vjp
def low(v):
    return lax.optimization_barrier(v.astype(jnp.bfloat16)).astype(jnp.float32)

@jax.custom_vjp
def low_back(v):
    return v

def low_keep(v):
    return (low(v), None)

def low_pass(kept, grad):
    return (grad,)

def back_keep(v):
    return (v, None)

def back_low(kept, grad):
    return (low(grad),)
low.defvjp(low_keep, low_pass)
low_back.defvjp(back_keep, back_low)

def layer_norm(values_in, gain_vec, shift_vec):
    row_mean = lax.optimization_barrier(jnp.mean(values_in, axis=-1, keepdims=True))
    centered = values_in - row_mean
    row_var = lax.optimization_barrier(jnp.mean(centered * centered, axis=-1, keepdims=True))
    return centered * lax.rsqrt(row_var + eps_norm) * gain_vec + shift_vec

def offsets(length_of, span_of, middle):
    places = jnp.arange(length_of)
    slots = jnp.arange(span_of)
    return (places[:, None, None] - places[None, :, None] + middle == slots[None, None, :]).astype(jnp.float32)

def pool_grid(field, kernel):
    padded = jnp.pad(field, ((0, 0), (1, 1), (1, 1), (1, 1), (0, 0), (0, 0), (0, 0)))
    total = jnp.zeros_like(field)
    for tap_index in range(27):
        shift_t = tap_index // 9
        shift_h = tap_index // 3 % 3
        shift_w = tap_index % 3
        total = total + padded[:, shift_t:shift_t + 8, shift_h:shift_h + 7, shift_w:shift_w + 7] * kernel[:, :, tap_index, :]
    return total

def rel_bias(queries, table):
    clip_count = queries.shape[0]
    head_count = queries.shape[2]
    projected = jnp.einsum('nqhd,hrd->nhqr', queries, table, precision=highest).reshape(clip_count, head_count, 8, 7, 7, 41)
    along_t = jnp.einsum('nhaber,akr->nhabek', projected[..., 0:15], offsets(8, 15, 7), precision=highest)
    along_h = jnp.einsum('nhaber,bkr->nhabek', projected[..., 15:28], offsets(7, 13, 6), precision=highest)
    along_w = jnp.einsum('nhaber,ekr->nhabek', projected[..., 28:41], offsets(7, 13, 6), precision=highest)
    total = along_t[..., :, None, None] + along_h[..., None, :, None] + along_w[..., None, None, :]
    return total.reshape(clip_count, head_count, 392, 392)

def stride_tables():
    out_frame = jnp.arange(4)[:, None, None]
    frames = jnp.arange(8)[None, :, None]
    tap_index = jnp.arange(8)[None, None, :]
    tables = []
    for section_level in range(3):
        stride = 2 ** (section_level + 1)
        allowed = (frames == stride * out_frame + tap_index) & (tap_index < stride) & (out_frame < 8 // stride)
        tables.append(allowed.astype(jnp.float32))
    return jnp.stack(tables)

def group_select(group_ids):
    return (group_ids[:, None] == jnp.arange(3)[None, :]).astype(jnp.float32)

def compress(bank, kernel, index_rows, group_ids):
    head_count = kernel.shape[0]
    head_size = kernel.shape[3]
    clip_count = index_rows.shape[0]
    chosen = jnp.take(bank, index_rows, axis=0).astype(jnp.float32).reshape(clip_count, 2, 2, 8, 49, head_count, head_size)
    pattern = jnp.einsum('ng,gtfj->ntfj', group_select(group_ids), stride_tables(), precision=highest)
    coeffs = jnp.einsum('ntfj,hkjd->nktfhd', pattern, kernel, precision=highest)
    packed = jnp.einsum('nktfhd,nmkfshd->knmtshd', coeffs, chosen, precision=highest)
    packed = packed.reshape(2, clip_count, 392, head_count, head_size)
    return (packed[0], packed[1])

def memory_valid(group_ids):
    clip_count = group_ids.shape[0]
    limits = lax.optimization_barrier(jnp.sum(group_select(group_ids) * jnp.array([4.0, 2.0, 1.0], dtype=jnp.float32), axis=-1))
    slot_pos = jnp.arange(4).astype(jnp.float32)
    allowed = slot_pos[None, :] < limits[:, None]
    return jnp.broadcast_to(allowed[:, None, :, None], (clip_count, 2, 4, 49)).reshape(clip_count, 392)

def gelu_exact(values_in):
    return jax.nn.gelu(values_in, approximate=False)

def layer_block(weights, block_in):
    ln1_gain, ln1_bias, w_qkv, pool_kernel, rel_table, comp_kernel, w_proj, proj_bias, ln2_gain, ln2_bias, w_up, up_bias, w_down, down_bias = weights
    token_rows, bank, index_rows, group_ids = block_in
    clip_count = group_ids.shape[0]
    head_count = pool_kernel.shape[0]
    head_size = pool_kernel.shape[3]
    score_scale = head_size ** (-0.5)
    norm1 = low(layer_norm(token_rows, ln1_gain, ln1_bias))
    qkv = low_back(jnp.dot(norm1, w_qkv, precision=highest))
    pooled = pool_grid(qkv.reshape(clip_count, 8, 7, 7, head_count, 3, head_size), pool_kernel)
    pooled = pooled.reshape(clip_count, 392, head_count, 3, head_size)
    queries = low(pooled[..., 0, :])
    key_part = low(pooled[..., 1, :])
    value_part = low(pooled[..., 2, :])
    mem_keys, mem_values = compress(bank, comp_kernel, index_rows, group_ids)
    all_keys = jnp.concatenate([key_part, low(mem_keys)], axis=1)
    all_values = jnp.concatenate([value_part, low(mem_values)], axis=1)
    scores = jnp.einsum('nqhd,nkhd->nhqk', queries, all_keys, precision=highest) * score_scale
    scores = jnp.concatenate([scores[..., :392] + rel_bias(queries, rel_table), scores[..., 392:]], axis=-1)
    scores = low_back(scores)
    key_mask = jnp.concatenate([jnp.ones((clip_count, 392), dtype=bool), memory_valid(group_ids)], axis=1)
    scores = jnp.where(key_mask[:, None, None, :], scores, neg_large)
    attn_probs = low(jax.nn.softmax(scores, axis=-1))
    attended = low_back(jnp.einsum('nhqk,nkhd->nqhd', attn_probs, all_values, precision=highest))
    head_out = low((attended + queries).reshape(clip_count * 392, head_count * head_size))
    branch = low_back(jnp.dot(head_out, w_proj, precision=highest) + proj_bias)
    midway = token_rows + branch
    norm2 = low(layer_norm(midway, ln2_gain, ln2_bias))
    hidden = low_back(jnp.dot(norm2, w_up, precision=highest) + up_bias)
    activated = low(gelu_exact(hidden))
    return midway + jnp.dot(activated, w_down, precision=highest) + down_bias

def reference(inputs, ln1_gain, ln1_bias, w_qkv, pool_kernel, rel_table, comp_kernel, memory_bank, mem_index, clip_group, w_proj, proj_bias, ln2_gain, ln2_bias, w_up, up_bias, w_down, down_bias, cotangent):
    weights = tuple((item.astype(jnp.float32) for item in (ln1_gain, ln1_bias, w_qkv, pool_kernel, rel_table, comp_kernel, w_proj, proj_bias, ln2_gain, ln2_bias, w_up, up_bias, w_down, down_bias)))
    rows_blocks = inputs.astype(jnp.float32).reshape(N_CLIP, CLIP_DEV * 392, D)
    bank_blocks = memory_bank.reshape(N_CLIP, MEM_DEV, 2, 392, D)
    index_blocks = mem_index.reshape(N_CLIP, CLIP_DEV, 2)
    group_blocks = clip_group.reshape(N_CLIP, CLIP_DEV)
    checked = jax.checkpoint(layer_block)

    def forward(rows_all, *params):
        return lax.map(lambda block_in: checked(params, block_in), (rows_all, bank_blocks, index_blocks, group_blocks))
    result, pullback = jax.vjp(forward, rows_blocks, *weights)
    grads = pullback(cotangent.astype(jnp.float32).reshape(N_CLIP, CLIP_DEV * 392, D))
    return (result.reshape(TOKENS, D).astype(jnp.bfloat16), grads[0].reshape(TOKENS, D), grads[1], grads[2], grads[3], grads[4], grads[5], grads[6], grads[7], grads[8], grads[9], grads[10], grads[11], grads[12], grads[13], grads[14])
```

```python
import functools

import jax
import jax.numpy as jnp
from jax import lax
from jax.experimental import pallas as pl
from jax.experimental.pallas import tpu as pltpu
from jax.sharding import PartitionSpec as P

f_type = jnp.float32
b_type = jnp.bfloat16
eps_norm = 1e-06
neg_large = -1000000000.0
clip_rows = 392
grid_rows = 448
slot_rows = 448
block_rows = 112
vmem_bytes = 56 * 1024 * 1024


def params():
    return pltpu.CompilerParams(vmem_limit_bytes=vmem_bytes)


def in_vmem(count):
    return [pl.BlockSpec(memory_space=pltpu.VMEM)] * count


def dot(a, b):
    return jnp.dot(a, b, preferred_element_type=f_type)


def dot_nt(a, b):
    return lax.dot_general(a, b, (((1,), (1,)), ((), ())), preferred_element_type=f_type)


def iota(shape, axis):
    return lax.broadcasted_iota(jnp.int32, shape, axis)


def one_hot(flag):
    return jnp.where(flag, 1.0, 0.0).astype(b_type)


def split(values):
    high = values.astype(b_type)
    return high, (values - high.astype(f_type)).astype(b_type)


def spread_matrix():
    row = iota((grid_rows, clip_rows), 0)
    token = iota((grid_rows, clip_rows), 1)
    place = row & 7
    return one_hot(((row >> 3) * 7 + place == token) & (place < 7))


def gather_matrix():
    row = iota((clip_rows, grid_rows), 1)
    token = iota((clip_rows, grid_rows), 0)
    place = row & 7
    return one_hot(((row >> 3) * 7 + place == token) & (place < 7))


def row_coords(shape, axis):
    row = iota(shape, axis)
    line = row >> 3
    frame = (line * 37) >> 8
    return frame, line - frame * 7, row & 7


def coord_of(kind, coords):
    frame, line, place = coords
    return jnp.where(kind == 0, frame, jnp.where(kind == 1, line, place))


def query_mask():
    shape = (grid_rows, 192)
    column = iota(shape, 1)
    coord = coord_of(column >> 6, row_coords(shape, 0))
    return jnp.where(((column >> 3) & 7) == coord, 1.0, 0.0)


def key_matrix():
    shape = (192, grid_rows)
    column = iota(shape, 0)
    coord = coord_of(column >> 6, row_coords(shape, 1))
    return one_hot((column & 7) == coord)


def table_slot(column):
    kind = column >> 6
    at_query = (column >> 3) & 7
    at_key = column & 7
    base = jnp.where(kind == 0, 7, jnp.where(kind == 1, 21, 34))
    valid = (kind == 0) | ((at_query < 7) & (at_key < 7))
    return jnp.where(valid, base + at_query - at_key, -1)


def table_matrix():
    return one_hot(table_slot(iota((192, 41), 0)) == iota((192, 41), 1))


def key_bias(limit):
    lane = iota((1, grid_rows), 1)
    own = jnp.where((lane & 7) == 7, neg_large, 0.0)
    group = jnp.zeros_like(lane)
    for step in range(1, 8):
        group = group + jnp.where(lane >= 56 * step, 1, 0)
    place = lane - 56 * group
    valid = (place < 49) & ((group & 3) < limit)
    return own, jnp.where(valid, 0.0, neg_large)


def clear_border(field):
    width = field.shape[-1]
    field[:, 0:1] = jnp.zeros((3, 1, 9, 8, width), f_type)
    field[:, 9:10] = jnp.zeros((3, 1, 9, 8, width), f_type)
    field[:, :, 0:1] = jnp.zeros((3, 10, 1, 8, width), f_type)
    field[:, :, 8:9] = jnp.zeros((3, 10, 1, 8, width), f_type)


def fill_field(field, values):
    width = values.shape[-1]
    lines = values.reshape(56, 8, width)
    field[0, 1:9, 1:8] = pltpu.roll(lines, 1, 1).reshape(8, 7, 8, width)
    field[1, 1:9, 1:8] = lines.reshape(8, 7, 8, width)
    field[2, 1:9, 1:8] = pltpu.roll(lines, 7, 1).reshape(8, 7, 8, width)


def convolve(field, taps, result, flip):
    width = field.shape[-1]
    for start in range(0, width, 128):
        lanes = slice(start, min(start + 128, width))

        def frame(t, carry):
            total = jnp.zeros((7, 8, lanes.stop - lanes.start), f_type)
            for dt in range(3):
                for dw in range(3):
                    near = field[dw, t + dt, :, :, lanes]
                    for dh in range(3):
                        tap = dt * 9 + dh * 3 + dw
                        tap = 26 - tap if flip else tap
                        total = total + near[dh : dh + 7] * taps[tap : tap + 1, lanes]
            result[t, :, :, lanes] = total
            return carry

        lax.fori_loop(0, 8, frame, 0)


def tap_grads(field, grads, result):
    width = field.shape[-1]
    for start in range(0, width, 128):
        lanes = slice(start, min(start + 128, width))
        size = lanes.stop - lanes.start

        def frame(t, sums):
            grad = grads[1, t + 1, 1:8, :, lanes]
            sums = list(sums)
            for dt in range(3):
                for dw in range(3):
                    near = field[dw, t + dt, :, :, lanes]
                    for dh in range(3):
                        tap = dt * 9 + dh * 3 + dw
                        sums[tap] = sums[tap] + jnp.sum(near[dh : dh + 7] * grad, axis=0)
            return tuple(sums)

        sums = lax.fori_loop(
            0, 8, frame, tuple(jnp.zeros((8, size), f_type) for _ in range(27))
        )
        for tap in range(27):
            result[tap : tap + 1, lanes] = jnp.sum(sums[tap], axis=0, keepdims=True)


def attend_kernel(
    heads,
    size,
    group_ref,
    tokens_ref,
    w_qkv_ref,
    taps_ref,
    table_ref,
    mem_ref,
    w_proj_ref,
    base_ref,
    out_ref,
    branch_ref,
    pooled_ref,
    probs_ref,
    field,
    pooled_wide,
    head_wide,
    rel_high,
    rel_low,
):
    scale = size ** (-0.5)
    clear_border(field)
    grid_tokens = dot(spread_matrix(), tokens_ref[...]).astype(b_type)
    fill_field(field, dot(grid_tokens, w_qkv_ref[...]))
    convolve(field, taps_ref, pooled_wide, False)
    pooled = pooled_wide[...].reshape(grid_rows, 3 * heads * size)
    filled = (iota((grid_rows, 1), 0) & 7) < 7
    pooled_ref[...] = jnp.where(filled, pooled, 0.0).astype(b_type)
    own_bias, mem_bias = key_bias(4 >> group_ref[0])
    expand = table_matrix()
    keys_at = key_matrix()
    for head in range(heads):
        at = 3 * head * size
        lanes = slice(head * size, (head + 1) * size)
        queries = pooled_ref[:, at : at + size]
        keys = pooled_ref[:, at + size : at + 2 * size]
        values = pooled_ref[:, at + 2 * size : at + 3 * size]
        mem_keys = mem_ref[0, :, lanes]
        mem_values = mem_ref[1, :, lanes]
        table_high, table_low = split(table_ref[head])
        rel = dot_nt(queries, dot(expand, table_high).astype(b_type)) + dot_nt(
            queries, dot(expand, table_low).astype(b_type)
        )
        high, low = split(rel * query_mask())
        rel_high[...] = high
        rel_low[...] = low

        def rows_step(step, carry, at=at, lanes=lanes, head=head, keys=keys, values=values,
                      mem_keys=mem_keys, mem_values=mem_values):
            rows = pl.ds(pl.multiple_of(step * block_rows, block_rows), block_rows)
            block = pooled_ref[rows, at : at + size]
            own = (
                dot_nt(block, keys) * scale
                + (dot(rel_high[rows, :], keys_at) + dot(rel_low[rows, :], keys_at))
                + own_bias
            )
            mem = dot_nt(block, mem_keys) * scale + mem_bias
            top = jnp.maximum(
                jnp.max(own, axis=-1, keepdims=True), jnp.max(mem, axis=-1, keepdims=True)
            )
            own = jnp.exp(own - top)
            mem = jnp.exp(mem - top)
            total = jnp.sum(own, axis=-1, keepdims=True) + jnp.sum(mem, axis=-1, keepdims=True)
            inverse = 1.0 / total
            own = own * inverse
            mem = mem * inverse
            probs_ref[head, 0, rows, :] = own
            probs_ref[head, 1, rows, :] = mem
            attended = dot(own.astype(b_type), values) + dot(mem.astype(b_type), mem_values)
            head_wide[rows, lanes] = attended + block.astype(f_type)
            return carry

        lax.fori_loop(0, grid_rows // block_rows, rows_step, 0)
    head_out = dot(gather_matrix(), head_wide[...].astype(b_type)).astype(b_type)
    out_ref[...] = head_out
    branch_ref[...] = base_ref[...] + dot(head_out, w_proj_ref[...])


def attend(group, tokens, w_qkv, taps, table, mem, w_proj, base):
    heads, _, size = table.shape
    width = heads * size
    return pl.pallas_call(
        functools.partial(attend_kernel, heads, size),
        out_shape=(
            jax.ShapeDtypeStruct((clip_rows, width), b_type),
            jax.ShapeDtypeStruct((clip_rows, w_proj.shape[1]), f_type),
            jax.ShapeDtypeStruct((grid_rows, 3 * width), b_type),
            jax.ShapeDtypeStruct((heads, 2, grid_rows, grid_rows), f_type),
        ),
        in_specs=[pl.BlockSpec(memory_space=pltpu.SMEM)] + in_vmem(7),
        out_specs=tuple(in_vmem(4)),
        scratch_shapes=[
            pltpu.VMEM((3, 10, 9, 8, 3 * width), f_type),
            pltpu.VMEM((8, 7, 8, 3 * width), f_type),
            pltpu.VMEM((grid_rows, width), f_type),
            pltpu.VMEM((grid_rows, 192), b_type),
            pltpu.VMEM((grid_rows, 192), b_type),
        ],
        compiler_params=params(),
        name="attend",
    )(group, tokens, w_qkv, taps, table, mem, w_proj, base)


def attend_back_kernel(
    heads,
    size,
    tokens_ref,
    w_qkv_ref,
    taps_ref,
    table_ref,
    mem_ref,
    w_proj_ref,
    pooled_ref,
    probs_ref,
    grad_ref,
    base_ref,
    d_qkv_ref,
    d_norm_ref,
    d_taps_ref,
    d_table_ref,
    d_mem_ref,
    field,
    grads,
    wide,
    d_head_ref,
    d_low_ref,
    probs_low,
    d_scores,
    d_query,
    d_pooled,
):
    scale = size ** (-0.5)
    clear_border(field)
    clear_border(grads)
    spread = spread_matrix()
    grid_tokens = dot(spread, tokens_ref[...]).astype(b_type)
    fill_field(field, dot(grid_tokens, w_qkv_ref[...]))
    d_branch = dot(spread, grad_ref[...]).astype(b_type)
    d_head = dot_nt(d_branch, w_proj_ref[...])
    d_head_ref[...] = d_head
    d_low_ref[...] = d_head.astype(b_type)
    expand = table_matrix()
    keys_at = key_matrix()
    for head in range(heads):
        at = 3 * head * size
        lanes = slice(head * size, (head + 1) * size)
        queries = pooled_ref[:, at : at + size]
        keys = pooled_ref[:, at + size : at + 2 * size]
        values = pooled_ref[:, at + 2 * size : at + 3 * size]
        mem_keys = mem_ref[0, :, lanes]
        mem_values = mem_ref[1, :, lanes]

        def rows_step(step, carry, lanes=lanes, head=head, keys=keys, values=values,
                      mem_keys=mem_keys, mem_values=mem_values):
            rows = pl.ds(pl.multiple_of(step * block_rows, block_rows), block_rows)
            d_att = d_low_ref[rows, lanes]
            own = probs_ref[head, 0, rows, :]
            mem = probs_ref[head, 1, rows, :]
            d_own = dot_nt(d_att, values)
            d_mem = dot_nt(d_att, mem_values)
            inner = jnp.sum(own * d_own, axis=-1, keepdims=True) + jnp.sum(
                mem * d_mem, axis=-1, keepdims=True
            )
            d_own = (own * (d_own - inner)).astype(b_type)
            d_mem = (mem * (d_mem - inner)).astype(b_type)
            probs_low[0, rows, :] = own.astype(b_type)
            probs_low[1, rows, :] = mem.astype(b_type)
            d_scores[0, rows, :] = d_own
            d_scores[1, rows, :] = d_mem
            d_query[rows, :] = (dot(d_own, keys) + dot(d_mem, mem_keys)) * scale
            return carry

        lax.fori_loop(0, grid_rows // block_rows, rows_step, 0)
        table_high, table_low = split(table_ref[head])
        rel = dot_nt(d_scores[0], keys_at) * query_mask()
        rel_high, rel_low = split(rel)
        wide_high = dot(expand, table_high).astype(b_type)
        wide_low = dot(expand, table_low).astype(b_type)
        d_rel = dot(rel_high, wide_high) + dot(rel_low, wide_high) + dot(rel_high, wide_low)
        d_pooled[:, at : at + size] = d_query[...] + d_head_ref[:, lanes] + d_rel
        queries_t = jnp.transpose(queries.astype(f_type)).astype(b_type)
        d_att_t = jnp.transpose(d_head_ref[:, lanes]).astype(b_type)
        spread_high, spread_low = split(dot(queries_t, rel_high) + dot(queries_t, rel_low))
        d_table_ref[head] = dot(spread_high, expand) + dot(spread_low, expand)
        d_pooled[:, at + size : at + 2 * size] = jnp.transpose(dot(queries_t, d_scores[0])) * scale
        d_mem_ref[0, :, lanes] = (jnp.transpose(dot(queries_t, d_scores[1])) * scale).astype(b_type)
        d_pooled[:, at + 2 * size : at + 3 * size] = jnp.transpose(dot(d_att_t, probs_low[0]))
        d_mem_ref[1, :, lanes] = jnp.transpose(dot(d_att_t, probs_low[1])).astype(b_type)
    fill_field(grads, d_pooled[...])
    tap_grads(field, grads, d_taps_ref)
    convolve(grads, taps_ref, wide, True)
    d_qkv = wide[...].reshape(grid_rows, 3 * heads * size).astype(b_type)
    d_qkv = dot(gather_matrix(), d_qkv).astype(b_type)
    d_qkv_ref[...] = d_qkv
    d_norm_ref[...] = base_ref[...] + dot_nt(d_qkv, w_qkv_ref[...])


def attend_back(tokens, w_qkv, taps, table, mem, w_proj, pooled, probs, grad, base):
    heads, _, size = table.shape
    width = heads * size
    return pl.pallas_call(
        functools.partial(attend_back_kernel, heads, size),
        out_shape=(
            jax.ShapeDtypeStruct((clip_rows, 3 * width), b_type),
            jax.ShapeDtypeStruct((clip_rows, w_proj.shape[1]), f_type),
            jax.ShapeDtypeStruct((27, 3 * width), f_type),
            jax.ShapeDtypeStruct((heads, size, 41), f_type),
            jax.ShapeDtypeStruct((2, slot_rows, width), b_type),
        ),
        in_specs=in_vmem(10),
        out_specs=tuple(in_vmem(5)),
        scratch_shapes=[
            pltpu.VMEM((3, 10, 9, 8, 3 * width), f_type),
            pltpu.VMEM((3, 10, 9, 8, 3 * width), f_type),
            pltpu.VMEM((8, 7, 8, 3 * width), f_type),
            pltpu.VMEM((grid_rows, width), f_type),
            pltpu.VMEM((grid_rows, width), b_type),
            pltpu.VMEM((2, grid_rows, grid_rows), b_type),
            pltpu.VMEM((2, grid_rows, grid_rows), b_type),
            pltpu.VMEM((grid_rows, size), f_type),
            pltpu.VMEM((grid_rows, 3 * width), f_type),
        ],
        compiler_params=params(),
        name="attend_back",
    )(tokens, w_qkv, taps, table, mem, w_proj, pooled, probs, grad, base)


def frame_sum(level, frames, taps_ref):
    stride = 2 ** (level + 1)
    width = frames.shape[-1]
    pieces = []
    for out_frame in range(4):
        piece = jnp.zeros((56, width), f_type)
        if out_frame < 8 // stride:
            for tap in range(stride):
                start = 49 * (stride * out_frame + tap)
                piece = piece + frames[start : start + 56, :] * taps_ref[0, tap : tap + 1, :]
        pieces.append(piece)
    return jnp.concatenate(pieces, axis=0)


def compress_kernel(rows_ref, group_ref, bank_ref, taps_ref, out_ref, frames):
    width = frames.shape[-1]
    frames[0:clip_rows, :] = bank_ref[0, 0].astype(f_type)
    frames[clip_rows:, :] = jnp.zeros((8, width), f_type)
    group = group_ref[pl.program_id(1)]
    for level in range(3):

        @pl.when(group == level)
        def _(level=level):
            out_ref[0, 0] = frame_sum(level, frames, taps_ref).astype(b_type)


def compress(bank, taps, index_rows, groups):
    clips = groups.shape[0]
    width = bank.shape[3]
    return pl.pallas_call(
        compress_kernel,
        out_shape=jax.ShapeDtypeStruct((clips, 2, slot_rows, width), b_type),
        grid_spec=pltpu.PrefetchScalarGridSpec(
            num_scalar_prefetch=2,
            grid=(2, clips, 2),
            in_specs=[
                pl.BlockSpec(
                    (1, 1, clip_rows, width), lambda k, n, m, rows, group: (rows[n, m], k, 0, 0)
                ),
                pl.BlockSpec((1, 8, width), lambda k, n, m, rows, group: (k, 0, 0)),
            ],
            out_specs=pl.BlockSpec(
                (1, 1, slot_rows // 2, width), lambda k, n, m, rows, group: (n, k, m, 0)
            ),
            scratch_shapes=[pltpu.VMEM((400, width), f_type)],
        ),
        compiler_params=params(),
        name="compress",
    )(index_rows, groups, bank, taps)


def compress_back_kernel(rows_ref, group_ref, bank_ref, grad_ref, out_ref, frames):
    width = frames.shape[-1]
    frames[0:clip_rows, :] = bank_ref[0, 0].astype(f_type)
    frames[clip_rows:, :] = jnp.zeros((8, width), f_type)
    group = group_ref[pl.program_id(1)]

    @pl.when((pl.program_id(1) == 0) & (pl.program_id(2) == 0))
    def _():
        out_ref[...] = jnp.zeros(out_ref.shape, f_type)

    grad = grad_ref[0, 0].astype(f_type)
    for level in range(3):

        @pl.when(group == level)
        def _(level=level):
            stride = 2 ** (level + 1)
            for tap in range(stride):
                total = jnp.zeros((56, width), f_type)
                for out_frame in range(8 // stride):
                    start = 49 * (stride * out_frame + tap)
                    total = total + (
                        frames[start : start + 56, :] * grad[56 * out_frame : 56 * out_frame + 56]
                    )
                out_ref[0, tap : tap + 1, :] += jnp.sum(total, axis=0, keepdims=True)


def compress_back(bank, grad, index_rows, groups):
    clips = groups.shape[0]
    width = bank.shape[3]
    return pl.pallas_call(
        compress_back_kernel,
        out_shape=jax.ShapeDtypeStruct((2, 8, width), f_type),
        grid_spec=pltpu.PrefetchScalarGridSpec(
            num_scalar_prefetch=2,
            grid=(2, clips, 2),
            in_specs=[
                pl.BlockSpec(
                    (1, 1, clip_rows, width), lambda k, n, m, rows, group: (rows[n, m], k, 0, 0)
                ),
                pl.BlockSpec(
                    (1, 1, slot_rows // 2, width), lambda k, n, m, rows, group: (n, k, m, 0)
                ),
            ],
            out_specs=pl.BlockSpec((1, 8, width), lambda k, n, m, rows, group: (k, 0, 0)),
            scratch_shapes=[pltpu.VMEM((400, width), f_type)],
        ),
        compiler_params=params(),
        name="compress_back",
    )(index_rows, groups, bank, grad)


def normal_rows(values):
    centered = values - jnp.mean(values, axis=-1, keepdims=True)
    inverse = lax.rsqrt(jnp.mean(centered * centered, axis=-1, keepdims=True) + eps_norm)
    return centered * inverse, inverse


def norm_back(normal, inverse, grad, gain):
    scaled = grad * gain
    return inverse * (
        scaled
        - jnp.mean(scaled, axis=-1, keepdims=True)
        - normal * jnp.mean(scaled * normal, axis=-1, keepdims=True)
    )


def column_sum(values):
    return jnp.sum(values, axis=0, keepdims=True)


def first_norm_kernel(rows_ref, gain_ref, shift_ref, out_ref):
    normal, _ = normal_rows(rows_ref[...].astype(f_type))
    out_ref[...] = (normal * gain_ref[...] + shift_ref[...]).astype(b_type)


def first_norm(rows, gain, shift):
    return pl.pallas_call(
        first_norm_kernel,
        out_shape=jax.ShapeDtypeStruct(rows.shape, b_type),
        in_specs=in_vmem(3),
        out_specs=in_vmem(1)[0],
        compiler_params=params(),
        name="first_norm",
    )(rows, gain, shift)


def second_norm_kernel(rows_ref, branch_ref, other_ref, bias_ref, gain_ref, shift_ref, mid_ref, out_ref):
    midway = rows_ref[...].astype(f_type) + (
        branch_ref[...] + other_ref[...].astype(f_type) + bias_ref[...]
    )
    mid_ref[...] = midway
    normal, _ = normal_rows(midway)
    out_ref[...] = (normal * gain_ref[...] + shift_ref[...]).astype(b_type)


def second_norm(rows, branch, other, bias, gain, shift):
    return pl.pallas_call(
        second_norm_kernel,
        out_shape=(
            jax.ShapeDtypeStruct(rows.shape, f_type),
            jax.ShapeDtypeStruct(rows.shape, b_type),
        ),
        in_specs=in_vmem(6),
        out_specs=tuple(in_vmem(2)),
        compiler_params=params(),
        name="second_norm",
    )(rows, branch, other, bias, gain, shift)


def second_back_kernel(mid_ref, grad_ref, other_ref, top_ref, gain_ref, d_mid_ref, d_low_ref, sums_ref):
    normal, inverse = normal_rows(mid_ref[...])
    grad = grad_ref[...] + other_ref[...].astype(f_type)
    top = top_ref[...].astype(f_type)
    d_mid = top + norm_back(normal, inverse, grad, gain_ref[...])
    d_mid_ref[...] = d_mid
    d_low = d_mid.astype(b_type)
    d_low_ref[...] = d_low
    sums_ref[0:1, :] = column_sum(d_low.astype(f_type))
    sums_ref[1:2, :] = column_sum(grad * normal)
    sums_ref[2:3, :] = column_sum(grad)
    sums_ref[3:4, :] = column_sum(top)


def second_back(midway, grad, other, top, gain):
    return pl.pallas_call(
        second_back_kernel,
        out_shape=(
            jax.ShapeDtypeStruct(midway.shape, f_type),
            jax.ShapeDtypeStruct(midway.shape, b_type),
            jax.ShapeDtypeStruct((4, midway.shape[1]), f_type),
        ),
        in_specs=in_vmem(5),
        out_specs=tuple(in_vmem(3)),
        compiler_params=params(),
        name="second_back",
    )(midway, grad, other, top, gain)


def first_back_kernel(rows_ref, grad_ref, other_ref, d_mid_ref, gain_ref, out_ref, sums_ref):
    normal, inverse = normal_rows(rows_ref[...].astype(f_type))
    grad = grad_ref[...] + other_ref[...].astype(f_type)
    out_ref[...] = d_mid_ref[...] + norm_back(normal, inverse, grad, gain_ref[...])
    sums_ref[0:1, :] = column_sum(grad * normal)
    sums_ref[1:2, :] = column_sum(grad)


def first_back(rows, grad, other, d_mid, gain):
    return pl.pallas_call(
        first_back_kernel,
        out_shape=(
            jax.ShapeDtypeStruct(rows.shape, f_type),
            jax.ShapeDtypeStruct((2, rows.shape[1]), f_type),
        ),
        in_specs=in_vmem(5),
        out_specs=tuple(in_vmem(2)),
        compiler_params=params(),
        name="first_back",
    )(rows, grad, other, d_mid, gain)


def error_function(values):
    x = jnp.clip(values, -4.0, 4.0)
    y = x * x
    top = -2.72614225801306e-10
    for term in (
        2.77068142495902e-08,
        -2.10102402082508e-06,
        -5.69250639462346e-05,
        -7.34990630326855e-04,
        -2.95459980854025e-03,
        -1.60960333262415e-02,
    ):
        top = top * y + term
    low = -1.45660718464996e-05
    for term in (
        -2.13374055278905e-04,
        -1.68282697438203e-03,
        -7.37332916720468e-03,
        -1.42647390514189e-02,
    ):
        low = low * y + term
    return x * top / low


def mlp_kernel(
    part,
    tokens_ref,
    top_ref,
    up_a,
    up_b,
    bias_a,
    bias_b,
    down_a,
    down_b,
    out_ref,
    d_norm_ref,
    act_ref,
    d_hid_ref,
    sums_ref,
):
    tokens = tokens_ref[...]
    top = top_ref[...]
    units = up_a.shape[1]
    out_ref[...] = jnp.zeros(out_ref.shape, f_type)
    d_norm_ref[...] = jnp.zeros(d_norm_ref.shape, f_type)
    for block, (up, bias, down) in enumerate(((up_a, bias_a, down_a), (up_b, bias_b, down_b))):
        for start in range(0, units, part):
            here = slice(start, start + part)
            hidden = dot(tokens, up[:, here]) + bias[:, here]
            half = 0.5 * (1.0 + error_function(hidden * (0.5**0.5)))
            slope = half + hidden * jnp.exp(-0.5 * hidden * hidden) * 0.3989422804014327
            act = (hidden * half).astype(b_type)
            d_hid = (dot_nt(top, down[here, :]) * slope).astype(b_type)
            act_ref[block, :, here] = act
            d_hid_ref[block, :, here] = d_hid
            sums_ref[block : block + 1, here] = column_sum(d_hid.astype(f_type))
            out_ref[...] += dot(act, down[here, :])
            d_norm_ref[...] += dot_nt(d_hid, up[:, here])


def mlp(tokens, top, up_a, up_b, bias_a, bias_b, down_a, down_b):
    rows, width = tokens.shape
    units = up_a.shape[1]
    part = 256 if units % 256 == 0 else units
    return pl.pallas_call(
        functools.partial(mlp_kernel, part),
        out_shape=(
            jax.ShapeDtypeStruct((rows, width), f_type),
            jax.ShapeDtypeStruct((rows, width), f_type),
            jax.ShapeDtypeStruct((2, rows, units), b_type),
            jax.ShapeDtypeStruct((2, rows, units), b_type),
            jax.ShapeDtypeStruct((2, units), f_type),
        ),
        in_specs=in_vmem(8),
        out_specs=tuple(in_vmem(5)),
        compiler_params=params(),
        name="mlp",
    )(tokens, top, up_a, up_b, bias_a, bias_b, down_a, down_b)


def swap_pairs(count, bit):
    return [(place, place ^ bit) for place in range(count)]


def ordered(flag, mine, other):
    return jnp.concatenate([jnp.where(flag, other, mine), jnp.where(flag, mine, other)], axis=0)


class Team:
    def __init__(self, heads_count, clips_count):
        self.total = heads_count
        self.half = heads_count // 2
        self.clips = clips_count
        self.here = lax.axis_index("head")
        self.clip = self.here // self.half
        self.seat = self.here % self.half
        self.spot = lax.axis_index("clip")

    def partner(self, values):
        return lax.ppermute(values, "head", swap_pairs(self.total, self.half))

    def gather(self, rows):
        pieces = [rows] + [
            lax.ppermute(rows, "head", swap_pairs(self.total, step))
            for step in range(1, self.half)
        ]
        return jnp.concatenate(
            [self.pick(place ^ self.seat, pieces) for place in range(self.half)], axis=0
        )

    def pick(self, which, pieces):
        if len(pieces) == 2:
            return jnp.where(which == 0, pieces[0], pieces[1])
        return lax.select_n(which.astype(jnp.int32), *pieces)

    def scatter(self, partial):
        rows = partial.shape[0] // self.half

        def part(place):
            return lax.dynamic_slice_in_dim(partial, place * rows, rows, axis=0)

        other = None
        for step in range(1, self.half):
            came = lax.ppermute(
                part(self.seat ^ step).astype(b_type), "head", swap_pairs(self.total, step)
            )
            other = came if other is None else other.astype(f_type) + came.astype(f_type)
        return part(self.seat), other

    def bits(self):
        bit, found = 1, []
        while bit < self.clips:
            found.append(bit)
            bit *= 2
        return found

    def swap(self, values, bit):
        return lax.ppermute(values, "clip", swap_pairs(self.clips, bit))

    def flag(self, bit):
        return (self.spot & bit) != 0

    def fetch(self, values):
        rows = values.shape[0] // 4
        quarter = lax.dynamic_slice_in_dim(values, (self.spot % 4) * rows, rows, axis=0)
        came = self.partner(quarter)
        came = ordered(self.flag(1), came, self.swap(came, 1))
        return ordered(self.flag(2), came, self.swap(came, 2))

    def reduce(self, own, other):
        current = jnp.stack([own, other])
        columns = own.shape[1]
        for bit in self.bits():
            rows = current.shape[1] // 2
            side = (self.spot // bit) % 2
            halves = current.reshape(2, 2, rows, columns)
            kept = lax.dynamic_index_in_dim(halves, side, axis=1, keepdims=False)
            sent = lax.dynamic_index_in_dim(halves, 1 - side, axis=1, keepdims=False)
            came = self.swap(sent, bit)
            current = (kept.astype(f_type) + came.astype(f_type)).astype(b_type)
        current = (
            current[0].astype(f_type) + self.partner(current[1]).astype(f_type)
        ).astype(b_type)
        for bit in reversed(self.bits()):
            current = ordered(self.flag(bit), current, self.swap(current, bit))
        return current.astype(f_type)


def on_device(
    heads_total,
    clips_total,
    inputs,
    ln1_gain,
    ln1_bias,
    w_qkv,
    pool_kernel,
    rel_table,
    comp_kernel,
    memory_bank,
    mem_index,
    clip_group,
    w_proj,
    proj_bias,
    ln2_gain,
    ln2_bias,
    w_up,
    up_bias,
    w_down,
    down_bias,
    cotangent,
):
    team = Team(heads_total, clips_total)
    heads, _, size = rel_table.shape
    units = w_up.shape[1]
    width = heads * size
    norm1 = first_norm(inputs, ln1_gain[None], ln1_bias[None])
    tokens1 = team.gather(norm1)

    taps = pool_kernel.reshape(3 * heads, 27, size).transpose(1, 0, 2).reshape(27, 3 * width)
    comp_taps = comp_kernel.transpose(1, 2, 0, 3).reshape(2, 8, width)
    small = jnp.concatenate([taps.reshape(-1), rel_table.reshape(-1), up_bias])
    small_far = team.partner(small)
    cut = [27 * 3 * width, 27 * 3 * width + 41 * width]
    taps_far = small_far[: cut[0]].reshape(27, 3 * width)
    table_far = small_far[cut[0] : cut[1]].reshape(heads, 41, size)
    bias_far = small_far[cut[1] :]

    w_qkv_far = team.fetch(w_qkv)
    w_proj_far = team.fetch(w_proj)
    memory = compress(memory_bank, comp_taps, mem_index, clip_group)
    mem_here = lax.dynamic_index_in_dim(memory, team.clip, axis=0, keepdims=False)
    mem_far = team.partner(
        lax.dynamic_index_in_dim(memory, 1 - team.clip, axis=0, keepdims=False)
    )
    w_up_far = team.fetch(w_up)
    w_down_far = team.fetch(w_down)
    top = team.gather(cotangent)
    group = lax.dynamic_slice_in_dim(clip_group, team.clip, 1)

    none = jnp.zeros((clip_rows, inputs.shape[1]), f_type)
    out_here, branch, pooled_here, probs_here = attend(
        group, tokens1, w_qkv, taps, rel_table, mem_here, w_proj, none
    )
    out_far, branch, pooled_far, probs_far = attend(
        group, tokens1, w_qkv_far, taps_far, table_far, mem_far, w_proj_far, branch
    )
    branch_here, branch_other = team.scatter(branch)
    midway, norm2 = second_norm(
        inputs, branch_here, branch_other, proj_bias[None], ln2_gain[None], ln2_bias[None]
    )
    tokens2 = team.gather(norm2)
    mlp_out, d_norm2, act, d_hid, d_up_bias = mlp(
        tokens2, top, w_up, w_up_far, up_bias[None], bias_far[None], w_down, w_down_far
    )
    d_norm2_here, d_norm2_other = team.scatter(d_norm2)
    mlp_here, mlp_other = team.scatter(mlp_out)
    output = (midway + (mlp_here + mlp_other.astype(f_type)) + down_bias).astype(b_type)
    d_mid, d_branch, sums2 = second_back(
        midway, d_norm2_here, d_norm2_other, cotangent, ln2_gain[None]
    )
    d_branch_all = team.gather(d_branch)

    def product(a, b):
        return lax.dot_general(
            a, b, (((0,), (0,)), ((), ())), preferred_element_type=f_type
        ).astype(b_type)

    g_mlp = [
        jnp.concatenate([product(tokens2, d_hid[k]), product(act[k], top)], axis=0)
        if units == inputs.shape[1]
        else None
        for k in range(2)
    ]
    if units == inputs.shape[1]:
        g_mlp = team.reduce(*g_mlp)
        g_w_up, g_w_down = g_mlp[: inputs.shape[1]], g_mlp[inputs.shape[1] :]
    else:
        g_w_up = team.reduce(product(tokens2, d_hid[0]), product(tokens2, d_hid[1]))
        g_w_down = team.reduce(product(act[0], top), product(act[1], top))

    none = jnp.zeros((clip_rows, inputs.shape[1]), f_type)
    d_qkv_far, d_norm1, d_taps_far, d_table_far, d_mem_far = attend_back(
        tokens1, w_qkv_far, taps_far, table_far, mem_far, w_proj_far, pooled_far, probs_far,
        d_branch_all, none,
    )
    d_qkv_here, d_norm1, d_taps_here, d_table_here, d_mem_here = attend_back(
        tokens1, w_qkv, taps, rel_table, mem_here, w_proj, pooled_here, probs_here,
        d_branch_all, d_norm1,
    )
    d_norm1_here, d_norm1_other = team.scatter(d_norm1)
    d_mem_back = team.partner(d_mem_far)
    first = team.clip == 0
    d_memory = jnp.stack(
        [jnp.where(first, d_mem_here, d_mem_back), jnp.where(first, d_mem_back, d_mem_here)]
    )
    g_comp = compress_back(memory_bank, d_memory, mem_index, clip_group)
    g_w_qkv = team.reduce(product(tokens1, d_qkv_here), product(tokens1, d_qkv_far))
    g_w_proj = team.reduce(product(out_here, d_branch_all), product(out_far, d_branch_all))
    grad_inputs, sums1 = first_back(inputs, d_norm1_here, d_norm1_other, d_mid, ln1_gain[None])

    small_far = jnp.concatenate([d_taps_far.reshape(-1), d_table_far.reshape(-1), d_up_bias[1]])
    small = jnp.concatenate([d_taps_here.reshape(-1), d_table_here.reshape(-1), d_up_bias[0]])
    small = small + team.partner(small_far)
    small = lax.psum(jnp.concatenate([small, g_comp.reshape(-1)]), "clip")
    cut = cut + [cut[1] + units]
    g_pool = small[: cut[0]].reshape(27, 3 * heads, size).transpose(1, 0, 2)
    g_pool = g_pool.reshape(heads, 3, 27, size)
    g_rel = small[cut[0] : cut[1]].reshape(heads, size, 41).transpose(0, 2, 1)
    g_up_bias = small[cut[1] : cut[2]]
    g_comp = small[cut[2] :].reshape(2, 8, heads, size).transpose(2, 0, 1, 3)
    sums = lax.psum(jnp.concatenate([sums2, sums1], axis=0), ("clip", "head"))
    return (
        output,
        grad_inputs,
        sums[4],
        sums[5],
        g_w_qkv,
        g_pool,
        g_rel,
        g_comp,
        g_w_proj,
        sums[0],
        sums[1],
        sums[2],
        g_w_up,
        g_up_bias,
        g_w_down,
        sums[3],
    )


def solution(mesh):
    return jax.shard_map(
        functools.partial(on_device, mesh.shape["head"], mesh.shape["clip"]),
        mesh=mesh,
        in_specs=(
            P(("clip", "head"), None),
            P(),
            P(),
            P(None, "head"),
            P("head", None, None, None),
            P("head", None, None),
            P("head", None, None, None),
            P("clip", None, None, "head"),
            P("clip", None),
            P("clip"),
            P("head", None),
            P(),
            P(),
            P(),
            P(None, "head"),
            P("head"),
            P("head", None),
            P(),
            P(("clip", "head"), None),
        ),
        out_specs=(
            P(("clip", "head"), None),
            P(("clip", "head"), None),
            P(),
            P(),
            P(None, "head"),
            P("head", None, None, None),
            P("head", None, None),
            P("head", None, None, None),
            P("head", None),
            P(),
            P(),
            P(),
            P(None, "head"),
            P("head"),
            P("head", None),
            P(),
        ),
        check_vma=False,
    )
```

```python
import functools

import jax
import jax.numpy as jnp
from jax import lax
from jax.experimental import pallas as pl
from jax.experimental.pallas import tpu as pltpu
from jax.sharding import PartitionSpec as P

f_type = jnp.float32
b_type = jnp.bfloat16
eps_norm = 1e-06
neg_large = -1000000000.0
clip_rows = 392
grid_rows = 448
slot_rows = 448
block_rows = 112
vmem_bytes = 56 * 1024 * 1024


def dot(a, b):
    return jnp.dot(a, b, preferred_element_type=f_type)


def dot_nt(a, b):
    return lax.dot_general(a, b, (((1,), (1,)), ((), ())), preferred_element_type=f_type)


def iota(shape, axis):
    return lax.broadcasted_iota(jnp.int32, shape, axis)


def one_hot(flag):
    return jnp.where(flag, 1.0, 0.0).astype(b_type)


def split(values):
    high = values.astype(b_type)
    return high, (values - high.astype(f_type)).astype(b_type)


def aligned(start, step):
    return pl.multiple_of(start, step)


def call(kernel, name, cost, results, scalars, arrays, scratch=(), after=()):
    def body(*refs):
        kept = refs[: len(scalars) + len(arrays)]
        kernel(*kept, *refs[len(kept) + len(after) :])

    single = not isinstance(results, tuple)
    shapes = (results,) if single else results
    outs = pl.pallas_call(
        body,
        out_shape=tuple(jax.ShapeDtypeStruct(shape, kind) for shape, kind in shapes),
        in_specs=[pl.BlockSpec(memory_space=pltpu.SMEM)] * len(scalars)
        + [pl.BlockSpec(memory_space=pltpu.VMEM)] * len(arrays)
        + [pl.BlockSpec(memory_space=pl.ANY)] * len(after),
        out_specs=tuple(pl.BlockSpec(memory_space=pltpu.VMEM) for _ in shapes),
        scratch_shapes=list(scratch),
        compiler_params=pltpu.CompilerParams(vmem_limit_bytes=vmem_bytes),
        cost_estimate=pl.CostEstimate(
            flops=int(cost * 1e9), bytes_accessed=int(cost * 3e6), transcendentals=0
        ),
        name=name,
    )(*scalars, *arrays, *after)
    return outs[0] if single else outs


def spread_matrix(start, count):
    row = iota((grid_rows, count), 0)
    place = row & 7
    return one_hot(
        ((row >> 3) * 7 + place - start == iota((grid_rows, count), 1)) & (place < 7)
    )


def gather_matrix(start, count):
    row = iota((count, grid_rows), 1)
    place = row & 7
    return one_hot(
        ((row >> 3) * 7 + place - start == iota((count, grid_rows), 0)) & (place < 7)
    )


def to_grid(seat, pieces):
    total = None
    for step, piece in enumerate(pieces):
        rows = piece.shape[0]
        part = dot(spread_matrix((seat ^ step) * rows, rows), piece[...])
        total = part if total is None else total + part
    return total.astype(b_type)


def row_coords(shape, axis):
    row = iota(shape, axis)
    line = row >> 3
    frame = (line * 37) >> 8
    return frame, line - frame * 7, row & 7


def coord_of(kind, coords):
    frame, line, place = coords
    return jnp.where(kind == 0, frame, jnp.where(kind == 1, line, place))


def query_mask():
    shape = (grid_rows, 192)
    column = iota(shape, 1)
    coord = coord_of(column >> 6, row_coords(shape, 0))
    return jnp.where(((column >> 3) & 7) == coord, 1.0, 0.0)


def key_matrix():
    shape = (192, grid_rows)
    column = iota(shape, 0)
    coord = coord_of(column >> 6, row_coords(shape, 1))
    return one_hot((column & 7) == coord)


def table_slot(column):
    kind = column >> 6
    at_query = (column >> 3) & 7
    at_key = column & 7
    base = jnp.where(kind == 0, 7, jnp.where(kind == 1, 21, 34))
    valid = (kind == 0) | ((at_query < 7) & (at_key < 7))
    return jnp.where(valid, base + at_query - at_key, -1)


def table_matrix():
    return one_hot(table_slot(iota((192, 41), 0)) == iota((192, 41), 1))


def key_bias(limit):
    lane = iota((1, grid_rows), 1)
    own = jnp.where((lane & 7) == 7, neg_large, 0.0)
    group = jnp.zeros_like(lane)
    for step in range(1, 8):
        group = group + jnp.where(lane >= 56 * step, 1, 0)
    place = lane - 56 * group
    valid = (place < 49) & ((group & 3) < limit)
    return own, jnp.where(valid, 0.0, neg_large)


def clear_border(field):
    width = field.shape[-1]
    field[:, 0:1] = jnp.zeros((3, 1, 9, 8, width), f_type)
    field[:, 9:10] = jnp.zeros((3, 1, 9, 8, width), f_type)
    field[:, :, 0:1] = jnp.zeros((3, 10, 1, 8, width), f_type)
    field[:, :, 8:9] = jnp.zeros((3, 10, 1, 8, width), f_type)


def fill_field(field, values):
    width = values.shape[-1]
    lines = values.reshape(56, 8, width)
    field[0, 1:9, 1:8] = pltpu.roll(lines, 1, 1).reshape(8, 7, 8, width)
    field[1, 1:9, 1:8] = lines.reshape(8, 7, 8, width)
    field[2, 1:9, 1:8] = pltpu.roll(lines, 7, 1).reshape(8, 7, 8, width)


def convolve(field, taps, result, flip):
    width = field.shape[-1]
    for start in range(0, width, 128):
        lanes = slice(start, min(start + 128, width))

        def frame(t, carry):
            total = jnp.zeros((7, 8, lanes.stop - lanes.start), f_type)
            for dt in range(3):
                for dw in range(3):
                    near = field[dw, t + dt, :, :, lanes]
                    for dh in range(3):
                        tap = dt * 9 + dh * 3 + dw
                        tap = 26 - tap if flip else tap
                        total = total + near[dh : dh + 7] * taps[tap : tap + 1, lanes]
            result[t, :, :, lanes] = total
            return carry

        lax.fori_loop(0, 8, frame, 0)


def tap_grads(field, grads, result):
    width = field.shape[-1]
    for start in range(0, width, 128):
        lanes = slice(start, min(start + 128, width))
        size = lanes.stop - lanes.start

        def frame(t, sums):
            grad = grads[1, t + 1, 1:8, :, lanes]
            sums = list(sums)
            for dt in range(3):
                for dw in range(3):
                    near = field[dw, t + dt, :, :, lanes]
                    for dh in range(3):
                        tap = dt * 9 + dh * 3 + dw
                        sums[tap] = sums[tap] + jnp.sum(near[dh : dh + 7] * grad, axis=0)
            return tuple(sums)

        sums = lax.fori_loop(
            0, 8, frame, tuple(jnp.zeros((8, size), f_type) for _ in range(27))
        )
        for tap in range(27):
            result[tap : tap + 1, lanes] = jnp.sum(sums[tap], axis=0, keepdims=True)


class Rows:
    def __init__(self, heads, units, width):
        self.taps = 0
        self.table = self.taps + 96 * heads
        self.bias = self.table + 48 * heads
        self.weights = self.bias + 8
        self.comp = self.weights
        self.sums = self.comp + 16 * heads
        self.total = self.sums + 48
        self.units = units // 128
        self.width = width // 128


def wide_row(ref, start, count):
    return jnp.concatenate([ref[start + k : start + k + 1, :] for k in range(count)], axis=1)


def put_row(ref, start, values):
    for k in range(values.shape[1] // 128):
        ref[start + k : start + k + 1, :] = values[:, 128 * k : 128 * k + 128]


def vector(ref):
    return wide_row(ref, 0, ref.shape[0])


def seat_of(place, half):
    return place[0] & (half - 1)


def clip_of(place, half):
    return place[0] >> (half.bit_length() - 1)


def core_of(place):
    return place[1] & 1


def put_halves(whole, place, halves):
    size = halves[0].shape[0]
    for step, item in enumerate(halves):
        whole[pl.ds(aligned((core_of(place) ^ step) * size, size), size), :] = item[...]


def weight_views(refs, width):
    if len(refs) == 2:
        return refs[0], refs[1]
    return refs[0].at[0 : 3 * width], refs[0].at[3 * width : 4 * width]


def load_taps(taps, small, heads, size):
    for index in range(3 * heads):
        taps[0:27, index * size : (index + 1) * size] = small[
            32 * index : 32 * index + 27, 0:size
        ]


def attend_kernel(rows, heads, size, half, far, *refs):
    refs = list(refs)

    def take(count):
        found = refs[:count]
        del refs[:count]
        return found

    place, groups = take(2)
    pieces = take(half)
    chunks = take(2)
    small, mem = take(2)
    base = take(1)[0] if far else None
    if far:
        mine_ref, other_ref, all_weights = take(3)
    else:
        (branch_ref,) = take(1)
    pooled_ref, probs_ref, head_ref = take(3)
    field, taps, pooled_wide, head_wide, rel_high, rel_low = refs
    width = heads * size
    scale = size ** (-0.5)
    seat = seat_of(place, half)
    if far:
        put_halves(all_weights, place, chunks)
        chunks = [all_weights]
    w_qkv, w_proj = weight_views(chunks, width)
    clear_border(field)
    load_taps(taps, small, heads, size)
    fill_field(field, dot_nt(to_grid(seat, pieces), w_qkv[...]))
    convolve(field, taps, pooled_wide, False)
    pooled = pooled_wide[...].reshape(grid_rows, 3 * width)
    filled = (iota((grid_rows, 1), 0) & 7) < 7
    pooled_ref[...] = jnp.where(filled, pooled, 0.0).astype(b_type)
    own_bias, mem_bias = key_bias(4 >> groups[clip_of(place, half)])
    expand = table_matrix()
    keys_at = key_matrix()
    mask = query_mask()
    for head in range(heads):
        at = 3 * head * size
        lanes = slice(head * size, (head + 1) * size)
        queries = pooled_ref[:, at : at + size]
        keys = pooled_ref[:, at + size : at + 2 * size]
        values = pooled_ref[:, at + 2 * size : at + 3 * size]
        mem_keys = mem[0, lanes, :]
        mem_values = mem[1, lanes, :]
        start = rows.table + 48 * head
        table_high, table_low = split(small[start : start + 41, 0:size])
        rel = dot_nt(queries, dot(expand, table_high).astype(b_type)) + dot_nt(
            queries, dot(expand, table_low).astype(b_type)
        )
        high, low = split(rel * mask)
        rel_high[...] = high
        rel_low[...] = low

        def rows_step(step, carry, at=at, lanes=lanes, head=head, keys=keys, values=values,
                      mem_keys=mem_keys, mem_values=mem_values):
            block_at = pl.ds(aligned(step * block_rows, block_rows), block_rows)
            block = pooled_ref[block_at, at : at + size]
            own = (
                dot_nt(block, keys) * scale
                + (dot(rel_high[block_at, :], keys_at) + dot(rel_low[block_at, :], keys_at))
                + own_bias
            )
            mem = dot(block, mem_keys) * scale + mem_bias
            top = jnp.maximum(
                jnp.max(own, axis=-1, keepdims=True), jnp.max(mem, axis=-1, keepdims=True)
            )
            own = jnp.exp(own - top)
            mem = jnp.exp(mem - top)
            total = jnp.sum(own, axis=-1, keepdims=True) + jnp.sum(mem, axis=-1, keepdims=True)
            inverse = 1.0 / total
            own = own * inverse
            mem = mem * inverse
            probs_ref[head, 0, block_at, :] = own
            probs_ref[head, 1, block_at, :] = mem
            attended = dot(own.astype(b_type), values) + dot_nt(mem.astype(b_type), mem_values)
            head_wide[block_at, lanes] = attended + block.astype(f_type)
            return carry

        lax.fori_loop(0, grid_rows // block_rows, rows_step, 0)
    head_ref[...] = head_wide[...].astype(b_type)
    count = pieces[0].shape[0]
    for step in range(half):
        head_out = dot(gather_matrix((seat ^ step) * count, count), head_ref[...]).astype(b_type)
        part = dot(head_out, w_proj[...])
        if not far:
            branch_ref[step] = part
        elif step == 0:
            mine_ref[...] = part + base[0]
        else:
            other_ref[step - 1] = (part + base[step]).astype(b_type)


def attend(rows, heads, size, place, groups, pieces, weights, small, mem, base=None, after=()):
    width = heads * size
    half = len(pieces)
    count, model = pieces[0].shape
    far = base is not None
    branch = (
        (((count, model), f_type), ((half - 1, count, model), b_type), ((4 * width, model), b_type))
        if far
        else (((half, count, model), f_type),)
    )
    return call(
        functools.partial(attend_kernel, rows, heads, size, half, far),
        "attend",
        16,
        branch
        + (
            ((grid_rows, 3 * width), b_type),
            ((heads, 2, grid_rows, grid_rows), f_type),
            ((grid_rows, width), b_type),
        ),
        (place, groups),
        (*pieces, *weights, small, mem) + ((base,) if far else ()),
        scratch=(
            pltpu.VMEM((3, 10, 9, 8, 3 * width), f_type),
            pltpu.VMEM((32, 3 * width), f_type),
            pltpu.VMEM((8, 7, 8, 3 * width), f_type),
            pltpu.VMEM((grid_rows, width), f_type),
            pltpu.VMEM((grid_rows, 192), b_type),
            pltpu.VMEM((grid_rows, 192), b_type),
        ),
        after=after,
    )


def scores_back_kernel(rows, heads, size, half, parts, *refs):
    place = refs[0]
    pieces = refs[1 : 1 + half]
    weights = refs[1 + half : 1 + half + parts]
    (
        small, mem, pooled_ref, probs_ref, head_ref,
        d_pooled, d_mem_ref, d_table_ref, d_proj_ref,
        d_head_ref, d_low_ref, probs_low, d_scores, d_query,
    ) = refs[1 + half + parts :]
    width = heads * size
    scale = size ** (-0.5)
    w_proj = weight_views(weights, width)[1]
    d_branch = to_grid(seat_of(place, half), pieces)
    d_head = dot_nt(d_branch, w_proj[...])
    d_head_ref[...] = d_head
    d_low_ref[...] = d_head.astype(b_type)
    expand = table_matrix()
    keys_at = key_matrix()
    mask = query_mask()
    for head in range(heads):
        at = 3 * head * size
        lanes = slice(head * size, (head + 1) * size)
        queries = pooled_ref[:, at : at + size]
        keys = pooled_ref[:, at + size : at + 2 * size]
        values = pooled_ref[:, at + 2 * size : at + 3 * size]
        mem_keys = mem[0, lanes, :]
        mem_values = mem[1, lanes, :]

        def rows_step(step, carry, lanes=lanes, head=head, keys=keys, values=values,
                      mem_keys=mem_keys, mem_values=mem_values):
            block_at = pl.ds(aligned(step * block_rows, block_rows), block_rows)
            d_att = d_low_ref[block_at, lanes]
            own = probs_ref[head, 0, block_at, :]
            mem = probs_ref[head, 1, block_at, :]
            d_own = dot_nt(d_att, values)
            d_mem = dot(d_att, mem_values)
            inner = jnp.sum(own * d_own, axis=-1, keepdims=True) + jnp.sum(
                mem * d_mem, axis=-1, keepdims=True
            )
            d_own = (own * (d_own - inner)).astype(b_type)
            d_mem = (mem * (d_mem - inner)).astype(b_type)
            probs_low[0, block_at, :] = own.astype(b_type)
            probs_low[1, block_at, :] = mem.astype(b_type)
            d_scores[0, block_at, :] = d_own
            d_scores[1, block_at, :] = d_mem
            d_query[block_at, :] = (dot(d_own, keys) + dot_nt(d_mem, mem_keys)) * scale
            return carry

        lax.fori_loop(0, grid_rows // block_rows, rows_step, 0)
        start = rows.table + 48 * head
        table_high, table_low = split(small[start : start + 41, 0:size])
        rel_high, rel_low = split(dot_nt(d_scores[0], keys_at) * mask)
        wide_high = dot(expand, table_high).astype(b_type)
        wide_low = dot(expand, table_low).astype(b_type)
        d_rel = dot(rel_high, wide_high) + dot(rel_low, wide_high) + dot(rel_high, wide_low)
        d_pooled[:, at : at + size] = d_query[...] + d_head_ref[:, lanes] + d_rel
        queries_t = jnp.transpose(queries.astype(f_type)).astype(b_type)
        d_att_t = jnp.transpose(d_head_ref[:, lanes]).astype(b_type)
        wide_high, wide_low = split(dot(queries_t, rel_high) + dot(queries_t, rel_low))
        d_table = dot(wide_high, expand) + dot(wide_low, expand)
        d_table_ref[48 * head : 48 * head + 41, 0:size] = jnp.transpose(d_table)
        d_pooled[:, at + size : at + 2 * size] = jnp.transpose(dot(queries_t, d_scores[0])) * scale
        d_mem_ref[0, lanes, :] = (dot(queries_t, d_scores[1]) * scale).astype(b_type)
        d_pooled[:, at + 2 * size : at + 3 * size] = jnp.transpose(dot(d_att_t, probs_low[0]))
        d_mem_ref[1, lanes, :] = dot(d_att_t, probs_low[1]).astype(b_type)
    head_t = jnp.transpose(head_ref[...].astype(f_type)).astype(b_type)
    d_proj_ref[...] = dot(head_t, d_branch).astype(b_type)


def scores_back(rows, heads, size, place, pieces, weights, small, mem, pooled, probs, head, after=()):
    width = heads * size
    return call(
        functools.partial(scores_back_kernel, rows, heads, size, len(pieces), len(weights)),
        "scores_back",
        13,
        (
            ((grid_rows, 3 * width), f_type),
            ((2, width, slot_rows), b_type),
            ((48 * heads, 128), f_type),
            ((width, pieces[0].shape[1]), b_type),
        ),
        (place,),
        (*pieces, *weights, small, mem, pooled, probs, head),
        scratch=(
            pltpu.VMEM((grid_rows, width), f_type),
            pltpu.VMEM((grid_rows, width), b_type),
            pltpu.VMEM((2, grid_rows, grid_rows), b_type),
            pltpu.VMEM((2, grid_rows, grid_rows), b_type),
            pltpu.VMEM((grid_rows, size), f_type),
        ),
        after=after,
    )


def pool_back_kernel(rows, heads, size, half, parts, last, *refs):
    place = refs[0]
    pieces = refs[1 : 1 + half]
    weights = refs[1 + half : 1 + half + parts]
    refs = list(refs[1 + half + parts :])
    small, d_pooled, d_table, d_proj, d_bias = refs[:5]
    del refs[:5]
    base = refs.pop(0) if last else None
    if last:
        mine_ref, other_ref = refs.pop(0), refs.pop(0)
    else:
        norm_ref = refs.pop(0)
    keep_ref, send_ref, small_ref, field, grads, taps, wide, packed, d_taps = refs
    width = heads * size
    seat = seat_of(place, half)
    w_qkv = weight_views(weights, width)[0]
    clear_border(field)
    clear_border(grads)
    load_taps(taps, small, heads, size)
    tokens = to_grid(seat, pieces)
    fill_field(field, dot_nt(tokens, w_qkv[...]))
    fill_field(grads, d_pooled[...])
    convolve(grads, taps, wide, True)
    d_qkv = wide[...].reshape(grid_rows, 3 * width)
    low = d_qkv.astype(b_type)
    count = pieces[0].shape[0]
    for step in range(half):
        part = dot(gather_matrix((seat ^ step) * count, count), low).astype(b_type)
        part = dot(part, w_qkv[...])
        if not last:
            norm_ref[step] = part
        elif step == 0:
            mine_ref[...] = part + base[0]
        else:
            other_ref[step - 1] = (part + base[step]).astype(b_type)
    packed[0 : 3 * width, :] = dot(jnp.transpose(d_qkv).astype(b_type), tokens).astype(b_type)
    packed[3 * width : 4 * width, :] = d_proj[...]
    core = core_of(place)
    keep_ref[...] = packed[pl.ds(aligned(core * (2 * width), 2 * width), 2 * width), :]
    send_ref[...] = packed[pl.ds(aligned((1 - core) * (2 * width), 2 * width), 2 * width), :]
    tap_grads(field, grads, d_taps)
    for index in range(3 * heads):
        small_ref[32 * index : 32 * index + 27, 0:size] = d_taps[
            0:27, index * size : (index + 1) * size
        ]
    small_ref[rows.table : rows.table + 48 * heads, :] = d_table[...]
    small_ref[rows.bias : rows.bias + 8, :] = d_bias[...]


def pool_back(rows, heads, size, place, pieces, weights, small, d_pooled, d_table, d_proj, d_bias,
              base=None, after=()):
    width = heads * size
    half = len(pieces)
    count, model = pieces[0].shape
    last = base is not None
    norm = (
        (((count, model), f_type), ((half - 1, count, model), b_type))
        if last
        else (((half, count, model), f_type),)
    )
    return call(
        functools.partial(pool_back_kernel, rows, heads, size, half, len(weights), last),
        "pool_back",
        9,
        norm
        + (
            ((2 * width, model), b_type),
            ((2 * width, model), b_type),
            ((rows.weights, 128), f_type),
        ),
        (place,),
        (*pieces, *weights, small, d_pooled, d_table, d_proj, d_bias) + ((base,) if last else ()),
        scratch=(
            pltpu.VMEM((3, 10, 9, 8, 3 * width), f_type),
            pltpu.VMEM((3, 10, 9, 8, 3 * width), f_type),
            pltpu.VMEM((32, 3 * width), f_type),
            pltpu.VMEM((8, 7, 8, 3 * width), f_type),
            pltpu.VMEM((4 * width, model), b_type),
            pltpu.VMEM((32, 3 * width), f_type),
        ),
        after=after,
    )


def frame_of(token):
    return (token * 669) >> 15


def tap_matrix(group):
    frame = frame_of(iota((8, clip_rows), 1))
    return one_hot((frame & ((2 << group) - 1)) == iota((8, clip_rows), 0))


def slot_matrix(which, group):
    token = iota((clip_rows, slot_rows), 0)
    slot = iota((clip_rows, slot_rows), 1)
    frame = frame_of(token)
    line = (slot * 586) >> 15
    return one_hot(
        ((line >> 2) == which)
        & ((line & 3) == (frame >> (group + 1)))
        & (slot - 56 * line == token - 49 * frame)
    )


def compress_kernel(half, other, place, rows_ref, groups, bank_a, bank_b, taps_ref, out_ref):
    group = groups[clip_of(place, half) ^ other]
    spread = tap_matrix(group)
    slots = [slot_matrix(which, group) for which in range(2)]
    for kind in range(2):
        high, low = split(taps_ref[kind])
        factor = dot(high, spread) + dot(low, spread)
        total = None
        for which, bank in enumerate((bank_a, bank_b)):
            high, low = split(bank[0, kind].astype(f_type) * factor)
            part = dot(high, slots[which]) + dot(low, slots[which])
            total = part if total is None else total + part
        out_ref[kind] = total.astype(b_type)


def bank_spec(width, half, other, which):
    def where(step, place, rows_ref, groups):
        return rows_ref[clip_of(place, half) ^ other, which], 0, 0, 0

    return pl.BlockSpec((1, 2, width, clip_rows), where)


def whole_spec(shape):
    return pl.BlockSpec(shape, lambda *_: (0,) * len(shape))


def compress(half, scalars, bank, taps, other):
    width = bank.shape[2]
    return pl.pallas_call(
        functools.partial(compress_kernel, half, other),
        out_shape=jax.ShapeDtypeStruct((2, width, slot_rows), b_type),
        grid_spec=pltpu.PrefetchScalarGridSpec(
            num_scalar_prefetch=3,
            grid=(1,),
            in_specs=[bank_spec(width, half, other, which) for which in range(2)]
            + [whole_spec((2, width, 8))],
            out_specs=whole_spec((2, width, slot_rows)),
        ),
        compiler_params=pltpu.CompilerParams(vmem_limit_bytes=vmem_bytes),
        cost_estimate=pl.CostEstimate(flops=3 * 10**9, bytes_accessed=10**7, transcendentals=0),
        name="compress",
    )(*scalars, bank, bank, taps)


def compress_back_kernel(half, place, rows_ref, groups, *refs):
    banks, grads, out_ref = refs[:4], refs[4:6], refs[6]
    totals = [None, None]
    for other in range(2):
        group = groups[clip_of(place, half) ^ other]
        taps = tap_matrix(group)
        for which in range(2):
            slots = slot_matrix(which, group)
            for kind in range(2):
                bank = banks[2 * other + which][0, kind].astype(f_type)
                high, low = split(bank * dot_nt(grads[other][kind], slots))
                part = dot_nt(taps, high) + dot_nt(taps, low)
                totals[kind] = part if totals[kind] is None else totals[kind] + part
    for kind in range(2):
        out_ref[kind] = totals[kind]


def compress_back(half, scalars, bank, grad_here, grad_other):
    width = bank.shape[2]
    return pl.pallas_call(
        functools.partial(compress_back_kernel, half),
        out_shape=jax.ShapeDtypeStruct((2, 8, width), f_type),
        grid_spec=pltpu.PrefetchScalarGridSpec(
            num_scalar_prefetch=3,
            grid=(1,),
            in_specs=[
                bank_spec(width, half, other, which) for other in range(2) for which in range(2)
            ]
            + [whole_spec((2, width, slot_rows))] * 2,
            out_specs=whole_spec((2, 8, width)),
        ),
        compiler_params=pltpu.CompilerParams(vmem_limit_bytes=vmem_bytes),
        cost_estimate=pl.CostEstimate(flops=5 * 10**9, bytes_accessed=10**7, transcendentals=0),
        name="compress_back",
    )(*scalars, bank, bank, bank, bank, grad_here, grad_other)


def normal_rows(values):
    centered = values - jnp.mean(values, axis=-1, keepdims=True)
    inverse = lax.rsqrt(jnp.mean(centered * centered, axis=-1, keepdims=True) + eps_norm)
    return centered * inverse, inverse


def norm_back(normal, inverse, grad, gain):
    scaled = grad * gain
    return inverse * (
        scaled
        - jnp.mean(scaled, axis=-1, keepdims=True)
        - normal * jnp.mean(scaled * normal, axis=-1, keepdims=True)
    )


def column_sum(values):
    return jnp.sum(values, axis=0, keepdims=True)


def add_pieces(mine, others):
    total = mine[...]
    for other in others:
        total = total + other[0].astype(f_type)
    return total


def open_kernel(rows, heads, size, rows_ref, gain, shift, pool, table, bias, out_ref, small):
    normal, _ = normal_rows(rows_ref[...].astype(f_type))
    out_ref[...] = (normal * vector(gain) + vector(shift)).astype(b_type)
    for head in range(heads):
        for part in range(3):
            start = 32 * (3 * head + part)
            for tap in range(27):
                small[start + tap : start + tap + 1, 0:size] = pool[part, tap, head : head + 1, :]
        start = rows.table + 48 * head
        for slot in range(41):
            small[start + slot : start + slot + 1, 0:size] = table[slot, head : head + 1, :]
    small[rows.bias : rows.bias + rows.units, :] = bias[...]


def second_norm_kernel(half, rows_ref, mine, *refs):
    others = refs[: half - 1]
    bias, gain, shift, mid_ref, out_ref = refs[half - 1 :]
    midway = rows_ref[...].astype(f_type) + (add_pieces(mine, others) + vector(bias))
    mid_ref[...] = midway
    normal, _ = normal_rows(midway)
    out_ref[...] = (normal * vector(gain) + vector(shift)).astype(b_type)


def second_back_kernel(half, mid_ref, mine, *refs):
    others = refs[: half - 1]
    top_ref, gain, d_mid_ref, d_low_ref, sums_ref = refs[half - 1 :]
    normal, inverse = normal_rows(mid_ref[...])
    grad = add_pieces(mine, others)
    top = top_ref[...].astype(f_type)
    d_mid = top + norm_back(normal, inverse, grad, vector(gain))
    d_mid_ref[...] = d_mid
    d_low = d_mid.astype(b_type)
    d_low_ref[...] = d_low
    put_row(sums_ref, 0, column_sum(d_low.astype(f_type)))
    put_row(sums_ref, 8, column_sum(grad * normal))
    put_row(sums_ref, 16, column_sum(grad))
    put_row(sums_ref, 24, column_sum(top))


def first_back_kernel(rows, heads, size, half, rows_ref, d_mid_ref, gain, mine, *refs):
    others = refs[: half - 1]
    refs = refs[half - 1 :]
    mid_ref, down_bias, mlp_mine = refs[:3]
    mlp_others = refs[3 : 2 + half]
    small_a, small_b, comp, sums, out_ref, y_ref, late = refs[2 + half :]
    normal, inverse = normal_rows(rows_ref[...].astype(f_type))
    grad = add_pieces(mine, others)
    out_ref[...] = d_mid_ref[...] + norm_back(normal, inverse, grad, vector(gain))
    y_ref[...] = (mid_ref[...] + add_pieces(mlp_mine, mlp_others) + vector(down_bias)).astype(b_type)
    late[0 : rows.weights, :] = small_a[...] + small_b[...]
    for head in range(heads):
        for part in range(2):
            start = rows.comp + 8 * (2 * head + part)
            late[start : start + 8, 0:size] = comp[part, :, head * size : (head + 1) * size]
    late[rows.sums : rows.sums + 32, :] = sums[...]
    put_row(late, rows.sums + 32, column_sum(grad * normal))
    put_row(late, rows.sums + 40, column_sum(grad))


def close_kernel(rows, heads, size, late, *refs):
    pool, table, comp, bias = refs[:4]
    for head in range(heads):
        for part in range(3):
            start = 32 * (3 * head + part)
            for tap in range(27):
                pool[part, tap, head : head + 1, :] = late[start + tap : start + tap + 1, 0:size]
        start = rows.table + 48 * head
        for slot in range(41):
            table[slot, head : head + 1, :] = late[start + slot : start + slot + 1, 0:size]
        for part in range(2):
            start = rows.comp + 8 * (2 * head + part)
            comp[head, part] = late[start : start + 8, 0:size]
    bias[...] = late[rows.bias : rows.bias + rows.units, :]


def error_function(values):
    x = jnp.clip(values, -4.0, 4.0)
    y = x * x
    top = -2.72614225801306e-10
    for term in (
        2.77068142495902e-08,
        -2.10102402082508e-06,
        -5.69250639462346e-05,
        -7.34990630326855e-04,
        -2.95459980854025e-03,
        -1.60960333262415e-02,
    ):
        top = top * y + term
    low = -1.45660718464996e-05
    for term in (
        -2.13374055278905e-04,
        -1.68282697438203e-03,
        -7.37332916720468e-03,
        -1.42647390514189e-02,
    ):
        low = low * y + term
    return x * top / low


def mlp_kernel(rows, half, flip, part, place, *refs):
    pieces, tops = refs[:half], refs[half : 2 * half]
    refs = refs[2 * half :]
    up, down = refs[:2]
    halves = refs[2:4]
    (
        bias, small, y_mine, y_other, d_mine, d_other,
        left_keep, right_keep, left_send, right_send, sums,
        tokens_all, top_all, far, y_all, d_all,
    ) = refs[4:]
    put_halves(far, place, halves)
    ups = halves[0].shape[0]
    count = pieces[0].shape[0]
    tokens = jnp.concatenate([piece[...].astype(f_type) for piece in pieces], axis=0).astype(b_type)
    top = jnp.concatenate([piece[...].astype(f_type) for piece in tops], axis=0).astype(b_type)
    units = down.shape[0]
    y_all[...] = jnp.zeros(y_all.shape, f_type)
    d_all[...] = jnp.zeros(d_all.shape, f_type)
    even = core_of(place) == 0
    for block in range(2):
        first = up if block == 0 else far.at[0:ups]
        second = down if block == 0 else far.at[ups : 2 * ups]
        shift = wide_row(bias, 0, rows.units) if block == 0 else wide_row(small, rows.bias, rows.units)
        for start in range(0, units, part):
            here = slice(start, start + part)
            if flip:
                hidden = dot_nt(tokens, first[here, :]) + shift[:, here]
            else:
                hidden = dot(tokens, first[:, here]) + shift[:, here]
            half_slope = 0.5 * (1.0 + error_function(hidden * (0.5**0.5)))
            slope = half_slope + hidden * jnp.exp(-0.5 * hidden * hidden) * 0.3989422804014327
            act = (hidden * half_slope).astype(b_type)
            d_hid = (dot_nt(top, second[here, :]) * slope).astype(b_type)
            put_row(sums, 8 * block + start // 128, column_sum(d_hid.astype(f_type)))
            y_all[...] += dot(act, second[here, :])
            if flip:
                d_all[...] += dot(d_hid, first[here, :])
            else:
                d_all[...] += dot_nt(d_hid, first[:, here])

            def store(keep, send, here=here, act=act, d_hid=d_hid, block=block):
                keep[0 if flip else 1][block, :, here] = d_hid
                send[0][block, :, here] = act

            @pl.when(even)
            def _():
                store((left_keep, right_keep), (left_send, right_send))

            @pl.when(jnp.logical_not(even))
            def _():
                store((left_send, right_send), (left_keep, right_keep))

        def fixed(keep, send, block=block):
            keep[1 if flip else 0][block] = tokens
            send[1][block] = top

        @pl.when(even)
        def _():
            fixed((left_keep, right_keep), (left_send, right_send))

        @pl.when(jnp.logical_not(even))
        def _():
            fixed((left_send, right_send), (left_keep, right_keep))

    y_mine[...] = y_all[0:count, :]
    d_mine[...] = d_all[0:count, :]
    for step in range(1, half):
        span = slice(step * count, (step + 1) * count)
        y_other[step - 1] = y_all[span, :].astype(b_type)
        d_other[step - 1] = d_all[span, :].astype(b_type)


def mlp(rows, flip, place, pieces, tops, up, down, chunks, bias, small, after=()):
    half = len(pieces)
    count, model = pieces[0].shape
    total = half * count
    units = down.shape[0]
    part = 256 if units % 256 == 0 else units
    left = ((2, total, units if flip else model), b_type)
    down_left = ((2, total, units), b_type)
    right = ((2, total, model), b_type)
    assert left == down_left
    return call(
        functools.partial(mlp_kernel, rows, half, flip, part),
        "mlp",
        12,
        (
            ((count, model), f_type),
            ((half - 1, count, model), b_type),
            ((count, model), f_type),
            ((half - 1, count, model), b_type),
            left,
            right,
            left,
            right,
            ((16, 128), f_type),
        ),
        (place,),
        (*pieces, *tops, up, down, *chunks, bias, small),
        scratch=(
            pltpu.VMEM((total, model), b_type),
            pltpu.VMEM((total, model), b_type),
            pltpu.VMEM((2 * chunks[0].shape[0], model), b_type),
            pltpu.VMEM((total, model), f_type),
            pltpu.VMEM((total, model), f_type),
        ),
        after=after,
    )


def swap_pairs(count, bit):
    return [(place, place ^ bit) for place in range(count)]


class Team:
    def __init__(self, heads_count, clips_count):
        self.total = heads_count
        self.half = heads_count // 2
        self.clips = clips_count
        self.here = lax.axis_index("head")
        self.clip = self.here // self.half
        self.seat = self.here % self.half
        self.spot = lax.axis_index("clip")

    def partner(self, values):
        return lax.ppermute(values, "head", swap_pairs(self.total, self.half))

    def seats(self, values, step):
        return lax.ppermute(values, "head", swap_pairs(self.total, step))

    def swap(self, values, bit):
        return lax.ppermute(values, "clip", swap_pairs(self.clips, bit))

    def gather(self, rows):
        return [rows] + [self.seats(rows, step) for step in range(1, self.half)]

    def scatter(self, others):
        return [self.seats(others[step - 1 : step], step) for step in range(1, self.half)]

    def eighth(self):
        return (self.spot & 1) * 4 + self.seat_in((2, 4))

    def share(self, came):
        mine = self.collect(came, (2, 4))
        return [mine, self.swap(mine, 1)]

    def quads(self):
        bit, found = 2, []
        while bit < self.clips:
            found.append((bit, 2 * bit))
            bit *= 4
        return found

    def seat_in(self, quad):
        return (self.spot // quad[0]) % 2 + 2 * ((self.spot // quad[1]) % 2)

    def peer(self, values, quad, step):
        return self.swap(values, (step & 1) * quad[0] + (step >> 1) * quad[1])

    def cut(self, values, quad):
        size = values[0].shape[-2] // 4
        seat = self.seat_in(quad)

        def quarter(place):
            total = None
            for item in values:
                part = lax.dynamic_slice_in_dim(item, place * size, size, axis=-2).astype(f_type)
                total = part if total is None else total + part
            return total

        return [quarter(seat)] + [quarter(seat ^ step).astype(b_type) for step in (1, 2, 3)]

    def collect(self, chunk, quad):
        seat = self.seat_in(quad)
        pieces = [chunk] + [self.peer(chunk, quad, step) for step in (1, 2, 3)]
        return jnp.concatenate(
            [lax.select_n((seat ^ place).astype(jnp.int32), *pieces) for place in range(4)], axis=0
        )

    def reduce(self, keep, send):
        values, sent = [keep, self.swap(send, 1)], ()
        for quad in self.quads():
            values = self.cut(values, quad)
            sent = sent or tuple(values)
            values = [values[0]] + [self.peer(values[step], quad, step) for step in (1, 2, 3)]
        return values, sent

    def finish(self, chunk):
        for quad in reversed(self.quads()):
            chunk = self.collect(chunk, quad)
        other = self.swap(chunk, 1)
        odd = (self.spot & 1) != 0
        return jnp.where(odd, other, chunk), jnp.where(odd, chunk, other)


def add(values):
    total = values[0].astype(f_type)
    for item in values[1:]:
        total = total + item.astype(f_type)
    return total


def on_device(
    heads_total,
    clips_total,
    inputs,
    ln1_gain,
    ln1_bias,
    w_qkv,
    pool_kernel,
    rel_table,
    comp_kernel,
    memory_bank,
    mem_index,
    clip_group,
    w_proj,
    proj_bias,
    ln2_gain,
    ln2_bias,
    w_up,
    up_bias,
    w_down,
    down_bias,
    cotangent,
):
    team = Team(heads_total, clips_total)
    half = team.half
    heads, _, size = rel_table.shape
    count, model = inputs.shape
    units = w_up.shape[1]
    width = heads * size
    rows = Rows(heads, units, model)
    flip = units != model
    lined = [
        item.reshape(model // 128, 128)
        for item in (ln1_gain, ln1_bias, proj_bias, ln2_gain, ln2_bias, down_bias)
    ]
    gain1, shift1, bias_proj, gain2, shift2, bias_down = lined
    bias_up = up_bias.reshape(units // 128, 128)
    w_qkv = w_qkv.T
    if flip:
        w_up = w_up.T
    bank = memory_bank.transpose(0, 1, 3, 2)
    place = jnp.stack([team.here, team.spot])
    scalars = (place, mem_index, clip_group)

    norm1, small = call(
        functools.partial(open_kernel, rows, heads, size),
        "open",
        2,
        (((count, model), b_type), ((rows.weights, 128), f_type)),
        (),
        (
            inputs,
            gain1,
            shift1,
            pool_kernel.transpose(1, 2, 0, 3),
            rel_table.transpose(1, 0, 2),
            bias_up,
        ),
    )
    tokens1 = team.gather(norm1)
    eighth = team.eighth()
    part = width // 2
    chunk_a = jnp.where(
        eighth < 6,
        lax.dynamic_slice_in_dim(w_qkv, jnp.minimum(eighth, 5) * part, part, axis=0),
        lax.dynamic_slice_in_dim(w_proj, (eighth & 1) * part, part, axis=0),
    )
    part = units // 4
    chunk_b = jnp.where(
        eighth < 4,
        lax.dynamic_slice_in_dim(w_up, (eighth & 3) * part, part, axis=0),
        lax.dynamic_slice_in_dim(w_down, (eighth & 3) * part, part, axis=0),
    )
    came_a = team.partner(chunk_a)
    comp_taps = comp_kernel.transpose(1, 0, 3, 2).reshape(2, width, 8)
    mem_far = team.partner(compress(half, scalars, bank, comp_taps, 1))
    mem_here = compress(half, scalars, bank, comp_taps, 0)
    small_far = team.partner(small)
    came_b = team.partner(chunk_b)
    tops = team.gather(cotangent)
    chunks_a = team.share(came_a)
    chunks_b = team.share(came_b)

    weights_here = (w_qkv, w_proj)
    branch, pooled_here, probs_here, heads_here = attend(
        rows, heads, size, place, clip_group, tokens1, weights_here, small, mem_here,
        after=(came_a, chunk_b),
    )
    branch, branch_other, weights, pooled_far, probs_far, heads_far = attend(
        rows, heads, size, place, clip_group, tokens1, chunks_a, small_far, mem_far, base=branch,
        after=(*tops,),
    )
    weights_far = (weights,)
    branch_came = team.scatter(branch_other)
    midway, norm2 = call(
        functools.partial(second_norm_kernel, half),
        "second_norm",
        2,
        (((count, model), f_type), ((count, model), b_type)),
        (),
        (inputs, branch, *branch_came, bias_proj, gain2, shift2),
    )
    tokens2 = team.gather(norm2)
    y, y_other, d_norm2, d_norm2_other, left_k, right_k, left_s, right_s, d_bias = mlp(
        rows, flip, place, tokens2, tops, w_up, w_down, chunks_b, bias_up, small_far
    )
    d_norm2_came = team.scatter(d_norm2_other)
    y_came = team.scatter(y_other)

    def product(a, b):
        return lax.dot_general(
            a, b, (((1,), (1,)), ((0,), (0,))), preferred_element_type=f_type
        ).astype(b_type)

    send_m = product(left_s, right_s)
    keep_m = product(left_k, right_k)
    sums_m, sent_m = team.reduce(keep_m, send_m)
    d_mid, d_branch, sums2 = call(
        functools.partial(second_back_kernel, half),
        "second_back",
        3,
        (((count, model), f_type), ((count, model), b_type), ((32, 128), f_type)),
        (),
        (midway, d_norm2, *d_norm2_came, cotangent, gain2),
    )
    d_branches = team.gather(d_branch)

    d_pooled, d_mem_far, d_table, d_proj = scores_back(
        rows, heads, size, place, d_branches, weights_far, small_far, mem_far, pooled_far,
        probs_far, heads_far, after=(*sent_m, *y_came),
    )
    d_mem_back = team.partner(d_mem_far)
    d_norm1, keep_f, send_f, grads_far = pool_back(
        rows, heads, size, place, tokens1, weights_far, small_far, d_pooled, d_table, d_proj,
        d_bias[8:16],
    )
    sums_f, sent_f = team.reduce(keep_f, send_f)
    grads_came = team.partner(grads_far)
    sum_m = add(sums_m)
    part_m = sum_m[1].astype(b_type)
    chunk_m = (sum_m[0] + team.partner(part_m).astype(f_type)).astype(b_type)
    d_pooled, d_mem_here, d_table, d_proj = scores_back(
        rows, heads, size, place, d_branches, weights_here, small, mem_here, pooled_here,
        probs_here, heads_here, after=(d_norm1, part_m),
    )
    d_norm1, d_norm1_other, keep_o, send_o, grads_here = pool_back(
        rows, heads, size, place, tokens1, weights_here, small, d_pooled, d_table, d_proj,
        d_bias[0:8], base=d_norm1, after=(chunk_m, *sent_f, d_mem_back, grads_came),
    )
    d_norm1_came = team.scatter(d_norm1_other)
    g_up, g_down = team.finish(chunk_m)
    sums_o, _ = team.reduce(keep_o, send_o)
    came_f = team.partner(add(sums_f).astype(b_type))
    chunk_o = add([*sums_o, came_f]).astype(b_type)
    g_a, g_b = team.finish(chunk_o)
    g_comp = compress_back(half, scalars, bank, d_mem_here, d_mem_back)
    grad_inputs, output, late = call(
        functools.partial(first_back_kernel, rows, heads, size, half),
        "first_back",
        3,
        (((count, model), f_type), ((count, model), b_type), ((rows.total, 128), f_type)),
        (),
        (
            inputs, d_mid, gain1, d_norm1, *d_norm1_came, midway, bias_down, y, *y_came,
            grads_here, grads_came, g_comp, sums2,
        ),
    )
    late = late + team.swap(late, 1)
    for quad in team.quads():
        late = add([late] + [team.peer(late, quad, step) for step in (1, 2, 3)])
    sums = late[rows.sums :]
    sums = add([sums] + [team.seats(sums, step) for step in range(1, team.total)])
    g_pool, g_rel, g_comp, g_bias = call(
        functools.partial(close_kernel, rows, heads, size),
        "close",
        1,
        (
            ((3, 27, heads, size), f_type),
            ((41, heads, size), f_type),
            ((heads, 2, 8, size), f_type),
            ((units // 128, 128), f_type),
        ),
        (),
        (late,),
    )
    g_attn = jnp.concatenate([g_a, g_b], axis=0).astype(f_type)
    g_up, g_down = g_up.astype(f_type), g_down.astype(f_type)
    if flip:
        g_up = g_up.T

    def total(index):
        return sums[8 * index : 8 * index + model // 128].reshape(model)

    return (
        output,
        grad_inputs,
        total(4),
        total(5),
        g_attn[: 3 * width].T,
        g_pool.transpose(2, 0, 1, 3),
        g_rel.transpose(1, 0, 2),
        g_comp,
        g_attn[3 * width :],
        total(0),
        total(1),
        total(2),
        g_up,
        g_bias.reshape(units),
        g_down,
        total(3),
    )


def solution(mesh):
    return jax.shard_map(
        functools.partial(on_device, mesh.shape["head"], mesh.shape["clip"]),
        mesh=mesh,
        in_specs=(
            P(("clip", "head"), None),
            P(),
            P(),
            P(None, "head"),
            P("head", None, None, None),
            P("head", None, None),
            P("head", None, None, None),
            P("clip", None, None, "head"),
            P("clip", None),
            P("clip"),
            P("head", None),
            P(),
            P(),
            P(),
            P(None, "head"),
            P("head"),
            P("head", None),
            P(),
            P(("clip", "head"), None),
        ),
        out_specs=(
            P(("clip", "head"), None),
            P(("clip", "head"), None),
            P(),
            P(),
            P(None, "head"),
            P("head", None, None, None),
            P("head", None, None),
            P("head", None, None, None),
            P("head", None),
            P(),
            P(),
            P(),
            P(None, "head"),
            P("head"),
            P("head", None),
            P(),
        ),
        check_vma=False,
    )
```

```python
import functools

import jax
import jax.numpy as jnp
from jax import lax
from jax.experimental import pallas as pl
from jax.experimental.pallas import tpu as pltpu
from jax.sharding import PartitionSpec as P

f_type = jnp.float32
b_type = jnp.bfloat16
eps_norm = 1e-06
neg_large = -1000000000.0
clip_rows = 392
grid_rows = 448
slot_rows = 448
vmem_bytes = 56 * 1024 * 1024


def dot(a, b):
    return jnp.dot(a, b, preferred_element_type=f_type)


def dot_nt(a, b):
    return lax.dot_general(a, b, (((1,), (1,)), ((), ())), preferred_element_type=f_type)


def iota(shape, axis):
    return lax.broadcasted_iota(jnp.int32, shape, axis)


def one_hot(flag):
    return jnp.where(flag, 1.0, 0.0).astype(b_type)


def split(values):
    high = values.astype(b_type)
    return high, (values - high.astype(f_type)).astype(b_type)


def aligned(start, step):
    return pl.multiple_of(start, step)


def call(kernel, name, cost, results, scalars, arrays, scratch=(), after=()):
    def body(*refs):
        kept = refs[: len(scalars) + len(arrays)]
        kernel(*kept, *refs[len(kept) + len(after) :])

    return pl.pallas_call(
        body,
        out_shape=tuple(jax.ShapeDtypeStruct(shape, kind) for shape, kind in results),
        in_specs=[pl.BlockSpec(memory_space=pltpu.SMEM)] * len(scalars)
        + [pl.BlockSpec(memory_space=pltpu.VMEM)] * len(arrays)
        + [pl.BlockSpec(memory_space=pl.ANY)] * len(after),
        out_specs=tuple(pl.BlockSpec(memory_space=pltpu.VMEM) for _ in results),
        scratch_shapes=list(scratch),
        compiler_params=pltpu.CompilerParams(vmem_limit_bytes=vmem_bytes),
        cost_estimate=pl.CostEstimate(
            flops=int(cost * 1e10), bytes_accessed=int(cost * 3e7), transcendentals=0
        ),
        name=name,
    )(*scalars, *arrays, *after)


def spread_matrix(start, count):
    row = iota((grid_rows, count), 0)
    place = row & 7
    return one_hot(
        ((row >> 3) * 7 + place - start == iota((grid_rows, count), 1)) & (place < 7)
    )


def gather_matrix(start, count):
    row = iota((count, grid_rows), 1)
    place = row & 7
    return one_hot(
        ((row >> 3) * 7 + place - start == iota((count, grid_rows), 0)) & (place < 7)
    )


def to_grid(seat, pieces):
    total = None
    for step, piece in enumerate(pieces):
        rows = piece.shape[0]
        part = dot(spread_matrix((seat ^ step) * rows, rows), piece[...])
        total = part if total is None else total + part
    return total.astype(b_type)


def row_coords(shape, axis):
    row = iota(shape, axis)
    line = row >> 3
    frame = (line * 37) >> 8
    return frame, line - frame * 7, row & 7


def coord_of(kind, coords):
    frame, line, place = coords
    return jnp.where(kind == 0, frame, jnp.where(kind == 1, line, place))


def query_mask():
    shape = (grid_rows, 192)
    column = iota(shape, 1)
    coord = coord_of(column >> 6, row_coords(shape, 0))
    return jnp.where(((column >> 3) & 7) == coord, 1.0, 0.0)


def key_matrix():
    shape = (192, grid_rows)
    column = iota(shape, 0)
    coord = coord_of(column >> 6, row_coords(shape, 1))
    return one_hot((column & 7) == coord)


def key_places():
    shape = (grid_rows, 192)
    column = iota(shape, 1)
    coord = coord_of(column >> 6, row_coords(shape, 0))
    return one_hot((column & 7) == coord)


def table_slot(column):
    kind = column >> 6
    at_query = (column >> 3) & 7
    at_key = column & 7
    base = jnp.where(kind == 0, 7, jnp.where(kind == 1, 21, 34))
    valid = (kind == 0) | ((at_query < 7) & (at_key < 7))
    return jnp.where(valid, base + at_query - at_key, -1)


def table_matrix():
    return one_hot(table_slot(iota((192, 41), 0)) == iota((192, 41), 1))


def own_bias(shape, axis):
    return jnp.where((iota(shape, axis) & 7) == 7, neg_large, 0.0)


def mem_bias(shape, axis, limit):
    slot = iota(shape, axis)
    line = (slot * 586) >> 15
    return jnp.where((slot - 56 * line < 49) & ((line & 3) < limit), 0.0, neg_large)


def clear_border(field):
    width = field.shape[-1]
    field[:, 0:1] = jnp.zeros((3, 1, 9, 8, width), f_type)
    field[:, 9:10] = jnp.zeros((3, 1, 9, 8, width), f_type)
    field[:, :, 0:1] = jnp.zeros((3, 10, 1, 8, width), f_type)
    field[:, :, 8:9] = jnp.zeros((3, 10, 1, 8, width), f_type)


def fill_field(field, values):
    width = values.shape[-1]
    lines = values.reshape(56, 8, width)
    field[0, 1:9, 1:8] = pltpu.roll(lines, 1, 1).reshape(8, 7, 8, width)
    field[1, 1:9, 1:8] = lines.reshape(8, 7, 8, width)
    field[2, 1:9, 1:8] = pltpu.roll(lines, 7, 1).reshape(8, 7, 8, width)


def convolve(field, taps, result, flip):
    width = field.shape[-1]
    for start in range(0, width, 128):
        lanes = slice(start, min(start + 128, width))

        def frame(t, carry):
            total = jnp.zeros((7, 8, lanes.stop - lanes.start), f_type)
            for dt in range(3):
                for dw in range(3):
                    near = field[dw, t + dt, :, :, lanes]
                    for dh in range(3):
                        tap = dt * 9 + dh * 3 + dw
                        tap = 26 - tap if flip else tap
                        total = total + near[dh : dh + 7] * taps[tap : tap + 1, lanes]
            result[t, :, :, lanes] = total
            return carry

        lax.fori_loop(0, 8, frame, 0, unroll=8)


def tap_grads(field, grads, result):
    width = field.shape[-1]
    for start in range(0, width, 128):
        lanes = slice(start, min(start + 128, width))
        size = lanes.stop - lanes.start

        def frame(t, sums):
            grad = grads[1, t + 1, 1:8, :, lanes]
            sums = list(sums)
            for dt in range(3):
                for dw in range(3):
                    near = field[dw, t + dt, :, :, lanes]
                    for dh in range(3):
                        tap = dt * 9 + dh * 3 + dw
                        sums[tap] = sums[tap] + jnp.sum(near[dh : dh + 7] * grad, axis=0)
            return tuple(sums)

        sums = lax.fori_loop(
            0, 8, frame, tuple(jnp.zeros((8, size), f_type) for _ in range(27)), unroll=8
        )
        for tap in range(27):
            result[tap : tap + 1, lanes] = jnp.sum(sums[tap], axis=0, keepdims=True)


class Rows:
    def __init__(self, heads, units, width):
        self.taps = 0
        self.table = self.taps + 96 * heads
        self.bias = self.table + 48 * heads
        self.weights = self.bias + 8
        self.comp = 48
        self.late = self.comp + 16 * heads
        self.units = units // 128
        self.width = width // 128
        self.extra = 64
        self.used = 32 * self.width * 2
        assert self.weights <= self.used


def wide_row(ref, start, count):
    return jnp.concatenate([ref[start + k : start + k + 1, :] for k in range(count)], axis=1)


def put_row(ref, start, values):
    for k in range(values.shape[1] // 128):
        ref[start + k : start + k + 1, :] = values[:, 128 * k : 128 * k + 128]


def vector(ref):
    return wide_row(ref, 0, ref.shape[0])


def seat_of(place, half):
    return place[0] & (half - 1)


def clip_of(place, half):
    return place[0] >> (half.bit_length() - 1)


def core_of(place):
    return place[1] & 1


def put_halves(whole, place, halves):
    size = halves[0].shape[0]
    for step, item in enumerate(halves):
        whole[pl.ds(aligned((core_of(place) ^ step) * size, size), size), :] = item[...]


def weight_views(refs, width):
    if len(refs) == 2:
        return refs[0], refs[1]
    return refs[0].at[0 : 3 * width], refs[0].at[3 * width : 4 * width]


def load_taps(taps, small, heads, size):
    for index in range(3 * heads):
        taps[0:27, index * size : (index + 1) * size] = small[
            32 * index : 32 * index + 27, 0:size
        ]


def pool_forward_kernel(heads, size, half, far, place, *refs):
    refs = list(refs)
    pieces = refs[:half]
    del refs[:half]
    if far:
        halves = refs[:2]
        small, pooled_ref, weights, field, taps, wide = refs[2:]
        put_halves(weights, place, halves)
    else:
        weights, small, pooled_ref, field, taps, wide = refs
    width = heads * size
    clear_border(field)
    load_taps(taps, small, heads, size)
    fill_field(
        field, dot_nt(to_grid(seat_of(place, half), pieces), weights[0 : 3 * width, :])
    )
    convolve(field, taps, wide, False)
    filled = (iota((grid_rows, 1), 0) & 7) < 7
    pooled_ref[...] = jnp.where(
        filled, wide[...].reshape(grid_rows, 3 * width), 0.0
    ).astype(b_type)


def pool_forward(heads, size, place, pieces, weights, small, after=()):
    width = heads * size
    half = len(pieces)
    model = pieces[0].shape[1]
    far = len(weights) == 2
    return call(
        functools.partial(pool_forward_kernel, heads, size, half, far),
        "pool_forward",
        6,
        (((grid_rows, 3 * width), b_type),)
        + ((((4 * width, model), b_type),) if far else ()),
        (place,),
        (*pieces, *weights, small),
        scratch=(
            pltpu.VMEM((3, 10, 9, 8, 3 * width), f_type),
            pltpu.VMEM((32, 3 * width), f_type),
            pltpu.VMEM((8, 7, 8, 3 * width), f_type),
        ),
        after=after,
    )


def attend_kernel(rows, heads, size, half, far, place, groups, *refs):
    refs = list(refs)
    small, mem, pooled, weights = refs[:4]
    del refs[:4]
    base = refs.pop(0)
    if far:
        mine_ref, other_ref = refs.pop(0), refs.pop(0)
    else:
        branch_ref, copy_ref = refs.pop(0), refs.pop(0)
        copy_ref[...] = base[...]
    probs_ref, head_ref, query_wide, key_wide, mem_wide, head_wide = refs
    width = heads * size
    scale = size ** (-0.5)
    seat = seat_of(place, half)
    w_proj = weight_views((weights,), width)[1] if far else weights
    rest = 128 - size
    ones = (iota((grid_rows, rest), 1) == 0).astype(f_type)
    query_wide[:, size:128] = ones.astype(b_type)
    key_wide[:, size:128] = (ones * own_bias((grid_rows, rest), 0)).astype(b_type)
    first = (iota((rest, grid_rows), 0) == 0).astype(f_type)
    limit = 4 >> groups[clip_of(place, half)]
    mem_wide[size:128, :] = (first * mem_bias((rest, grid_rows), 1, limit)).astype(b_type)
    keys_at = key_places()
    key_wide[:, 128:320] = keys_at
    key_wide[:, 320:512] = keys_at
    expand = table_matrix()
    mask = query_mask() * (1.0 / scale)
    for head in range(heads):
        at = 3 * head * size
        lanes = slice(head * size, (head + 1) * size)
        queries = pooled[:, at : at + size]
        values = pooled[:, at + 2 * size : at + 3 * size]
        start = rows.table + 48 * head
        table_high, table_low = split(small[start : start + 41, 0:size])
        rel = dot_nt(queries, dot(expand, table_high).astype(b_type)) + dot_nt(
            queries, dot(expand, table_low).astype(b_type)
        )
        high, low = split(rel * mask)
        query_wide[:, 0:size] = queries
        query_wide[:, 128:320] = high
        query_wide[:, 320:512] = low
        key_wide[:, 0:size] = pooled[:, at + size : at + 2 * size]
        mem_wide[0:size, :] = mem[0, lanes, :]
        own = dot_nt(query_wide[...], key_wide[...])
        far_scores = dot(query_wide[:, 0:128], mem_wide[...])
        top = jnp.maximum(
            jnp.max(own, axis=-1, keepdims=True), jnp.max(far_scores, axis=-1, keepdims=True)
        )
        own = jnp.exp((own - top) * scale)
        far_scores = jnp.exp((far_scores - top) * scale)
        total = jnp.sum(own, axis=-1, keepdims=True) + jnp.sum(far_scores, axis=-1, keepdims=True)
        inverse = 1.0 / total
        own = own * inverse
        far_scores = far_scores * inverse
        probs_ref[head, 0] = own
        probs_ref[head, 1] = far_scores
        attended = dot(own.astype(b_type), values) + dot_nt(
            far_scores.astype(b_type), mem[1, lanes, :]
        )
        head_wide[:, lanes] = attended + queries.astype(f_type)
    head_ref[...] = head_wide[...].astype(b_type)
    count = base.shape[1] if far else branch_ref.shape[1]
    for step in range(half):
        head_out = dot(gather_matrix((seat ^ step) * count, count), head_ref[...]).astype(b_type)
        part = dot(head_out, w_proj[...])
        if not far:
            branch_ref[step] = part
        elif step == 0:
            mine_ref[...] = part + base[0]
        else:
            other_ref[step - 1] = (part + base[step]).astype(b_type)


def attend(rows, heads, size, half, place, groups, small, mem, pooled, weights, base, after=()):
    width = heads * size
    model = weights.shape[1]
    count = clip_rows // half
    far = base.dtype == f_type
    branch = (
        (((count, model), f_type), ((half - 1, count, model), b_type))
        if far
        else (((half, count, model), f_type), (base.shape, base.dtype))
    )
    return call(
        functools.partial(attend_kernel, rows, heads, size, half, far),
        "attend",
        10,
        branch
        + (((heads, 2, grid_rows, grid_rows), f_type), ((grid_rows, width), b_type)),
        (place, groups),
        (small, mem, pooled, weights, base),
        scratch=(
            pltpu.VMEM((grid_rows, 512), b_type),
            pltpu.VMEM((grid_rows, 512), b_type),
            pltpu.VMEM((128, grid_rows), b_type),
            pltpu.VMEM((grid_rows, width), f_type),
        ),
        after=after,
    )


def scores_back_kernel(rows, heads, size, half, parts, *refs):
    place = refs[0]
    pieces = refs[1 : 1 + half]
    weights = refs[1 + half : 1 + half + parts]
    (
        small, mem, pooled_ref, probs_ref, head_ref,
        d_pooled, d_mem_ref, d_table_ref, d_proj_ref,
        d_head_ref, d_low_ref, probs_low, d_scores,
    ) = refs[1 + half + parts :]
    width = heads * size
    scale = size ** (-0.5)
    w_proj = weight_views(weights, width)[1]
    d_branch = to_grid(seat_of(place, half), pieces)
    d_head = dot_nt(d_branch, w_proj[...])
    d_head_ref[...] = d_head
    d_low_ref[...] = d_head.astype(b_type)
    expand = table_matrix()
    keys_at = key_matrix()
    mask = query_mask()
    for head in range(heads):
        at = 3 * head * size
        lanes = slice(head * size, (head + 1) * size)
        queries = pooled_ref[:, at : at + size]
        keys = pooled_ref[:, at + size : at + 2 * size]
        values = pooled_ref[:, at + 2 * size : at + 3 * size]
        mem_keys = mem[0, lanes, :]
        mem_values = mem[1, lanes, :]

        d_att = d_low_ref[:, lanes]
        own = probs_ref[head, 0]
        far_probs = probs_ref[head, 1]
        d_own = dot_nt(d_att, values)
        d_far = dot(d_att, mem_values)
        inner = jnp.sum(own * d_own, axis=-1, keepdims=True) + jnp.sum(
            far_probs * d_far, axis=-1, keepdims=True
        )
        d_scores[0] = (own * (d_own - inner)).astype(b_type)
        d_scores[1] = (far_probs * (d_far - inner)).astype(b_type)
        probs_low[0] = own.astype(b_type)
        probs_low[1] = far_probs.astype(b_type)
        d_query = (dot(d_scores[0], keys) + dot_nt(d_scores[1], mem_keys)) * scale
        start = rows.table + 48 * head
        table_high, table_low = split(small[start : start + 41, 0:size])
        rel_high, rel_low = split(dot_nt(d_scores[0], keys_at) * mask)
        wide_high = dot(expand, table_high).astype(b_type)
        wide_low = dot(expand, table_low).astype(b_type)
        d_rel = dot(rel_high, wide_high) + dot(rel_low, wide_high) + dot(rel_high, wide_low)
        d_pooled[:, at : at + size] = d_query + d_head_ref[:, lanes] + d_rel
        queries_t = jnp.transpose(queries.astype(f_type)).astype(b_type)
        d_att_t = jnp.transpose(d_head_ref[:, lanes]).astype(b_type)
        wide_high, wide_low = split(dot(queries_t, rel_high) + dot(queries_t, rel_low))
        d_table = dot(wide_high, expand) + dot(wide_low, expand)
        d_table_ref[48 * head : 48 * head + 41, 0:size] = jnp.transpose(d_table)
        d_pooled[:, at + size : at + 2 * size] = jnp.transpose(dot(queries_t, d_scores[0])) * scale
        d_mem_ref[0, lanes, :] = (dot(queries_t, d_scores[1]) * scale).astype(b_type)
        d_pooled[:, at + 2 * size : at + 3 * size] = jnp.transpose(dot(d_att_t, probs_low[0]))
        d_mem_ref[1, lanes, :] = dot(d_att_t, probs_low[1]).astype(b_type)
    head_t = jnp.transpose(head_ref[...].astype(f_type)).astype(b_type)
    d_proj_ref[...] = dot(head_t, d_branch).astype(b_type)


def scores_back(rows, heads, size, place, pieces, weights, small, mem, pooled, probs, head, after=()):
    width = heads * size
    return call(
        functools.partial(scores_back_kernel, rows, heads, size, len(pieces), len(weights)),
        "scores_back",
        13,
        (
            ((grid_rows, 3 * width), f_type),
            ((2, width, slot_rows), b_type),
            ((48 * heads, 128), f_type),
            ((width, pieces[0].shape[1]), b_type),
        ),
        (place,),
        (*pieces, *weights, small, mem, pooled, probs, head),
        scratch=(
            pltpu.VMEM((grid_rows, width), f_type),
            pltpu.VMEM((grid_rows, width), b_type),
            pltpu.VMEM((2, grid_rows, grid_rows), b_type),
            pltpu.VMEM((2, grid_rows, grid_rows), b_type),
        ),
        after=after,
    )


def pool_back_kernel(rows, heads, size, half, parts, last, *refs):
    place = refs[0]
    pieces = refs[1 : 1 + half]
    weights = refs[1 + half : 1 + half + parts]
    refs = list(refs[1 + half + parts :])
    small, d_pooled, d_table, d_proj, d_bias = refs[:5]
    del refs[:5]
    base = refs.pop(0) if last else None
    if last:
        mine_ref, other_ref = refs.pop(0), refs.pop(0)
    else:
        norm_ref = refs.pop(0)
    keep_ref, send_ref, field, grads, taps, wide, packed, d_taps, small_grads = refs
    width = heads * size
    seat = seat_of(place, half)
    w_qkv = weight_views(weights, width)[0]
    clear_border(field)
    clear_border(grads)
    load_taps(taps, small, heads, size)
    tokens = to_grid(seat, pieces)
    fill_field(field, dot_nt(tokens, w_qkv[...]))
    fill_field(grads, d_pooled[...])
    convolve(grads, taps, wide, True)
    d_qkv = wide[...].reshape(grid_rows, 3 * width)
    low = d_qkv.astype(b_type)
    count = pieces[0].shape[0]
    for step in range(half):
        part = dot(gather_matrix((seat ^ step) * count, count), low).astype(b_type)
        part = dot(part, w_qkv[...])
        if not last:
            norm_ref[step] = part
        elif step == 0:
            mine_ref[...] = part + base[0]
        else:
            other_ref[step - 1] = (part + base[step]).astype(b_type)
    side = 2 * width
    g_qkv = dot(jnp.transpose(d_qkv).astype(b_type), tokens).astype(b_type)
    packed[0, 0:side, :] = g_qkv[0:side]
    packed[1, 0:width, :] = g_qkv[side : 3 * width]
    packed[1, width:side, :] = d_proj[...]
    tap_grads(field, grads, d_taps)
    small_grads[...] = jnp.zeros(small_grads.shape, f_type)
    for index in range(3 * heads):
        small_grads[32 * index : 32 * index + 27, 0:size] = d_taps[
            0:27, index * size : (index + 1) * size
        ]
    for head in range(heads):
        start = rows.table + 48 * head
        small_grads[start : start + 41, 0:size] = d_table[48 * head : 48 * head + 41, 0:size]
    small_grads[rows.bias : rows.bias + rows.units, :] = d_bias[0 : rows.units, :]
    packed[:, side:, :] = jnp.zeros((2, rows.extra, packed.shape[2]), b_type)
    for line in range(2 * rows.width):
        column = 128 * (line % rows.width)
        packed[line // rows.width, side : side + 32, column : column + 128] = small_grads[
            32 * line : 32 * line + 32, :
        ].astype(b_type)
    core = core_of(place)
    keep_ref[...] = packed[core]
    send_ref[...] = packed[1 - core]


def pool_back(rows, heads, size, place, pieces, weights, small, d_pooled, d_table, d_proj, d_bias,
              base=None, after=()):
    width = heads * size
    half = len(pieces)
    count, model = pieces[0].shape
    last = base is not None
    norm = (
        (((count, model), f_type), ((half - 1, count, model), b_type))
        if last
        else (((half, count, model), f_type),)
    )
    return call(
        functools.partial(pool_back_kernel, rows, heads, size, half, len(weights), last),
        "pool_back",
        9,
        norm
        + (
            ((2 * width + rows.extra, model), b_type),
            ((2 * width + rows.extra, model), b_type),
        ),
        (place,),
        (*pieces, *weights, small, d_pooled, d_table, d_proj, d_bias) + ((base,) if last else ()),
        scratch=(
            pltpu.VMEM((3, 10, 9, 8, 3 * width), f_type),
            pltpu.VMEM((3, 10, 9, 8, 3 * width), f_type),
            pltpu.VMEM((32, 3 * width), f_type),
            pltpu.VMEM((8, 7, 8, 3 * width), f_type),
            pltpu.VMEM((2, 2 * width + rows.extra, model), b_type),
            pltpu.VMEM((32, 3 * width), f_type),
            pltpu.VMEM((rows.used, 128), f_type),
        ),
        after=after,
    )


def frame_of(token):
    return (token * 669) >> 15


def tap_matrix(group):
    frame = frame_of(iota((8, clip_rows), 1))
    return one_hot((frame & ((2 << group) - 1)) == iota((8, clip_rows), 0))


def slot_matrix(which, group):
    token = iota((clip_rows, slot_rows), 0)
    slot = iota((clip_rows, slot_rows), 1)
    frame = frame_of(token)
    line = (slot * 586) >> 15
    return one_hot(
        ((line >> 2) == which)
        & ((line & 3) == (frame >> (group + 1)))
        & (slot - 56 * line == token - 49 * frame)
    )


def compress_kernel(half, place, rows_ref, groups, *refs):
    banks, taps_ref = refs[:4], refs[4]
    outs, products = refs[-3:-1], refs[-1]
    width = taps_ref.shape[1]
    for other in range(2):
        group = groups[clip_of(place, half) ^ other]
        spread = tap_matrix(group)
        factors = []
        for kind in range(2):
            high, low = split(taps_ref[kind])
            factors.append(dot(high, spread) + dot(low, spread))
        total = None
        for which in range(2):
            for kind in range(2):
                bank = banks[2 * other + which][0, kind].astype(f_type)
                high, low = split(bank * factors[kind])
                products[2 * kind * width : (2 * kind + 1) * width, :] = high
                products[(2 * kind + 1) * width : (2 * kind + 2) * width, :] = low
            part = dot(products[...], slot_matrix(which, group))
            total = part if total is None else total + part
        for kind in range(2):
            start = 2 * kind * width
            outs[other][kind] = (
                total[start : start + width] + total[start + width : start + 2 * width]
            ).astype(b_type)


def bank_spec(width, half, other, which):
    def where(step, place, rows_ref, groups):
        return rows_ref[clip_of(place, half) ^ other, which], 0, 0, 0

    return pl.BlockSpec((1, 2, width, clip_rows), where)


def bank_specs(width, half):
    return [bank_spec(width, half, other, which) for other in range(2) for which in range(2)]


def whole_spec(shape):
    return pl.BlockSpec(shape, lambda *_: (0,) * len(shape))


def compress(half, scalars, bank, taps, after=()):
    width = bank.shape[2]
    shape = (2, width, slot_rows)
    return pl.pallas_call(
        functools.partial(compress_kernel, half),
        out_shape=(jax.ShapeDtypeStruct(shape, b_type),) * 2,
        grid_spec=pltpu.PrefetchScalarGridSpec(
            num_scalar_prefetch=3,
            grid=(1,),
            in_specs=bank_specs(width, half)
            + [whole_spec((2, width, 8))]
            + [pl.BlockSpec(memory_space=pl.ANY)] * len(after),
            out_specs=(whole_spec(shape),) * 2,
            scratch_shapes=[pltpu.VMEM((4 * width, clip_rows), b_type)],
        ),
        compiler_params=pltpu.CompilerParams(vmem_limit_bytes=vmem_bytes),
        cost_estimate=pl.CostEstimate(
            flops=5 * 10**10, bytes_accessed=15 * 10**7, transcendentals=0
        ),
        name="compress",
    )(*scalars, *([bank] * 4), taps, *after)


def compress_back_kernel(half, place, rows_ref, groups, *refs):
    banks, grads, out_ref, products = refs[:4], refs[4:6], refs[-2], refs[-1]
    width = grads[0].shape[1]
    total = None
    for other in range(2):
        group = groups[clip_of(place, half) ^ other]
        grad = grads[other][...].reshape(2 * width, slot_rows)
        taps = tap_matrix(group)
        for which in range(2):
            spread = dot_nt(grad, slot_matrix(which, group))
            for kind in range(2):
                bank = banks[2 * other + which][0, kind].astype(f_type)
                high, low = split(bank * spread[kind * width : (kind + 1) * width])
                products[2 * kind * width : (2 * kind + 1) * width, :] = high
                products[(2 * kind + 1) * width : (2 * kind + 2) * width, :] = low
            part = dot_nt(taps, products[...])
            total = part if total is None else total + part
    out_ref[...] = total


def compress_back(half, scalars, bank, grad_here, grad_other, after=()):
    width = bank.shape[2]
    return pl.pallas_call(
        functools.partial(compress_back_kernel, half),
        out_shape=jax.ShapeDtypeStruct((8, 4 * width), f_type),
        grid_spec=pltpu.PrefetchScalarGridSpec(
            num_scalar_prefetch=3,
            grid=(1,),
            in_specs=bank_specs(width, half)
            + [whole_spec((2, width, slot_rows))] * 2
            + [pl.BlockSpec(memory_space=pl.ANY)] * len(after),
            out_specs=whole_spec((8, 4 * width)),
            scratch_shapes=[pltpu.VMEM((4 * width, clip_rows), b_type)],
        ),
        compiler_params=pltpu.CompilerParams(vmem_limit_bytes=vmem_bytes),
        cost_estimate=pl.CostEstimate(
            flops=5 * 10**10, bytes_accessed=15 * 10**7, transcendentals=0
        ),
        name="compress_back",
    )(*scalars, *([bank] * 4), grad_here, grad_other, *after)


def normal_rows(values):
    centered = values - jnp.mean(values, axis=-1, keepdims=True)
    inverse = lax.rsqrt(jnp.mean(centered * centered, axis=-1, keepdims=True) + eps_norm)
    return centered * inverse, inverse


def norm_back(normal, inverse, grad, gain):
    scaled = grad * gain
    return inverse * (
        scaled
        - jnp.mean(scaled, axis=-1, keepdims=True)
        - normal * jnp.mean(scaled * normal, axis=-1, keepdims=True)
    )


def column_sum(values):
    return jnp.sum(values, axis=0, keepdims=True)


def add_pieces(mine, others):
    total = mine[...]
    for other in others:
        total = total + other[0].astype(f_type)
    return total


def open_kernel(rows, heads, size, rows_ref, gain, shift, pool, table, bias, out_ref, small):
    normal, _ = normal_rows(rows_ref[...].astype(f_type))
    out_ref[...] = (normal * vector(gain) + vector(shift)).astype(b_type)
    for head in range(heads):
        for part in range(3):
            start = 32 * (3 * head + part)
            for tap in range(27):
                small[start + tap : start + tap + 1, 0:size] = pool[part, tap, head : head + 1, :]
        start = rows.table + 48 * head
        for slot in range(41):
            small[start + slot : start + slot + 1, 0:size] = table[slot, head : head + 1, :]
    small[rows.bias : rows.bias + rows.units, :] = bias[...]


def second_norm_kernel(half, rows_ref, mine, *refs):
    others = refs[: half - 1]
    bias, gain, shift, mid_ref, out_ref = refs[half - 1 :]
    midway = rows_ref[...].astype(f_type) + (add_pieces(mine, others) + vector(bias))
    mid_ref[...] = midway
    normal, _ = normal_rows(midway)
    out_ref[...] = (normal * vector(gain) + vector(shift)).astype(b_type)


def second_back_kernel(half, mid_ref, mine, *refs):
    others = refs[: half - 1]
    top_ref, gain, d_mid_ref, d_low_ref, sums_ref = refs[half - 1 :]
    normal, inverse = normal_rows(mid_ref[...])
    grad = add_pieces(mine, others)
    top = top_ref[...].astype(f_type)
    d_mid = top + norm_back(normal, inverse, grad, vector(gain))
    d_mid_ref[...] = d_mid
    d_low = d_mid.astype(b_type)
    d_low_ref[...] = d_low
    put_row(sums_ref, 0, column_sum(d_low.astype(f_type)))
    put_row(sums_ref, 8, column_sum(grad * normal))
    put_row(sums_ref, 16, column_sum(grad))
    put_row(sums_ref, 24, column_sum(top))


def first_back_kernel(rows, heads, size, half, rows_ref, d_mid_ref, gain, mine, *refs):
    others = refs[: half - 1]
    refs = refs[half - 1 :]
    mid_ref, down_bias, mlp_mine = refs[:3]
    mlp_others = refs[3 : 2 + half]
    comp, sums, out_ref, y_ref, late = refs[2 + half :]
    normal, inverse = normal_rows(rows_ref[...].astype(f_type))
    grad = add_pieces(mine, others)
    out_ref[...] = d_mid_ref[...] + norm_back(normal, inverse, grad, vector(gain))
    y_ref[...] = (mid_ref[...] + add_pieces(mlp_mine, mlp_others) + vector(down_bias)).astype(b_type)
    late[...] = jnp.zeros(late.shape, f_type)
    late[0:32, :] = sums[...]
    put_row(late, 32, column_sum(grad * normal))
    put_row(late, 40, column_sum(grad))
    width = heads * size
    for head in range(heads):
        for part in range(2):
            start = rows.comp + 8 * (2 * head + part)
            at = 2 * part * width + head * size
            late[start : start + 8, 0:size] = (
                comp[:, at : at + size] + comp[:, at + width : at + width + size]
            )


def close_kernel(rows, heads, size, place, *refs):
    halves, late = refs[:2], refs[2]
    w_qkv, w_proj, pool, table, bias, comp, whole, small = refs[3:]
    width = heads * size
    side = 2 * width
    core = core_of(place)
    for step in range(2):
        whole[core ^ step] = halves[step][...]
    w_qkv[0:side, :] = whole[0, 0:side, :].astype(f_type)
    w_qkv[side:, :] = whole[1, 0:width, :].astype(f_type)
    w_proj[...] = whole[1, width:side, :].astype(f_type)
    for line in range(2 * rows.width):
        column = 128 * (line % rows.width)
        small[32 * line : 32 * line + 32, :] = whole[
            line // rows.width, side : side + 32, column : column + 128
        ].astype(f_type)
    for head in range(heads):
        for part in range(3):
            start = 32 * (3 * head + part)
            for tap in range(27):
                pool[part, tap, head : head + 1, :] = small[start + tap : start + tap + 1, 0:size]
        start = rows.table + 48 * head
        for slot in range(41):
            table[slot, head : head + 1, :] = small[start + slot : start + slot + 1, 0:size]
        for part in range(2):
            start = rows.comp + 8 * (2 * head + part)
            comp[head, part] = late[start : start + 8, 0:size]
    bias[...] = small[rows.bias : rows.bias + rows.units, :]


def error_function(values):
    x = jnp.clip(values, -4.0, 4.0)
    y = x * x
    top = -2.72614225801306e-10
    for term in (
        2.77068142495902e-08,
        -2.10102402082508e-06,
        -5.69250639462346e-05,
        -7.34990630326855e-04,
        -2.95459980854025e-03,
        -1.60960333262415e-02,
    ):
        top = top * y + term
    low = -1.45660718464996e-05
    for term in (
        -2.13374055278905e-04,
        -1.68282697438203e-03,
        -7.37332916720468e-03,
        -1.42647390514189e-02,
    ):
        low = low * y + term
    return x * top / low


def mlp_kernel(rows, half, flip, part, place, *refs):
    pieces, tops = refs[:half], refs[half : 2 * half]
    refs = refs[2 * half :]
    up, down = refs[:2]
    halves = refs[2:4]
    (
        bias, small, y_mine, y_other, d_mine, d_other,
        left_keep, right_keep, left_send, right_send, sums,
        tokens_all, top_all, far, y_all, d_all,
    ) = refs[4:]
    put_halves(far, place, halves)
    ups = halves[0].shape[0]
    count = pieces[0].shape[0]
    tokens = jnp.concatenate([piece[...].astype(f_type) for piece in pieces], axis=0).astype(b_type)
    top = jnp.concatenate([piece[...].astype(f_type) for piece in tops], axis=0).astype(b_type)
    units = down.shape[0]
    y_all[...] = jnp.zeros(y_all.shape, f_type)
    d_all[...] = jnp.zeros(d_all.shape, f_type)
    even = core_of(place) == 0
    for block in range(2):
        first = up if block == 0 else far.at[0:ups]
        second = down if block == 0 else far.at[ups : 2 * ups]
        shift = wide_row(bias, 0, rows.units) if block == 0 else wide_row(small, rows.bias, rows.units)
        for start in range(0, units, part):
            here = slice(start, start + part)
            if flip:
                hidden = dot_nt(tokens, first[here, :]) + shift[:, here]
            else:
                hidden = dot(tokens, first[:, here]) + shift[:, here]
            half_slope = 0.5 * (1.0 + error_function(hidden * (0.5**0.5)))
            slope = half_slope + hidden * jnp.exp(-0.5 * hidden * hidden) * 0.3989422804014327
            act = (hidden * half_slope).astype(b_type)
            d_hid = (dot_nt(top, second[here, :]) * slope).astype(b_type)
            put_row(sums, 8 * block + start // 128, column_sum(d_hid.astype(f_type)))
            y_all[...] += dot(act, second[here, :])
            if flip:
                d_all[...] += dot(d_hid, first[here, :])
            else:
                d_all[...] += dot_nt(d_hid, first[:, here])

            def store(keep, send, here=here, act=act, d_hid=d_hid, block=block):
                keep[0 if flip else 1][block, :, here] = d_hid
                send[0][block, :, here] = act

            @pl.when(even)
            def _():
                store((left_keep, right_keep), (left_send, right_send))

            @pl.when(jnp.logical_not(even))
            def _():
                store((left_send, right_send), (left_keep, right_keep))

        def fixed(keep, send, block=block):
            keep[1 if flip else 0][block] = tokens
            send[1][block] = top

        @pl.when(even)
        def _():
            fixed((left_keep, right_keep), (left_send, right_send))

        @pl.when(jnp.logical_not(even))
        def _():
            fixed((left_send, right_send), (left_keep, right_keep))

    y_mine[...] = y_all[0:count, :]
    d_mine[...] = d_all[0:count, :]
    for step in range(1, half):
        span = slice(step * count, (step + 1) * count)
        y_other[step - 1] = y_all[span, :].astype(b_type)
        d_other[step - 1] = d_all[span, :].astype(b_type)


def mlp(rows, flip, place, pieces, tops, up, down, chunks, bias, small, after=()):
    half = len(pieces)
    count, model = pieces[0].shape
    total = half * count
    units = down.shape[0]
    part = units
    left = ((2, total, units if flip else model), b_type)
    down_left = ((2, total, units), b_type)
    right = ((2, total, model), b_type)
    assert left == down_left
    return call(
        functools.partial(mlp_kernel, rows, half, flip, part),
        "mlp",
        12,
        (
            ((count, model), f_type),
            ((half - 1, count, model), b_type),
            ((count, model), f_type),
            ((half - 1, count, model), b_type),
            left,
            right,
            left,
            right,
            ((16, 128), f_type),
        ),
        (place,),
        (*pieces, *tops, up, down, *chunks, bias, small),
        scratch=(
            pltpu.VMEM((total, model), b_type),
            pltpu.VMEM((total, model), b_type),
            pltpu.VMEM((2 * chunks[0].shape[0], model), b_type),
            pltpu.VMEM((total, model), f_type),
            pltpu.VMEM((total, model), f_type),
        ),
        after=after,
    )


def product_kernel(left, right, out_ref):
    for k in range(2):
        out_ref[k] = lax.dot_general(
            left[k], right[k], (((0,), (0,)), ((), ())), preferred_element_type=f_type
        ).astype(b_type)


def product(left, right, after=()):
    shape = (2, left.shape[2], right.shape[2])
    return call(product_kernel, "product", 4, ((shape, b_type),), (), (left, right), after=after)[0]


def pick_kernel(count, eighth, *refs):
    sources, out_ref, sem = refs[:count], refs[-2], refs[-1]
    rows = out_ref.shape[0]
    start = 0
    for source in sources:
        parts = source.shape[0] // rows

        @pl.when((eighth[0] >= start) & (eighth[0] < start + parts))
        def _(source=source, start=start):
            copy = pltpu.make_async_copy(
                source.at[pl.ds(aligned((eighth[0] - start) * rows, rows), rows), :], out_ref, sem
            )
            copy.start()
            copy.wait()

        start += parts


def pick(eighth, sources, after=()):
    rows = sum(item.shape[0] for item in sources) // 8
    return pl.pallas_call(
        functools.partial(pick_kernel, len(sources)),
        out_shape=jax.ShapeDtypeStruct((rows, sources[0].shape[1]), b_type),
        in_specs=[pl.BlockSpec(memory_space=pltpu.SMEM)]
        + [pl.BlockSpec(memory_space=pl.ANY)] * (len(sources) + len(after)),
        out_specs=pl.BlockSpec(memory_space=pltpu.VMEM),
        scratch_shapes=[pltpu.SemaphoreType.DMA],
        cost_estimate=pl.CostEstimate(flops=10**10, bytes_accessed=10**7, transcendentals=0),
        name="pick",
    )(eighth, *sources, *after)


def add_kernel(*refs):
    total = refs[0][...].astype(f_type)
    for item in refs[1:-1]:
        total = total + item[...].astype(f_type)
    refs[-1][...] = total.astype(b_type)


def add_low(values, after=()):
    return call(add_kernel, "add", 1, ((values[0].shape, b_type),), (), values, after=after)[0]


def seat_in(spot, quad):
    low, high = (bit.bit_length() - 1 for bit in quad)
    return ((spot >> low) & 1) + 2 * ((spot >> high) & 1)


def cut_kernel(quad, count, place, *refs):
    values, outs = refs[:count], refs[count:]
    seat = seat_in(place[1], quad)
    size = outs[0].shape[-2]
    for step, out in enumerate(outs):
        rows = pl.ds(aligned((seat ^ step) * size, size), size)
        total = None
        for item in values:
            part = (item[:, rows, :] if len(item.shape) == 3 else item[rows, :]).astype(f_type)
            total = part if total is None else total + part
        out[...] = total.astype(out.dtype)


def sum_kernel(*refs):
    mine, came, kept, sent = refs[0], refs[1:-2], refs[-2], refs[-1]
    total = mine[...]
    for item in came:
        total = total + item[...].astype(f_type)
    kept[...] = total[0]
    sent[...] = total[1].astype(b_type)


def sum_pair(values, after=()):
    shape = values[0].shape[1:]
    return call(sum_kernel, "sum", 2, ((shape, f_type), (shape, b_type)), (), values, after=after)


def swap_pairs(count, bit):
    return [(place, place ^ bit) for place in range(count)]


class Team:
    def __init__(self, heads_count, clips_count):
        self.total = heads_count
        self.half = heads_count // 2
        self.clips = clips_count
        self.here = lax.axis_index("head")
        self.clip = self.here // self.half
        self.seat = self.here % self.half
        self.spot = lax.axis_index("clip")
        self.place = jnp.stack([self.here, self.spot])

    def partner(self, values):
        return lax.ppermute(values, "head", swap_pairs(self.total, self.half))

    def seats(self, values, step):
        return lax.ppermute(values, "head", swap_pairs(self.total, step))

    def swap(self, values, bit):
        return lax.ppermute(values, "clip", swap_pairs(self.clips, bit))

    def gather(self, rows):
        return [rows] + [self.seats(rows, step) for step in range(1, self.half)]

    def scatter(self, others):
        return [self.seats(others[step - 1 : step], step) for step in range(1, self.half)]

    def eighth(self):
        return (self.spot & 1) * 4 + self.seat_in((2, 4))

    def share(self, came):
        mine = self.collect(came, (2, 4))
        return [mine, self.swap(mine, 1)]

    def quads(self):
        bit, found = 2, []
        while bit < self.clips:
            found.append((bit, 2 * bit))
            bit *= 4
        return found

    def seat_in(self, quad):
        return seat_in(self.spot, quad)

    def peer(self, values, quad, step):
        return self.swap(values, (step & 1) * quad[0] + (step >> 1) * quad[1])

    def cut(self, values, quad, after=()):
        size = values[0].shape[-2] // 4
        if size % 16 == 0:
            shape = (*values[0].shape[:-2], size, values[0].shape[-1])
            return call(
                functools.partial(cut_kernel, quad, len(values)),
                "cut",
                2,
                ((shape, f_type),) + ((shape, b_type),) * 3,
                (self.place,),
                values,
                after=after,
            )
        seat = self.seat_in(quad)

        def quarter(place):
            total = None
            for item in values:
                part = lax.dynamic_slice_in_dim(item, place * size, size, axis=-2).astype(f_type)
                total = part if total is None else total + part
            return total

        return [quarter(seat)] + [quarter(seat ^ step).astype(b_type) for step in (1, 2, 3)]

    def collect(self, chunk, quad):
        seat = self.seat_in(quad)
        pieces = [chunk] + [self.peer(chunk, quad, step) for step in (1, 2, 3)]
        return jnp.concatenate(
            [lax.select_n((seat ^ place).astype(jnp.int32), *pieces) for place in range(4)], axis=0
        )

    def reduce(self, keep, send, after=()):
        values, sent = [keep, self.swap(send, 1)], ()
        for quad in self.quads():
            values = self.cut(values, quad, after)
            sent = sent or tuple(values)
            values = [values[0]] + [self.peer(values[step], quad, step) for step in (1, 2, 3)]
        return values, sent

    def finish(self, chunk):
        for quad in reversed(self.quads()):
            chunk = self.collect(chunk, quad)
        return chunk, self.swap(chunk, 1)


def add(values):
    total = values[0].astype(f_type)
    for item in values[1:]:
        total = total + item.astype(f_type)
    return total


def on_device(
    heads_total,
    clips_total,
    inputs,
    ln1_gain,
    ln1_bias,
    w_qkv,
    pool_kernel,
    rel_table,
    comp_kernel,
    memory_bank,
    mem_index,
    clip_group,
    w_proj,
    proj_bias,
    ln2_gain,
    ln2_bias,
    w_up,
    up_bias,
    w_down,
    down_bias,
    cotangent,
):
    team = Team(heads_total, clips_total)
    half = team.half
    heads, _, size = rel_table.shape
    count, model = inputs.shape
    units = w_up.shape[1]
    width = heads * size
    rows = Rows(heads, units, model)
    flip = units != model
    lined = [
        item.reshape(model // 128, 128)
        for item in (ln1_gain, ln1_bias, proj_bias, ln2_gain, ln2_bias, down_bias)
    ]
    gain1, shift1, bias_proj, gain2, shift2, bias_down = lined
    bias_up = up_bias.reshape(units // 128, 128)
    w_qkv = w_qkv.T
    if flip:
        w_up = w_up.T
    bank = memory_bank.transpose(0, 1, 3, 2)
    place = team.place
    scalars = (place, mem_index, clip_group)

    norm1, small = call(
        functools.partial(open_kernel, rows, heads, size),
        "open",
        2,
        (((count, model), b_type), ((rows.weights, 128), f_type)),
        (),
        (
            inputs,
            gain1,
            shift1,
            pool_kernel.transpose(1, 2, 0, 3),
            rel_table.transpose(1, 0, 2),
            bias_up,
        ),
    )
    tokens1 = team.gather(norm1)
    eighth = team.eighth().reshape(1).astype(jnp.int32)
    chunk_a = pick(eighth, (w_qkv, w_proj), after=(norm1,))
    comp_taps = comp_kernel.transpose(1, 0, 3, 2).reshape(2, width, 8)
    mem_here, mem_there = compress(half, scalars, bank, comp_taps, after=(chunk_a,))
    came_a = team.partner(chunk_a)
    mem_far = team.partner(mem_there)
    small_far = team.partner(small)
    chunks_a = team.share(came_a)

    (pooled_here,) = pool_forward(
        heads, size, place, tokens1, (w_qkv,), small, after=(came_a, mem_here)
    )
    chunk_b = pick(eighth, (w_up, w_down), after=(pooled_here, chunks_a[0]))
    came_b = team.partner(chunk_b)
    chunks_b = team.share(came_b)
    branch, top, probs_here, heads_here = attend(
        rows, heads, size, half, place, clip_group, small, mem_here, pooled_here, w_proj,
        cotangent, after=(chunk_b,),
    )
    tops = team.gather(top)
    pooled_far, weights = pool_forward(
        heads, size, place, tokens1, chunks_a, small_far, after=(branch,)
    )
    branch, branch_other, probs_far, heads_far = attend(
        rows, heads, size, half, place, clip_group, small_far, mem_far, pooled_far, weights,
        branch, after=(*tops, came_b),
    )
    weights_here, weights_far = (w_qkv, w_proj), (weights,)
    branch_came = team.scatter(branch_other)
    midway, norm2 = call(
        functools.partial(second_norm_kernel, half),
        "second_norm",
        2,
        (((count, model), f_type), ((count, model), b_type)),
        (),
        (inputs, branch, *branch_came, bias_proj, gain2, shift2),
        after=(chunks_b[0],),
    )
    tokens2 = team.gather(norm2)
    y, y_other, d_norm2, d_norm2_other, left_k, right_k, left_s, right_s, d_bias = mlp(
        rows, flip, place, tokens2, tops, w_up, w_down, chunks_b, bias_up, small_far
    )
    d_norm2_came = team.scatter(d_norm2_other)
    send_m = product(left_s, right_s)
    d_mid, d_branch, sums2 = call(
        functools.partial(second_back_kernel, half),
        "second_back",
        3,
        (((count, model), f_type), ((count, model), b_type), ((32, 128), f_type)),
        (),
        (midway, d_norm2, *d_norm2_came, cotangent, gain2),
        after=(send_m,),
    )
    d_branches = team.gather(d_branch)
    keep_m = product(left_k, right_k, after=(d_branch,))
    sums_m, sent_m = team.reduce(keep_m, send_m)
    y_came = team.scatter(y_other)

    d_pooled, d_mem_far, d_table, d_proj = scores_back(
        rows, heads, size, place, d_branches, weights_far, small_far, mem_far, pooled_far,
        probs_far, heads_far, after=sent_m,
    )
    d_mem_back = team.partner(d_mem_far)
    d_norm1, keep_f, send_f = pool_back(
        rows, heads, size, place, tokens1, weights_far, small_far, d_pooled, d_table, d_proj,
        d_bias[8:16], after=(*y_came,),
    )
    sum_m, part_m = sum_pair(sums_m, after=(d_norm1,))
    came_m = team.partner(part_m)
    sums_f, sent_f = team.reduce(keep_f, send_f, after=(part_m,))
    d_pooled, d_mem_here, d_table, d_proj = scores_back(
        rows, heads, size, place, d_branches, weights_here, small, mem_here, pooled_here,
        probs_here, heads_here, after=(d_norm1, part_m, *sent_f),
    )
    part_f = add_low(sums_f, after=(d_pooled,))
    chunk_m = add_low([sum_m, came_m], after=(d_pooled, part_f))
    d_norm1, d_norm1_other, keep_o, send_o = pool_back(
        rows, heads, size, place, tokens1, weights_here, small, d_pooled, d_table, d_proj,
        d_bias[0:8], base=d_norm1, after=(chunk_m, part_f, d_mem_back),
    )
    came_f = team.partner(part_f)
    d_norm1_came = team.scatter(d_norm1_other)
    halves_m = team.finish(chunk_m)
    g_comp = compress_back(half, scalars, bank, d_mem_here, d_mem_back, after=(keep_o,))
    sums_o, sent_o = team.reduce(keep_o, send_o, after=(g_comp,))
    chunk_o = add([*sums_o, came_f]).astype(b_type)
    halves_o = team.finish(chunk_o)
    grad_inputs, output, late = call(
        functools.partial(first_back_kernel, rows, heads, size, half),
        "first_back",
        3,
        (((count, model), f_type), ((count, model), b_type), ((rows.late, 128), f_type)),
        (),
        (
            inputs, d_mid, gain1, d_norm1, *d_norm1_came, midway, bias_down, y, *y_came,
            g_comp, sums2,
        ),
        after=sent_o,
    )
    late = late + team.swap(late, 1)
    for quad in team.quads():
        late = add([late] + [team.peer(late, quad, step) for step in (1, 2, 3)])
    sums = late[:48]
    sums = add([sums] + [team.seats(sums, step) for step in range(1, team.total)])
    odd = core_of((0, team.spot)) != 0
    g_up = jnp.where(odd, halves_m[1], halves_m[0]).astype(f_type)
    g_down = jnp.where(odd, halves_m[0], halves_m[1]).astype(f_type)
    g_qkv, g_proj, g_pool, g_rel, g_bias, g_comp = call(
        functools.partial(close_kernel, rows, heads, size),
        "close",
        3,
        (
            ((3 * width, model), f_type),
            ((width, model), f_type),
            ((3, 27, heads, size), f_type),
            ((41, heads, size), f_type),
            ((units // 128, 128), f_type),
            ((heads, 2, 8, size), f_type),
        ),
        (place,),
        (*halves_o, late),
        scratch=(
            pltpu.VMEM((2, 2 * width + rows.extra, model), b_type),
            pltpu.VMEM((rows.used, 128), f_type),
        ),
    )
    if flip:
        g_up = g_up.T

    def total(index):
        return sums[8 * index : 8 * index + model // 128].reshape(model)

    return (
        output,
        grad_inputs,
        total(4),
        total(5),
        g_qkv.T,
        g_pool.transpose(2, 0, 1, 3),
        g_rel.transpose(1, 0, 2),
        g_comp,
        g_proj,
        total(0),
        total(1),
        total(2),
        g_up,
        g_bias.reshape(units),
        g_down,
        total(3),
    )


def solution(mesh):
    return jax.shard_map(
        functools.partial(on_device, mesh.shape["head"], mesh.shape["clip"]),
        mesh=mesh,
        in_specs=(
            P(("clip", "head"), None),
            P(),
            P(),
            P(None, "head"),
            P("head", None, None, None),
            P("head", None, None),
            P("head", None, None, None),
            P("clip", None, None, "head"),
            P("clip", None),
            P("clip"),
            P("head", None),
            P(),
            P(),
            P(),
            P(None, "head"),
            P("head"),
            P("head", None),
            P(),
            P(("clip", "head"), None),
        ),
        out_specs=(
            P(("clip", "head"), None),
            P(("clip", "head"), None),
            P(),
            P(),
            P(None, "head"),
            P("head", None, None, None),
            P("head", None, None),
            P("head", None, None, None),
            P("head", None),
            P(),
            P(),
            P(),
            P(None, "head"),
            P("head"),
            P("head", None),
            P(),
        ),
        check_vma=False,
    )
```

```python
import functools

import jax
import jax.numpy as jnp
from jax import lax
from jax.experimental import pallas as pl
from jax.experimental.pallas import tpu as pltpu
from jax.sharding import PartitionSpec as P

f_type = jnp.float32
b_type = jnp.bfloat16
eps_norm = 1e-06
neg_large = -1000000000.0
clip_rows = 392
grid_rows = 448
slot_rows = 448
vmem_bytes = 56 * 1024 * 1024


def dot(a, b):
    return jnp.dot(a, b, preferred_element_type=f_type)


def dot_nt(a, b):
    return lax.dot_general(a, b, (((1,), (1,)), ((), ())), preferred_element_type=f_type)


def dot_tn(a, b):
    return lax.dot_general(a, b, (((0,), (0,)), ((), ())), preferred_element_type=f_type)


def iota(shape, axis):
    return lax.broadcasted_iota(jnp.int32, shape, axis)


def one_hot(flag):
    return jnp.where(flag, 1.0, 0.0).astype(b_type)


def split(values):
    high = values.astype(b_type)
    return high, (values - high.astype(f_type)).astype(b_type)


def aligned(start, step):
    return pl.multiple_of(start, step)


def call(kernel, name, cost, results, scalars, arrays, scratch=(), after=()):
    def body(*refs):
        kept = refs[: len(scalars) + len(arrays)]
        kernel(*kept, *refs[len(kept) + len(after) :])

    return pl.pallas_call(
        body,
        out_shape=tuple(jax.ShapeDtypeStruct(shape, kind) for shape, kind in results),
        in_specs=[pl.BlockSpec(memory_space=pltpu.SMEM)] * len(scalars)
        + [pl.BlockSpec(memory_space=pltpu.VMEM)] * len(arrays)
        + [pl.BlockSpec(memory_space=pl.ANY)] * len(after),
        out_specs=tuple(pl.BlockSpec(memory_space=pltpu.VMEM) for _ in results),
        scratch_shapes=list(scratch),
        compiler_params=pltpu.CompilerParams(vmem_limit_bytes=vmem_bytes),
        cost_estimate=pl.CostEstimate(
            flops=int(cost * 1e10), bytes_accessed=int(cost * 3e7), transcendentals=0
        ),
        name=name,
    )(*scalars, *arrays, *after)


def spread_matrix(start, count):
    row = iota((grid_rows, count), 0)
    place = row & 7
    return one_hot(
        ((row >> 3) * 7 + place - start == iota((grid_rows, count), 1)) & (place < 7)
    )


def gather_matrix(start, count):
    row = iota((count, grid_rows), 1)
    place = row & 7
    return one_hot(
        ((row >> 3) * 7 + place - start == iota((count, grid_rows), 0)) & (place < 7)
    )


def to_grid(seat, pieces):
    total = None
    for step, piece in enumerate(pieces):
        rows = piece.shape[0]
        part = dot(spread_matrix((seat ^ step) * rows, rows), piece[...])
        total = part if total is None else total + part
    return total.astype(b_type)


def row_coords(shape, axis):
    row = iota(shape, axis)
    line = row >> 3
    frame = (line * 37) >> 8
    return frame, line - frame * 7, row & 7


def coord_of(kind, coords):
    frame, line, place = coords
    return jnp.where(kind == 0, frame, jnp.where(kind == 1, line, place))


def query_mask():
    shape = (grid_rows, 192)
    column = iota(shape, 1)
    coord = coord_of(column >> 6, row_coords(shape, 0))
    return jnp.where(((column >> 3) & 7) == coord, 1.0, 0.0)


def key_matrix():
    shape = (192, grid_rows)
    column = iota(shape, 0)
    coord = coord_of(column >> 6, row_coords(shape, 1))
    return one_hot((column & 7) == coord)


def key_places():
    shape = (grid_rows, 192)
    column = iota(shape, 1)
    coord = coord_of(column >> 6, row_coords(shape, 0))
    return one_hot((column & 7) == coord)


def table_slot(column):
    kind = column >> 6
    at_query = (column >> 3) & 7
    at_key = column & 7
    base = jnp.where(kind == 0, 7, jnp.where(kind == 1, 21, 34))
    valid = (kind == 0) | ((at_query < 7) & (at_key < 7))
    return jnp.where(valid, base + at_query - at_key, -1)


def table_matrix():
    return one_hot(table_slot(iota((192, 41), 0)) == iota((192, 41), 1))


def own_bias(shape, axis):
    return jnp.where((iota(shape, axis) & 7) == 7, neg_large, 0.0)


def mem_bias(shape, axis, limit):
    slot = iota(shape, axis)
    line = (slot * 586) >> 15
    return jnp.where((slot - 56 * line < 49) & ((line & 3) < limit), 0.0, neg_large)


def clear_border(field):
    width = field.shape[-1]
    field[:, 0:1] = jnp.zeros((3, 1, 9, 8, width), f_type)
    field[:, 9:10] = jnp.zeros((3, 1, 9, 8, width), f_type)
    field[:, :, 0:1] = jnp.zeros((3, 10, 1, 8, width), f_type)
    field[:, :, 8:9] = jnp.zeros((3, 10, 1, 8, width), f_type)


def fill_field(field, values):
    width = values.shape[-1]
    lines = values.reshape(56, 8, width)
    field[0, 1:9, 1:8] = pltpu.roll(lines, 1, 1).reshape(8, 7, 8, width)
    field[1, 1:9, 1:8] = lines.reshape(8, 7, 8, width)
    field[2, 1:9, 1:8] = pltpu.roll(lines, 7, 1).reshape(8, 7, 8, width)


def convolve(field, taps, result, flip):
    width = field.shape[-1]
    for start in range(0, width, 128):
        lanes = slice(start, min(start + 128, width))

        def frame(t, carry):
            total = jnp.zeros((7, 8, lanes.stop - lanes.start), f_type)
            for dt in range(3):
                for dw in range(3):
                    near = field[dw, t + dt, :, :, lanes]
                    for dh in range(3):
                        tap = dt * 9 + dh * 3 + dw
                        tap = 26 - tap if flip else tap
                        total = total + near[dh : dh + 7] * taps[tap : tap + 1, lanes]
            result[t, :, :, lanes] = total
            return carry

        lax.fori_loop(0, 8, frame, 0, unroll=8)


def tap_grads(field, grads, result):
    width = field.shape[-1]
    for start in range(0, width, 128):
        lanes = slice(start, min(start + 128, width))
        size = lanes.stop - lanes.start

        def frame(t, sums):
            grad = grads[1, t + 1, 1:8, :, lanes]
            sums = list(sums)
            for dt in range(3):
                for dw in range(3):
                    near = field[dw, t + dt, :, :, lanes]
                    for dh in range(3):
                        tap = dt * 9 + dh * 3 + dw
                        sums[tap] = sums[tap] + jnp.sum(near[dh : dh + 7] * grad, axis=0)
            return tuple(sums)

        sums = lax.fori_loop(
            0, 8, frame, tuple(jnp.zeros((8, size), f_type) for _ in range(27)), unroll=8
        )
        for tap in range(27):
            result[tap : tap + 1, lanes] = jnp.sum(sums[tap], axis=0, keepdims=True)


class Rows:
    def __init__(self, heads, units, width):
        self.taps = 0
        self.table = self.taps + 96 * heads
        self.bias = self.table + 48 * heads
        self.weights = self.bias + 8
        self.comp = 48
        self.late = self.comp + 16 * heads
        self.units = units // 128
        self.width = width // 128
        self.extra = 64
        self.used = 32 * self.width * 2
        assert self.weights <= self.used


def wide_row(ref, start, count):
    return jnp.concatenate([ref[start + k : start + k + 1, :] for k in range(count)], axis=1)


def put_row(ref, start, values):
    for k in range(values.shape[1] // 128):
        ref[start + k : start + k + 1, :] = values[:, 128 * k : 128 * k + 128]


def vector(ref):
    return wide_row(ref, 0, ref.shape[0])


def seat_of(place, half):
    return place[0] & (half - 1)


def clip_of(place, half):
    return place[0] >> (half.bit_length() - 1)


def core_of(place):
    return place[1] & 1


def put_halves(whole, place, halves):
    size = halves[0].shape[0]
    for step, item in enumerate(halves):
        whole[pl.ds(aligned((core_of(place) ^ step) * size, size), size), :] = item[...]


def weight_views(refs, width):
    if len(refs) == 2:
        return refs[0], refs[1]
    return refs[0].at[0 : 3 * width], refs[0].at[3 * width : 4 * width]


def pack_small(rows, heads, size, pool, table, bias, small):
    for head in range(heads):
        for part in range(3):
            start = 32 * (3 * head + part)
            for tap in range(27):
                small[start + tap : start + tap + 1, 0:size] = pool[part, tap, head : head + 1, :]
        start = rows.table + 48 * head
        for slot in range(41):
            small[start + slot : start + slot + 1, 0:size] = table[slot, head : head + 1, :]
    small[rows.bias : rows.bias + rows.units, :] = bias[...]


def load_taps(taps, small, heads, size):
    for index in range(3 * heads):
        taps[0:27, index * size : (index + 1) * size] = small[
            32 * index : 32 * index + 27, 0:size
        ]


def pool_forward_kernel(rows, heads, size, half, far, passing, place, *refs):
    refs = list(refs)
    pieces = refs[:half]
    del refs[:half]
    if far:
        halves = refs[:2]
        small, pooled_ref, weights, field, taps, wide = refs[2:]
        put_halves(weights, place, halves)
    else:
        gain, shift, weights, *raw = refs[:6]
        del refs[:6]
        passed = refs[:passing]
        pooled_ref, small, *passed_on = refs[passing : 2 + 2 * passing]
        rows_refs, pieces = pieces, refs[2 + 2 * passing : -3]
        pack_small(rows, heads, size, *raw, small)
        field, taps, wide = refs[-3:]
        for source, out in zip(passed, passed_on):
            out[...] = source[...]
        for source, norm in zip(rows_refs, pieces):
            normal, _ = normal_rows(source[...].astype(f_type))
            norm[...] = (normal * vector(gain) + vector(shift)).astype(b_type)
    width = heads * size
    clear_border(field)
    load_taps(taps, small, heads, size)
    fill_field(
        field, dot_nt(to_grid(seat_of(place, half), pieces), weights[0 : 3 * width, :])
    )
    convolve(field, taps, wide, False)
    filled = (iota((grid_rows, 1), 0) & 7) < 7
    pooled_ref[...] = jnp.where(
        filled, wide[...].reshape(grid_rows, 3 * width), 0.0
    ).astype(b_type)


def pool_forward(rows, heads, size, place, pieces, weights, small, norm=(), passed=(), after=()):
    width = heads * size
    half = len(pieces)
    model = pieces[0].shape[1]
    far = not norm
    return call(
        functools.partial(pool_forward_kernel, rows, heads, size, half, far, len(passed)),
        "pool_forward",
        6,
        (((grid_rows, 3 * width), b_type),)
        + (
            (((4 * width, model), b_type),)
            if far
            else (((rows.weights, 128), f_type),)
            + tuple((piece.shape, b_type) for piece in (*passed, *pieces))
        ),
        (place,),
        (*pieces, *norm, *weights, *small, *passed),
        scratch=(
            pltpu.VMEM((3, 10, 9, 8, 3 * width), f_type),
            pltpu.VMEM((32, 3 * width), f_type),
            pltpu.VMEM((8, 7, 8, 3 * width), f_type),
        ),
        after=after,
    )


def attend_kernel(rows, heads, size, half, far, place, groups, *refs):
    refs = list(refs)
    small, mem, pooled, weights = refs[:4]
    del refs[:4]
    base = refs.pop(0) if far else None
    if far:
        mine_ref, other_ref = refs.pop(0), refs.pop(0)
    else:
        branch_ref = refs.pop(0)
    probs_ref, head_ref, query_wide, key_wide, mem_wide, head_wide = refs
    width = heads * size
    scale = size ** (-0.5)
    seat = seat_of(place, half)
    w_proj = weight_views((weights,), width)[1] if far else weights
    rest = 128 - size
    ones = (iota((grid_rows, rest), 1) == 0).astype(f_type)
    query_wide[:, size:128] = ones.astype(b_type)
    key_wide[:, size:128] = (ones * own_bias((grid_rows, rest), 0)).astype(b_type)
    first = (iota((rest, grid_rows), 0) == 0).astype(f_type)
    limit = 4 >> groups[clip_of(place, half)]
    mem_wide[size:128, :] = (first * mem_bias((rest, grid_rows), 1, limit)).astype(b_type)
    keys_at = key_places()
    key_wide[:, 128:320] = keys_at
    key_wide[:, 320:512] = keys_at
    expand = table_matrix()
    mask = query_mask() * (1.0 / scale)
    for head in range(heads):
        at = 3 * head * size
        lanes = slice(head * size, (head + 1) * size)
        queries = pooled[:, at : at + size]
        values = pooled[:, at + 2 * size : at + 3 * size]
        start = rows.table + 48 * head
        table_high, table_low = split(small[start : start + 41, 0:size])
        rel = dot_nt(queries, dot(expand, table_high).astype(b_type)) + dot_nt(
            queries, dot(expand, table_low).astype(b_type)
        )
        high, low = split(rel * mask)
        query_wide[:, 0:size] = queries
        query_wide[:, 128:320] = high
        query_wide[:, 320:512] = low
        key_wide[:, 0:size] = pooled[:, at + size : at + 2 * size]
        mem_wide[0:size, :] = mem[0, lanes, :]
        own = dot_nt(query_wide[...], key_wide[...])
        far_scores = dot(query_wide[:, 0:128], mem_wide[...])
        top = jnp.maximum(
            jnp.max(own, axis=-1, keepdims=True), jnp.max(far_scores, axis=-1, keepdims=True)
        )
        own = jnp.exp((own - top) * scale)
        far_scores = jnp.exp((far_scores - top) * scale)
        total = jnp.sum(own, axis=-1, keepdims=True) + jnp.sum(far_scores, axis=-1, keepdims=True)
        inverse = 1.0 / total
        own = own * inverse
        far_scores = far_scores * inverse
        probs_ref[head, 0] = own
        probs_ref[head, 1] = far_scores
        attended = dot(own.astype(b_type), values) + dot_nt(
            far_scores.astype(b_type), mem[1, lanes, :]
        )
        head_wide[:, lanes] = attended + queries.astype(f_type)
    head_ref[...] = head_wide[...].astype(b_type)
    count = base.shape[1] if far else branch_ref.shape[1]
    for step in range(half):
        head_out = dot(gather_matrix((seat ^ step) * count, count), head_ref[...]).astype(b_type)
        part = dot(head_out, w_proj[...])
        if not far:
            branch_ref[step] = part
        elif step == 0:
            mine_ref[...] = part + base[0]
        else:
            other_ref[step - 1] = (part + base[step]).astype(b_type)


def attend(rows, heads, size, half, place, groups, small, mem, pooled, weights, base=None, after=()):
    width = heads * size
    model = weights.shape[1]
    count = clip_rows // half
    far = base is not None
    branch = (
        (((count, model), f_type), ((half - 1, count, model), b_type))
        if far
        else (((half, count, model), f_type),)
    )
    return call(
        functools.partial(attend_kernel, rows, heads, size, half, far),
        "attend",
        10,
        branch
        + (((heads, 2, grid_rows, grid_rows), f_type), ((grid_rows, width), b_type)),
        (place, groups),
        (small, mem, pooled, weights) + ((base,) if far else ()),
        scratch=(
            pltpu.VMEM((grid_rows, 512), b_type),
            pltpu.VMEM((grid_rows, 512), b_type),
            pltpu.VMEM((128, grid_rows), b_type),
            pltpu.VMEM((grid_rows, width), f_type),
        ),
        after=after,
    )


def scores_back_kernel(rows, heads, size, half, parts, *refs):
    place = refs[0]
    pieces = refs[1 : 1 + half]
    weights = refs[1 + half : 1 + half + parts]
    (
        small, mem, pooled_ref, probs_ref, head_ref,
        d_pooled, d_mem_ref, d_table_ref, d_proj_ref,
        d_head_ref, d_low_ref, probs_low, d_scores,
    ) = refs[1 + half + parts :]
    width = heads * size
    scale = size ** (-0.5)
    w_proj = weight_views(weights, width)[1]
    d_branch = to_grid(seat_of(place, half), pieces)
    d_head = dot_nt(d_branch, w_proj[...])
    d_head_ref[...] = d_head
    d_low_ref[...] = d_head.astype(b_type)
    expand = table_matrix()
    keys_at = key_matrix()
    mask = query_mask()
    for head in range(heads):
        at = 3 * head * size
        lanes = slice(head * size, (head + 1) * size)
        queries = pooled_ref[:, at : at + size]
        keys = pooled_ref[:, at + size : at + 2 * size]
        values = pooled_ref[:, at + 2 * size : at + 3 * size]
        mem_keys = mem[0, lanes, :]
        mem_values = mem[1, lanes, :]

        d_att = d_low_ref[:, lanes]
        own = probs_ref[head, 0]
        far_probs = probs_ref[head, 1]
        d_own = dot_nt(d_att, values)
        d_far = dot(d_att, mem_values)
        inner = jnp.sum(own * d_own, axis=-1, keepdims=True) + jnp.sum(
            far_probs * d_far, axis=-1, keepdims=True
        )
        d_scores[0] = (own * (d_own - inner)).astype(b_type)
        d_scores[1] = (far_probs * (d_far - inner)).astype(b_type)
        probs_low[0] = own.astype(b_type)
        probs_low[1] = far_probs.astype(b_type)
        d_query = (dot(d_scores[0], keys) + dot_nt(d_scores[1], mem_keys)) * scale
        start = rows.table + 48 * head
        table_high, table_low = split(small[start : start + 41, 0:size])
        rel_high, rel_low = split(dot_nt(d_scores[0], keys_at) * mask)
        wide_high = dot(expand, table_high).astype(b_type)
        wide_low = dot(expand, table_low).astype(b_type)
        d_rel = dot(rel_high, wide_high) + dot(rel_low, wide_high) + dot(rel_high, wide_low)
        d_pooled[:, at : at + size] = d_query + d_head_ref[:, lanes] + d_rel
        queries_t = jnp.transpose(queries.astype(f_type)).astype(b_type)
        d_att_t = jnp.transpose(d_head_ref[:, lanes]).astype(b_type)
        wide_high, wide_low = split(dot(queries_t, rel_high) + dot(queries_t, rel_low))
        d_table = dot(wide_high, expand) + dot(wide_low, expand)
        d_table_ref[48 * head : 48 * head + 41, 0:size] = jnp.transpose(d_table)
        d_pooled[:, at + size : at + 2 * size] = jnp.transpose(dot(queries_t, d_scores[0])) * scale
        d_mem_ref[0, lanes, :] = (dot(queries_t, d_scores[1]) * scale).astype(b_type)
        d_pooled[:, at + 2 * size : at + 3 * size] = jnp.transpose(dot(d_att_t, probs_low[0]))
        d_mem_ref[1, lanes, :] = dot(d_att_t, probs_low[1]).astype(b_type)
    head_t = jnp.transpose(head_ref[...].astype(f_type)).astype(b_type)
    d_proj_ref[...] = dot(head_t, d_branch).astype(b_type)


def scores_back(rows, heads, size, place, pieces, weights, small, mem, pooled, probs, head, after=()):
    width = heads * size
    return call(
        functools.partial(scores_back_kernel, rows, heads, size, len(pieces), len(weights)),
        "scores_back",
        13,
        (
            ((grid_rows, 3 * width), f_type),
            ((2, width, slot_rows), b_type),
            ((48 * heads, 128), f_type),
            ((width, pieces[0].shape[1]), b_type),
        ),
        (place,),
        (*pieces, *weights, small, mem, pooled, probs, head),
        scratch=(
            pltpu.VMEM((grid_rows, width), f_type),
            pltpu.VMEM((grid_rows, width), b_type),
            pltpu.VMEM((2, grid_rows, grid_rows), b_type),
            pltpu.VMEM((2, grid_rows, grid_rows), b_type),
        ),
        after=after,
    )


def pool_back_kernel(rows, heads, size, half, parts, last, *refs):
    place = refs[0]
    pieces = refs[1 : 1 + half]
    weights = refs[1 + half : 1 + half + parts]
    refs = list(refs[1 + half + parts :])
    small, d_pooled, d_table, d_proj, d_bias = refs[:5]
    del refs[:5]
    if last:
        base, sums_early = refs[:2]
        inputs = refs[2 : 2 + half]
        mine_ref, other_ref, sums_ref = refs[2 + half : 5 + half]
        del refs[: 5 + half]
    else:
        norm_ref = refs.pop(0)
    keep_ref, send_ref, field, grads, taps, wide, packed, d_taps, small_grads = refs
    width = heads * size
    seat = seat_of(place, half)
    w_qkv = weight_views(weights, width)[0]
    clear_border(field)
    clear_border(grads)
    load_taps(taps, small, heads, size)
    tokens = to_grid(seat, pieces)
    fill_field(field, dot_nt(tokens, w_qkv[...]))
    fill_field(grads, d_pooled[...])
    convolve(grads, taps, wide, True)
    d_qkv = wide[...].reshape(grid_rows, 3 * width)
    low = d_qkv.astype(b_type)
    count = pieces[0].shape[0]
    gains, shifts = [], []
    for step in range(half):
        part = dot(gather_matrix((seat ^ step) * count, count), low).astype(b_type)
        part = dot(part, w_qkv[...])
        if not last:
            norm_ref[step] = part
            continue
        part = part + base[step]
        if step == 0:
            mine_ref[...] = part
        else:
            other_ref[step - 1] = part.astype(b_type)
        normal, _ = normal_rows(inputs[step][...].astype(f_type))
        gains.append(column_sum(part * normal))
        shifts.append(column_sum(part))
    if last:
        sums_ref[0:32, :] = sums_early[...]
        put_row(sums_ref, 32, sum(gains[1:], gains[0]))
        put_row(sums_ref, 40, sum(shifts[1:], shifts[0]))
    side = 2 * width
    g_qkv = dot(jnp.transpose(d_qkv).astype(b_type), tokens).astype(b_type)
    packed[0, 0:side, :] = g_qkv[0:side]
    packed[1, 0:width, :] = g_qkv[side : 3 * width]
    packed[1, width:side, :] = d_proj[...]
    tap_grads(field, grads, d_taps)
    small_grads[...] = jnp.zeros(small_grads.shape, f_type)
    for index in range(3 * heads):
        small_grads[32 * index : 32 * index + 27, 0:size] = d_taps[
            0:27, index * size : (index + 1) * size
        ]
    for head in range(heads):
        start = rows.table + 48 * head
        small_grads[start : start + 41, 0:size] = d_table[48 * head : 48 * head + 41, 0:size]
    small_grads[rows.bias : rows.bias + rows.units, :] = d_bias[0 : rows.units, :]
    packed[:, side:, :] = jnp.zeros((2, rows.extra, packed.shape[2]), b_type)
    for line in range(2 * rows.width):
        column = 128 * (line % rows.width)
        packed[line // rows.width, side : side + 32, column : column + 128] = small_grads[
            32 * line : 32 * line + 32, :
        ].astype(b_type)
    core = core_of(place)
    keep_ref[...] = packed[core]
    send_ref[...] = packed[1 - core]


def pool_back(rows, heads, size, place, pieces, weights, small, d_pooled, d_table, d_proj, d_bias,
              late=(), after=()):
    width = heads * size
    half = len(pieces)
    count, model = pieces[0].shape
    last = bool(late)
    norm = (
        (((count, model), f_type), ((half - 1, count, model), b_type), ((48, 128), f_type))
        if last
        else (((half, count, model), f_type),)
    )
    return call(
        functools.partial(pool_back_kernel, rows, heads, size, half, len(weights), last),
        "pool_back",
        9,
        norm
        + (
            ((2 * width + rows.extra, model), b_type),
            ((2 * width + rows.extra, model), b_type),
        ),
        (place,),
        (*pieces, *weights, small, d_pooled, d_table, d_proj, d_bias, *late),
        scratch=(
            pltpu.VMEM((3, 10, 9, 8, 3 * width), f_type),
            pltpu.VMEM((3, 10, 9, 8, 3 * width), f_type),
            pltpu.VMEM((32, 3 * width), f_type),
            pltpu.VMEM((8, 7, 8, 3 * width), f_type),
            pltpu.VMEM((2, 2 * width + rows.extra, model), b_type),
            pltpu.VMEM((32, 3 * width), f_type),
            pltpu.VMEM((rows.used, 128), f_type),
        ),
        after=after,
    )


def frame_of(token):
    return (token * 669) >> 15


def tap_matrix(group):
    frame = frame_of(iota((8, clip_rows), 1))
    return one_hot((frame & ((2 << group) - 1)) == iota((8, clip_rows), 0))


def slot_matrix(which, group):
    token = iota((clip_rows, slot_rows), 0)
    slot = iota((clip_rows, slot_rows), 1)
    frame = frame_of(token)
    line = (slot * 586) >> 15
    return one_hot(
        ((line >> 2) == which)
        & ((line & 3) == (frame >> (group + 1)))
        & (slot - 56 * line == token - 49 * frame)
    )


def compress_kernel(half, place, rows_ref, groups, *refs):
    banks, taps_ref = refs[:4], refs[4]
    outs, products, factors = refs[-4:-2], refs[-2], refs[-1]
    heads, _, _, size = taps_ref.shape
    width = heads * size
    for other in range(2):
        group = groups[clip_of(place, half) ^ other]
        spread = tap_matrix(group)
        for kind in range(2):
            for head in range(heads):
                high, low = split(taps_ref[head, kind])
                factors[kind, head * size : (head + 1) * size, :] = dot_tn(high, spread) + dot_tn(
                    low, spread
                )
        total = None
        for which in range(2):
            for kind in range(2):
                bank = banks[2 * other + which][0, kind].astype(f_type)
                high, low = split(bank * factors[kind])
                products[2 * kind * width : (2 * kind + 1) * width, :] = high
                products[(2 * kind + 1) * width : (2 * kind + 2) * width, :] = low
            part = dot(products[...], slot_matrix(which, group))
            total = part if total is None else total + part
        for kind in range(2):
            start = 2 * kind * width
            outs[other][kind] = (
                total[start : start + width] + total[start + width : start + 2 * width]
            ).astype(b_type)


def bank_spec(width, half, other, which):
    def where(step, place, rows_ref, groups):
        return rows_ref[clip_of(place, half) ^ other, which], 0, 0, 0

    return pl.BlockSpec((1, 2, width, clip_rows), where)


def bank_specs(width, half):
    return [bank_spec(width, half, other, which) for other in range(2) for which in range(2)]


def whole_spec(shape):
    return pl.BlockSpec(shape, lambda *_: (0,) * len(shape))


def compress(half, scalars, bank, taps, after=()):
    width = bank.shape[2]
    shape = (2, width, slot_rows)
    return pl.pallas_call(
        functools.partial(compress_kernel, half),
        out_shape=(jax.ShapeDtypeStruct(shape, b_type),) * 2,
        grid_spec=pltpu.PrefetchScalarGridSpec(
            num_scalar_prefetch=3,
            grid=(1,),
            in_specs=bank_specs(width, half)
            + [whole_spec(taps.shape)]
            + [pl.BlockSpec(memory_space=pl.ANY)] * len(after),
            out_specs=(whole_spec(shape),) * 2,
            scratch_shapes=[
                pltpu.VMEM((4 * width, clip_rows), b_type),
                pltpu.VMEM((2, width, clip_rows), f_type),
            ],
        ),
        compiler_params=pltpu.CompilerParams(vmem_limit_bytes=vmem_bytes),
        cost_estimate=pl.CostEstimate(
            flops=5 * 10**10, bytes_accessed=15 * 10**7, transcendentals=0
        ),
        name="compress",
    )(*scalars, *([bank] * 4), taps, *after)


def compress_back_kernel(rows, heads, size, half, place, rows_ref, groups, *refs):
    banks, grads, out_ref, products = refs[:4], refs[4:6], refs[-2], refs[-1]
    width = grads[0].shape[1]
    total = None
    for other in range(2):
        group = groups[clip_of(place, half) ^ other]
        grad = grads[other][...].reshape(2 * width, slot_rows)
        taps = tap_matrix(group)
        for which in range(2):
            spread = dot_nt(grad, slot_matrix(which, group))
            for kind in range(2):
                bank = banks[2 * other + which][0, kind].astype(f_type)
                high, low = split(bank * spread[kind * width : (kind + 1) * width])
                products[2 * kind * width : (2 * kind + 1) * width, :] = high
                products[(2 * kind + 1) * width : (2 * kind + 2) * width, :] = low
            part = dot_nt(taps, products[...])
            total = part if total is None else total + part
    out_ref[...] = jnp.zeros(out_ref.shape, f_type)
    for head in range(heads):
        for part in range(2):
            start = 8 * (2 * head + part)
            at = 2 * part * width + head * size
            out_ref[start : start + 8, 0:size] = (
                total[:, at : at + size] + total[:, at + width : at + width + size]
            )


def compress_back(rows, heads, size, half, scalars, bank, grad_here, grad_other, after=()):
    width = bank.shape[2]
    return pl.pallas_call(
        functools.partial(compress_back_kernel, rows, heads, size, half),
        out_shape=jax.ShapeDtypeStruct((16 * heads, 128), f_type),
        grid_spec=pltpu.PrefetchScalarGridSpec(
            num_scalar_prefetch=3,
            grid=(1,),
            in_specs=bank_specs(width, half)
            + [whole_spec((2, width, slot_rows))] * 2
            + [pl.BlockSpec(memory_space=pl.ANY)] * len(after),
            out_specs=whole_spec((16 * heads, 128)),
            scratch_shapes=[pltpu.VMEM((4 * width, clip_rows), b_type)],
        ),
        compiler_params=pltpu.CompilerParams(vmem_limit_bytes=vmem_bytes),
        cost_estimate=pl.CostEstimate(
            flops=5 * 10**10, bytes_accessed=15 * 10**7, transcendentals=0
        ),
        name="compress_back",
    )(*scalars, *([bank] * 4), grad_here, grad_other, *after)


def normal_rows(values):
    centered = values - jnp.mean(values, axis=-1, keepdims=True)
    inverse = lax.rsqrt(jnp.mean(centered * centered, axis=-1, keepdims=True) + eps_norm)
    return centered * inverse, inverse


def norm_back(normal, inverse, grad, gain):
    scaled = grad * gain
    return inverse * (
        scaled
        - jnp.mean(scaled, axis=-1, keepdims=True)
        - normal * jnp.mean(scaled * normal, axis=-1, keepdims=True)
    )


def column_sum(values):
    return jnp.sum(values, axis=0, keepdims=True)


def add_pieces(mine, others):
    total = mine[...]
    for other in others:
        total = total + other[0].astype(f_type)
    return total


def second_norm_kernel(half, rows_ref, mine, *refs):
    others = refs[: half - 1]
    bias, gain, shift, mid_ref, out_ref = refs[half - 1 :]
    midway = rows_ref[...].astype(f_type) + (add_pieces(mine, others) + vector(bias))
    mid_ref[...] = midway
    normal, _ = normal_rows(midway)
    out_ref[...] = (normal * vector(gain) + vector(shift)).astype(b_type)


def second_back_kernel(half, mid_ref, mine, *refs):
    others = refs[: half - 1]
    top_ref, gain, d_mid_ref, d_low_ref, sums_ref = refs[half - 1 :]
    normal, inverse = normal_rows(mid_ref[...])
    grad = add_pieces(mine, others)
    top = top_ref[...].astype(f_type)
    d_mid = top + norm_back(normal, inverse, grad, vector(gain))
    d_mid_ref[...] = d_mid
    d_low = d_mid.astype(b_type)
    d_low_ref[...] = d_low
    put_row(sums_ref, 0, column_sum(d_low.astype(f_type)))
    put_row(sums_ref, 8, column_sum(grad * normal))
    put_row(sums_ref, 16, column_sum(grad))
    put_row(sums_ref, 24, column_sum(top))


def first_back_kernel(half, rows_ref, d_mid_ref, gain, mine, *refs):
    others = refs[: half - 1]
    refs = refs[half - 1 :]
    mid_ref, down_bias, mlp_mine = refs[:3]
    mlp_others = refs[3 : 2 + half]
    sums, comp, out_ref, y_ref, late = refs[2 + half :]
    late[0:48, :] = sums[...]
    late[48:, :] = comp[...]
    normal, inverse = normal_rows(rows_ref[...].astype(f_type))
    grad = add_pieces(mine, others)
    out_ref[...] = d_mid_ref[...] + norm_back(normal, inverse, grad, vector(gain))
    y_ref[...] = (mid_ref[...] + add_pieces(mlp_mine, mlp_others) + vector(down_bias)).astype(b_type)


def close_kernel(rows, heads, size, place, *refs):
    halves, late = refs[:2], refs[2]
    w_qkv, w_proj, pool, table, bias, comp, whole, small = refs[3:]
    width = heads * size
    side = 2 * width
    core = core_of(place)
    for step in range(2):
        whole[core ^ step] = halves[step][...]
    w_qkv[0:side, :] = whole[0, 0:side, :].astype(f_type)
    w_qkv[side:, :] = whole[1, 0:width, :].astype(f_type)
    w_proj[...] = whole[1, width:side, :].astype(f_type)
    for line in range(2 * rows.width):
        column = 128 * (line % rows.width)
        small[32 * line : 32 * line + 32, :] = whole[
            line // rows.width, side : side + 32, column : column + 128
        ].astype(f_type)
    for head in range(heads):
        for part in range(3):
            start = 32 * (3 * head + part)
            for tap in range(27):
                pool[part, tap, head : head + 1, :] = small[start + tap : start + tap + 1, 0:size]
        start = rows.table + 48 * head
        for slot in range(41):
            table[slot, head : head + 1, :] = small[start + slot : start + slot + 1, 0:size]
        for part in range(2):
            start = rows.comp + 8 * (2 * head + part)
            comp[head, part] = late[start : start + 8, 0:size]
    bias[...] = small[rows.bias : rows.bias + rows.units, :]


def error_function(values):
    x = jnp.clip(values, -4.0, 4.0)
    y = x * x
    top = -2.72614225801306e-10
    for term in (
        2.77068142495902e-08,
        -2.10102402082508e-06,
        -5.69250639462346e-05,
        -7.34990630326855e-04,
        -2.95459980854025e-03,
        -1.60960333262415e-02,
    ):
        top = top * y + term
    low = -1.45660718464996e-05
    for term in (
        -2.13374055278905e-04,
        -1.68282697438203e-03,
        -7.37332916720468e-03,
        -1.42647390514189e-02,
    ):
        low = low * y + term
    return x * top / low


def mlp_kernel(rows, half, flip, part, place, *refs):
    pieces, tops = refs[:half], refs[half : 2 * half]
    refs = refs[2 * half :]
    up, down = refs[:2]
    halves = refs[2:4]
    (
        bias, small, y_mine, y_other, d_mine, d_other,
        left_keep, right_keep, left_send, right_send, sums,
        tokens_all, top_all, far, y_all, d_all,
    ) = refs[4:]
    put_halves(far, place, halves)
    ups = halves[0].shape[0]
    count = pieces[0].shape[0]
    tokens = jnp.concatenate([piece[...].astype(f_type) for piece in pieces], axis=0).astype(b_type)
    top = jnp.concatenate([piece[...].astype(f_type) for piece in tops], axis=0).astype(b_type)
    units = down.shape[0]
    y_all[...] = jnp.zeros(y_all.shape, f_type)
    d_all[...] = jnp.zeros(d_all.shape, f_type)
    even = core_of(place) == 0
    for block in range(2):
        first = up if block == 0 else far.at[0:ups]
        second = down if block == 0 else far.at[ups : 2 * ups]
        shift = wide_row(bias, 0, rows.units) if block == 0 else wide_row(small, rows.bias, rows.units)
        for start in range(0, units, part):
            here = slice(start, start + part)
            if flip:
                hidden = dot_nt(tokens, first[here, :]) + shift[:, here]
            else:
                hidden = dot(tokens, first[:, here]) + shift[:, here]
            half_slope = 0.5 * (1.0 + error_function(hidden * (0.5**0.5)))
            slope = half_slope + hidden * jnp.exp(-0.5 * hidden * hidden) * 0.3989422804014327
            act = (hidden * half_slope).astype(b_type)
            d_hid = (dot_nt(top, second[here, :]) * slope).astype(b_type)
            put_row(sums, 8 * block + start // 128, column_sum(d_hid.astype(f_type)))
            y_all[...] += dot(act, second[here, :])
            if flip:
                d_all[...] += dot(d_hid, first[here, :])
            else:
                d_all[...] += dot_nt(d_hid, first[:, here])

            def store(keep, send, here=here, act=act, d_hid=d_hid, block=block):
                keep[0 if flip else 1][block, :, here] = d_hid
                send[0][block, :, here] = act

            @pl.when(even)
            def _():
                store((left_keep, right_keep), (left_send, right_send))

            @pl.when(jnp.logical_not(even))
            def _():
                store((left_send, right_send), (left_keep, right_keep))

        def fixed(keep, send, block=block):
            keep[1 if flip else 0][block] = tokens
            send[1][block] = top

        @pl.when(even)
        def _():
            fixed((left_keep, right_keep), (left_send, right_send))

        @pl.when(jnp.logical_not(even))
        def _():
            fixed((left_send, right_send), (left_keep, right_keep))

    y_mine[...] = y_all[0:count, :]
    d_mine[...] = d_all[0:count, :]
    for step in range(1, half):
        span = slice(step * count, (step + 1) * count)
        y_other[step - 1] = y_all[span, :].astype(b_type)
        d_other[step - 1] = d_all[span, :].astype(b_type)


def mlp(rows, flip, place, pieces, tops, up, down, chunks, bias, small, after=()):
    half = len(pieces)
    count, model = pieces[0].shape
    total = half * count
    units = down.shape[0]
    part = units
    left = ((2, total, units if flip else model), b_type)
    down_left = ((2, total, units), b_type)
    right = ((2, total, model), b_type)
    assert left == down_left
    return call(
        functools.partial(mlp_kernel, rows, half, flip, part),
        "mlp",
        12,
        (
            ((count, model), f_type),
            ((half - 1, count, model), b_type),
            ((count, model), f_type),
            ((half - 1, count, model), b_type),
            left,
            right,
            left,
            right,
            ((16, 128), f_type),
        ),
        (place,),
        (*pieces, *tops, up, down, *chunks, bias, small),
        scratch=(
            pltpu.VMEM((total, model), b_type),
            pltpu.VMEM((total, model), b_type),
            pltpu.VMEM((2 * chunks[0].shape[0], model), b_type),
            pltpu.VMEM((total, model), f_type),
            pltpu.VMEM((total, model), f_type),
        ),
        after=after,
    )


def product_kernel(left, right, out_ref):
    for k in range(2):
        out_ref[k] = lax.dot_general(
            left[k], right[k], (((0,), (0,)), ((), ())), preferred_element_type=f_type
        ).astype(b_type)


def product(left, right, after=()):
    shape = (2, left.shape[2], right.shape[2])
    return call(product_kernel, "product", 4, ((shape, b_type),), (), (left, right), after=after)[0]


def product_cut_kernel(quad, place, left, right, came, *refs):
    outs, total = refs[:-1], refs[-1]
    seat = seat_in(place[1], quad)
    size = outs[0].shape[1]
    for k in range(2):
        total[...] = dot_tn(left[k], right[k])
        for step, out in enumerate(outs):
            rows = pl.ds(aligned((seat ^ step) * size, size), size)
            part = total[rows, :].astype(b_type).astype(f_type)
            out[k] = (part + came[k, rows, :].astype(f_type)).astype(out.dtype)


def pick_kernel(count, eighth, *refs):
    sources, out_ref, sem = refs[:count], refs[-2], refs[-1]
    rows = out_ref.shape[0]
    start = 0
    for source in sources:
        parts = source.shape[0] // rows

        @pl.when((eighth[0] >= start) & (eighth[0] < start + parts))
        def _(source=source, start=start):
            copy = pltpu.make_async_copy(
                source.at[pl.ds(aligned((eighth[0] - start) * rows, rows), rows), :], out_ref, sem
            )
            copy.start()
            copy.wait()

        start += parts


def pick(eighth, sources, after=()):
    rows = sum(item.shape[0] for item in sources) // 8
    return pl.pallas_call(
        functools.partial(pick_kernel, len(sources)),
        out_shape=jax.ShapeDtypeStruct((rows, sources[0].shape[1]), b_type),
        in_specs=[pl.BlockSpec(memory_space=pltpu.SMEM)]
        + [pl.BlockSpec(memory_space=pl.ANY)] * (len(sources) + len(after)),
        out_specs=pl.BlockSpec(memory_space=pltpu.VMEM),
        scratch_shapes=[pltpu.SemaphoreType.DMA],
        cost_estimate=pl.CostEstimate(flops=10**10, bytes_accessed=10**7, transcendentals=0),
        name="pick",
    )(eighth, *sources, *after)


def add_kernel(*refs):
    total = refs[0][...].astype(f_type)
    for item in refs[1:-1]:
        total = total + item[...].astype(f_type)
    refs[-1][...] = total.astype(refs[-1].dtype)


def powers(count):
    return [1 << place for place in range(count.bit_length() - 1)]


def add_wide(values, after=()):
    return call(add_kernel, "add", 1, ((values[0].shape, f_type),), (), values, after=after)[0]


def add_low(values, after=()):
    return call(add_kernel, "add", 1, ((values[0].shape, b_type),), (), values, after=after)[0]


def seat_in(spot, quad):
    low, high = (bit.bit_length() - 1 for bit in quad)
    return ((spot >> low) & 1) + 2 * ((spot >> high) & 1)


def cut_kernel(quad, count, place, *refs):
    values, outs = refs[:count], refs[count:]
    seat = seat_in(place[1], quad)
    size = outs[0].shape[-2]
    for step, out in enumerate(outs):
        rows = pl.ds(aligned((seat ^ step) * size, size), size)
        total = None
        for item in values:
            part = (item[:, rows, :] if len(item.shape) == 3 else item[rows, :]).astype(f_type)
            total = part if total is None else total + part
        out[...] = total.astype(out.dtype)


def add_both_kernel(first, *refs):
    for values, out in ((refs[:first], refs[-2]), (refs[first:-2], refs[-1])):
        total = values[0][...].astype(f_type)
        for item in values[1:]:
            total = total + item[...].astype(f_type)
        out[...] = total.astype(out.dtype)


def add_both(one, two, after=()):
    return call(
        functools.partial(add_both_kernel, len(one)),
        "add_both",
        2,
        ((one[0].shape, b_type), (two[0].shape, b_type)),
        (),
        (*one, *two),
        after=after,
    )


def sum_kernel(*refs):
    mine, came, kept, sent = refs[0], refs[1:-2], refs[-2], refs[-1]
    total = mine[...]
    for item in came:
        total = total + item[...].astype(f_type)
    kept[...] = total[0]
    sent[...] = total[1].astype(b_type)


def sum_pair(values, after=()):
    shape = values[0].shape[1:]
    return call(sum_kernel, "sum", 2, ((shape, f_type), (shape, b_type)), (), values, after=after)


def swap_pairs(count, bit):
    return [(place, place ^ bit) for place in range(count)]


class Team:
    def __init__(self, heads_count, clips_count):
        self.total = heads_count
        self.half = heads_count // 2
        self.clips = clips_count
        self.here = lax.axis_index("head")
        self.clip = self.here // self.half
        self.seat = self.here % self.half
        self.spot = lax.axis_index("clip")
        self.place = jnp.stack([self.here, self.spot])

    def partner(self, values):
        return lax.ppermute(values, "head", swap_pairs(self.total, self.half))

    def seats(self, values, step):
        return lax.ppermute(values, "head", swap_pairs(self.total, step))

    def swap(self, values, bit):
        return lax.ppermute(values, "clip", swap_pairs(self.clips, bit))

    def gather(self, rows):
        return [rows] + [self.seats(rows, step) for step in range(1, self.half)]

    def scatter(self, others):
        return [self.seats(others[step - 1 : step], step) for step in range(1, self.half)]

    def eighth(self):
        return (self.spot & 1) * 4 + self.seat_in((2, 4))

    def share(self, came):
        mine = self.collect(came, (2, 4))
        return [mine, self.swap(mine, 1)]

    def quads(self):
        bit, found = 2, []
        while bit < self.clips:
            found.append((bit, 2 * bit))
            bit *= 4
        return found

    def seat_in(self, quad):
        return seat_in(self.spot, quad)

    def peer(self, values, quad, step):
        return self.swap(values, (step & 1) * quad[0] + (step >> 1) * quad[1])

    def cut(self, values, quad, after=()):
        size = values[0].shape[-2] // 4
        if size % 16 == 0:
            shape = (*values[0].shape[:-2], size, values[0].shape[-1])
            return call(
                functools.partial(cut_kernel, quad, len(values)),
                "cut",
                2,
                ((shape, f_type),) + ((shape, b_type),) * 3,
                (self.place,),
                values,
                after=after,
            )
        seat = self.seat_in(quad)

        def quarter(place):
            total = None
            for item in values:
                part = lax.dynamic_slice_in_dim(item, place * size, size, axis=-2).astype(f_type)
                total = part if total is None else total + part
            return total

        return [quarter(seat)] + [quarter(seat ^ step).astype(b_type) for step in (1, 2, 3)]

    def product_cut(self, left, right, came, after=()):
        quad = self.quads()[0]
        rows, columns = left.shape[2], right.shape[2]
        size = rows // 4
        if size % 16:
            return self.cut([product(left, right, after), came], quad)
        shape = (2, size, columns)
        return call(
            functools.partial(product_cut_kernel, quad),
            "product_cut",
            6,
            ((shape, f_type),) + ((shape, b_type),) * 3,
            (self.place,),
            (left, right, came),
            scratch=(pltpu.VMEM((rows, columns), f_type),),
            after=after,
        )

    def join(self, pieces, quad):
        seat = self.seat_in(quad)
        return jnp.concatenate(
            [lax.select_n((seat ^ place).astype(jnp.int32), *pieces) for place in range(4)], axis=0
        )

    def reduce_further(self, values, start=0, after=()):
        quads = self.quads()
        sent = tuple(values)
        for index in range(start, len(quads) + 1):
            quad = quads[index - 1]
            values = [values[0]] + [self.peer(values[step], quad, step) for step in (1, 2, 3)]
            if index < len(quads):
                values = self.cut(values, quads[index], after)
        return values, sent

    def collect(self, chunk, quad):
        pieces = [chunk] + [self.peer(chunk, quad, step) for step in (1, 2, 3)]
        return self.join(pieces, quad)

    def reduce(self, keep, send, after=()):
        values, sent = [keep, self.swap(send, 1)], ()
        for quad in self.quads():
            values = self.cut(values, quad, after)
            sent = sent or tuple(values)
            values = [values[0]] + [self.peer(values[step], quad, step) for step in (1, 2, 3)]
        return values, sent

    def finish(self, chunk):
        for quad in reversed(self.quads()):
            chunk = self.collect(chunk, quad)
        return chunk, self.swap(chunk, 1)


def add(values):
    total = values[0].astype(f_type)
    for item in values[1:]:
        total = total + item.astype(f_type)
    return total


def on_device(
    heads_total,
    clips_total,
    inputs,
    ln1_gain,
    ln1_bias,
    w_qkv,
    pool_kernel,
    rel_table,
    comp_kernel,
    memory_bank,
    mem_index,
    clip_group,
    w_proj,
    proj_bias,
    ln2_gain,
    ln2_bias,
    w_up,
    up_bias,
    w_down,
    down_bias,
    cotangent,
):
    team = Team(heads_total, clips_total)
    half = team.half
    heads, _, size = rel_table.shape
    count, model = inputs.shape
    units = w_up.shape[1]
    width = heads * size
    rows = Rows(heads, units, model)
    flip = units != model
    lined = [
        item.reshape(model // 128, 128)
        for item in (ln1_gain, ln1_bias, proj_bias, ln2_gain, ln2_bias, down_bias)
    ]
    gain1, shift1, bias_proj, gain2, shift2, bias_down = lined
    bias_up = up_bias.reshape(units // 128, 128)
    w_qkv = w_qkv.T
    if flip:
        w_up = w_up.T
    bank = memory_bank.transpose(0, 1, 3, 2)
    place = team.place
    scalars = (place, mem_index, clip_group)

    given = team.gather(inputs)
    eighth = team.eighth().reshape(1).astype(jnp.int32)
    chunk_a = pick(eighth, (w_qkv, w_proj))
    came_a = team.partner(chunk_a)
    mem_here, mem_there = compress(half, scalars, bank, comp_kernel, after=(chunk_a,))
    mem_far = team.partner(mem_there)
    pooled_here, small, came_a, top, *tokens1 = pool_forward(
        rows,
        heads,
        size,
        place,
        given,
        (w_qkv,),
        (pool_kernel.transpose(1, 2, 0, 3), rel_table.transpose(1, 0, 2), bias_up),
        norm=(gain1, shift1),
        passed=(came_a, cotangent),
        after=(mem_here,),
    )
    small_far = team.partner(small)
    chunks_a = team.share(came_a)
    tops = team.gather(top)
    chunk_b = pick(eighth, (w_up, w_down), after=(pooled_here,))
    came_b = team.partner(chunk_b)
    chunks_b = team.share(came_b)
    branch, probs_here, heads_here = attend(
        rows, heads, size, half, place, clip_group, small, mem_here, pooled_here, w_proj,
        after=(mem_far, chunk_b),
    )
    pooled_far, weights = pool_forward(
        rows, heads, size, place, tokens1, chunks_a, (small_far,), after=(branch,)
    )
    branch, branch_other, probs_far, heads_far = attend(
        rows, heads, size, half, place, clip_group, small_far, mem_far, pooled_far, weights,
        branch, after=(came_b, *tops),
    )
    weights_here, weights_far = (w_qkv, w_proj), (weights,)
    branch_came = team.scatter(branch_other)
    midway, norm2 = call(
        functools.partial(second_norm_kernel, half),
        "second_norm",
        2,
        (((count, model), f_type), ((count, model), b_type)),
        (),
        (inputs, branch, *branch_came, bias_proj, gain2, shift2),
    )
    tokens2 = team.gather(norm2)
    y, y_other, d_norm2, d_norm2_other, left_k, right_k, left_s, right_s, d_bias = mlp(
        rows, flip, place, tokens2, tops, w_up, w_down, chunks_b, bias_up, small_far
    )
    d_norm2_came = team.scatter(d_norm2_other)
    send_m = product(left_s, right_s)
    d_mid, d_branch, sums2 = call(
        functools.partial(second_back_kernel, half),
        "second_back",
        3,
        (((count, model), f_type), ((count, model), b_type), ((32, 128), f_type)),
        (),
        (midway, d_norm2, *d_norm2_came, cotangent, gain2),
        after=(send_m,),
    )
    d_branches = team.gather(d_branch)
    cut_m = team.product_cut(left_k, right_k, team.swap(send_m, 1), after=(d_branch,))
    sums_m, sent_m = team.reduce_further(cut_m, 1)
    y_came = team.scatter(y_other)

    d_pooled, d_mem_far, d_table, d_proj = scores_back(
        rows, heads, size, place, d_branches, weights_far, small_far, mem_far, pooled_far,
        probs_far, heads_far, after=(*sent_m, *y_came),
    )
    d_mem_back = team.partner(d_mem_far)
    d_norm1, keep_f, send_f = pool_back(
        rows, heads, size, place, tokens1, weights_far, small_far, d_pooled, d_table, d_proj,
        d_bias[8:16],
    )
    sum_m, part_m = sum_pair(sums_m, after=(d_norm1,))
    came_m = team.partner(part_m)
    sums_f, sent_f = team.reduce(keep_f, send_f, after=(part_m,))
    d_pooled, d_mem_here, d_table, d_proj = scores_back(
        rows, heads, size, place, d_branches, weights_here, small, mem_here, pooled_here,
        probs_here, heads_here, after=(d_norm1, *sent_f),
    )
    part_f, chunk_m = add_both(sums_f, [sum_m, came_m], after=(d_pooled,))
    came_f = team.partner(part_f)
    d_norm1, d_norm1_other, sums, keep_o, send_o = pool_back(
        rows, heads, size, place, tokens1, weights_here, small, d_pooled, d_table, d_proj,
        d_bias[0:8], late=(d_norm1, sums2, *given), after=(part_f, chunk_m, d_mem_back),
    )
    d_norm1_came = team.scatter(d_norm1_other)
    halves_m = team.finish(chunk_m)
    g_comp = compress_back(
        rows, heads, size, half, scalars, bank, d_mem_here, d_mem_back, after=(keep_o,)
    )
    sums_o, sent_o = team.reduce(keep_o, send_o, after=(g_comp,))
    chunk_o = add([*sums_o, came_f]).astype(b_type)
    halves_o = team.finish(chunk_o)
    grad_inputs, output, late = call(
        functools.partial(first_back_kernel, half),
        "first_back",
        3,
        (((count, model), f_type), ((count, model), b_type), ((rows.late, 128), f_type)),
        (),
        (
            inputs, d_mid, gain1, d_norm1, *d_norm1_came, midway, bias_down, y, *y_came,
            sums, g_comp,
        ),
        after=sent_o,
    )
    late = late + team.swap(late, 1)
    for quad in team.quads():
        late = add([late] + [team.peer(late, quad, step) for step in (1, 2, 3)])
    sums = late[:48]
    sums = add([sums] + [team.seats(sums, step) for step in range(1, team.total)])
    odd = core_of((0, team.spot)) != 0
    g_up = jnp.where(odd, halves_m[1], halves_m[0]).astype(f_type)
    g_down = jnp.where(odd, halves_m[0], halves_m[1]).astype(f_type)
    g_qkv, g_proj, g_pool, g_rel, g_bias, g_comp = call(
        functools.partial(close_kernel, rows, heads, size),
        "close",
        3,
        (
            ((3 * width, model), f_type),
            ((width, model), f_type),
            ((3, 27, heads, size), f_type),
            ((41, heads, size), f_type),
            ((units // 128, 128), f_type),
            ((heads, 2, 8, size), f_type),
        ),
        (place,),
        (*halves_o, late),
        scratch=(
            pltpu.VMEM((2, 2 * width + rows.extra, model), b_type),
            pltpu.VMEM((rows.used, 128), f_type),
        ),
    )
    if flip:
        g_up = g_up.T

    def total(index):
        return sums[8 * index : 8 * index + model // 128].reshape(model)

    return (
        output,
        grad_inputs,
        total(4),
        total(5),
        g_qkv.T,
        g_pool.transpose(2, 0, 1, 3),
        g_rel.transpose(1, 0, 2),
        g_comp,
        g_proj,
        total(0),
        total(1),
        total(2),
        g_up,
        g_bias.reshape(units),
        g_down,
        total(3),
    )


def solution(mesh):
    return jax.shard_map(
        functools.partial(on_device, mesh.shape["head"], mesh.shape["clip"]),
        mesh=mesh,
        in_specs=(
            P(("clip", "head"), None),
            P(),
            P(),
            P(None, "head"),
            P("head", None, None, None),
            P("head", None, None),
            P("head", None, None, None),
            P("clip", None, None, "head"),
            P("clip", None),
            P("clip"),
            P("head", None),
            P(),
            P(),
            P(),
            P(None, "head"),
            P("head"),
            P("head", None),
            P(),
            P(("clip", "head"), None),
        ),
        out_specs=(
            P(("clip", "head"), None),
            P(("clip", "head"), None),
            P(),
            P(),
            P(None, "head"),
            P("head", None, None, None),
            P("head", None, None),
            P("head", None, None, None),
            P("head", None),
            P(),
            P(),
            P(),
            P(None, "head"),
            P("head"),
            P("head", None),
            P(),
        ),
        check_vma=False,
    )
```

```python
import functools

import jax
import jax.numpy as jnp
from jax import lax
from jax.experimental import pallas as pl
from jax.experimental.pallas import tpu as pltpu
from jax.sharding import PartitionSpec as P

f_type = jnp.float32
b_type = jnp.bfloat16
eps_norm = 1e-06
neg_large = -1000000000.0
clip_rows = 392
grid_rows = 448
slot_rows = 448
vmem_bytes = 24 * 1024 * 1024


def dot(a, b):
    return jnp.dot(a, b, preferred_element_type=f_type)


def dot_nt(a, b):
    return lax.dot_general(a, b, (((1,), (1,)), ((), ())), preferred_element_type=f_type)


def dot_tn(a, b):
    return lax.dot_general(a, b, (((0,), (0,)), ((), ())), preferred_element_type=f_type)


def iota(shape, axis):
    return lax.broadcasted_iota(jnp.int32, shape, axis)


def one_hot(flag):
    return jnp.where(flag, 1.0, 0.0).astype(b_type)


def split(values):
    high = values.astype(b_type)
    return high, (values - high.astype(f_type)).astype(b_type)


def aligned(start, step):
    return pl.multiple_of(start, step)


def call(kernel, name, cost, results, scalars, arrays, scratch=(), after=()):
    def body(*refs):
        kept = refs[: len(scalars) + len(arrays)]
        kernel(*kept, *refs[len(kept) + len(after) :])

    return pl.pallas_call(
        body,
        out_shape=tuple(jax.ShapeDtypeStruct(shape, kind) for shape, kind in results),
        in_specs=[pl.BlockSpec(memory_space=pltpu.SMEM)] * len(scalars)
        + [pl.BlockSpec(memory_space=pltpu.VMEM)] * len(arrays)
        + [pl.BlockSpec(memory_space=pl.ANY)] * len(after),
        out_specs=tuple(pl.BlockSpec(memory_space=pltpu.VMEM) for _ in results),
        scratch_shapes=list(scratch),
        compiler_params=pltpu.CompilerParams(vmem_limit_bytes=vmem_bytes),
        cost_estimate=pl.CostEstimate(
            flops=int(cost * 1e10), bytes_accessed=int(cost * 3e7), transcendentals=0
        ),
        name=name,
    )(*scalars, *arrays, *after)


def spread_matrix(start, count):
    row = iota((grid_rows, count), 0)
    place = row & 7
    return one_hot(
        ((row >> 3) * 7 + place - start == iota((grid_rows, count), 1)) & (place < 7)
    )


def gather_matrix(start, count):
    row = iota((count, grid_rows), 1)
    place = row & 7
    return one_hot(
        ((row >> 3) * 7 + place - start == iota((count, grid_rows), 0)) & (place < 7)
    )


def to_grid(seat, pieces):
    total = None
    for step, piece in enumerate(pieces):
        rows = piece.shape[0]
        part = dot(spread_matrix((seat ^ step) * rows, rows), piece[...])
        total = part if total is None else total + part
    return total.astype(b_type)


def row_coords(shape, axis):
    row = iota(shape, axis)
    line = row >> 3
    frame = (line * 37) >> 8
    return frame, line - frame * 7, row & 7


def coord_of(kind, coords):
    frame, line, place = coords
    return jnp.where(kind == 0, frame, jnp.where(kind == 1, line, place))


def query_mask():
    shape = (grid_rows, 192)
    column = iota(shape, 1)
    coord = coord_of(column >> 6, row_coords(shape, 0))
    return jnp.where(((column >> 3) & 7) == coord, 1.0, 0.0)


def key_matrix():
    shape = (192, grid_rows)
    column = iota(shape, 0)
    coord = coord_of(column >> 6, row_coords(shape, 1))
    return one_hot((column & 7) == coord)


def key_places():
    shape = (grid_rows, 192)
    column = iota(shape, 1)
    coord = coord_of(column >> 6, row_coords(shape, 0))
    return one_hot((column & 7) == coord)


def table_slot(column):
    kind = column >> 6
    at_query = (column >> 3) & 7
    at_key = column & 7
    base = jnp.where(kind == 0, 7, jnp.where(kind == 1, 21, 34))
    valid = (kind == 0) | ((at_query < 7) & (at_key < 7))
    return jnp.where(valid, base + at_query - at_key, -1)


def table_matrix():
    return one_hot(table_slot(iota((192, 41), 0)) == iota((192, 41), 1))


def own_bias(shape, axis):
    return jnp.where((iota(shape, axis) & 7) == 7, neg_large, 0.0)


def mem_bias(shape, axis, limit):
    slot = iota(shape, axis)
    line = (slot * 586) >> 15
    return jnp.where((slot - 56 * line < 49) & ((line & 3) < limit), 0.0, neg_large)


def clear_border(field):
    width = field.shape[-1]
    field[:, 0:1] = jnp.zeros((3, 1, 9, 8, width), f_type)
    field[:, 9:10] = jnp.zeros((3, 1, 9, 8, width), f_type)
    field[:, :, 0:1] = jnp.zeros((3, 10, 1, 8, width), f_type)
    field[:, :, 8:9] = jnp.zeros((3, 10, 1, 8, width), f_type)


def fill_field(field, values):
    width = values.shape[-1]
    lines = values.reshape(56, 8, width)
    field[0, 1:9, 1:8] = pltpu.roll(lines, 1, 1).reshape(8, 7, 8, width)
    field[1, 1:9, 1:8] = lines.reshape(8, 7, 8, width)
    field[2, 1:9, 1:8] = pltpu.roll(lines, 7, 1).reshape(8, 7, 8, width)


def convolve(field, taps, result, flip):
    width = field.shape[-1]
    for start in range(0, width, 128):
        lanes = slice(start, min(start + 128, width))

        def frame(t, carry):
            total = jnp.zeros((7, 8, lanes.stop - lanes.start), f_type)
            for dt in range(3):
                for dw in range(3):
                    near = field[dw, t + dt, :, :, lanes]
                    for dh in range(3):
                        tap = dt * 9 + dh * 3 + dw
                        tap = 26 - tap if flip else tap
                        total = total + near[dh : dh + 7] * taps[tap : tap + 1, lanes]
            result[t, :, :, lanes] = total
            return carry

        lax.fori_loop(0, 8, frame, 0, unroll=8)


def tap_grads(field, grads, result):
    width = field.shape[-1]
    for start in range(0, width, 128):
        lanes = slice(start, min(start + 128, width))
        size = lanes.stop - lanes.start

        def frame(t, sums):
            grad = grads[1, t + 1, 1:8, :, lanes]
            sums = list(sums)
            for dt in range(3):
                for dw in range(3):
                    near = field[dw, t + dt, :, :, lanes]
                    for dh in range(3):
                        tap = dt * 9 + dh * 3 + dw
                        sums[tap] = sums[tap] + jnp.sum(near[dh : dh + 7] * grad, axis=0)
            return tuple(sums)

        sums = lax.fori_loop(
            0, 8, frame, tuple(jnp.zeros((8, size), f_type) for _ in range(27)), unroll=8
        )
        for tap in range(27):
            result[tap : tap + 1, lanes] = jnp.sum(sums[tap], axis=0, keepdims=True)


class Rows:
    def __init__(self, heads, units, width):
        self.taps = 0
        self.table = self.taps + 96 * heads
        self.bias = self.table + 48 * heads
        self.weights = self.bias + 8
        self.comp = 48
        self.late = self.comp + 16 * heads
        self.units = units // 128
        self.width = width // 128
        self.extra = 64
        self.used = 32 * self.width * 2
        assert self.weights <= self.used


def wide_row(ref, start, count):
    return jnp.concatenate([ref[start + k : start + k + 1, :] for k in range(count)], axis=1)


def put_row(ref, start, values):
    for k in range(values.shape[1] // 128):
        ref[start + k : start + k + 1, :] = values[:, 128 * k : 128 * k + 128]


def vector(ref):
    return wide_row(ref, 0, ref.shape[0])


def seat_of(place, half):
    return place[0] & (half - 1)


def clip_of(place, half):
    return place[0] >> (half.bit_length() - 1)


def core_of(place):
    return place[1] & 1


def put_halves(whole, place, halves):
    size = halves[0].shape[0]
    for step, item in enumerate(halves):
        whole[pl.ds(aligned((core_of(place) ^ step) * size, size), size), :] = item[...]


def weight_views(refs, width):
    if len(refs) == 2:
        return refs[0], refs[1]
    return refs[0].at[0 : 3 * width], refs[0].at[3 * width : 4 * width]


def pack_small(rows, heads, size, pool, table, bias, small):
    for head in range(heads):
        for part in range(3):
            start = 32 * (3 * head + part)
            for tap in range(27):
                small[start + tap : start + tap + 1, 0:size] = pool[part, tap, head : head + 1, :]
        start = rows.table + 48 * head
        for slot in range(41):
            small[start + slot : start + slot + 1, 0:size] = table[slot, head : head + 1, :]
    small[rows.bias : rows.bias + rows.units, :] = bias[...]


def load_taps(taps, small, heads, size):
    for index in range(3 * heads):
        taps[0:27, index * size : (index + 1) * size] = small[
            32 * index : 32 * index + 27, 0:size
        ]


def pool_forward_kernel(rows, heads, size, half, far, passing, place, *refs):
    refs = list(refs)
    pieces = refs[:half]
    del refs[:half]
    if far:
        halves = refs[:2]
        small, pooled_ref, weights, field, taps, wide = refs[2:]
        put_halves(weights, place, halves)
    else:
        gain, shift, weights, *raw = refs[:6]
        del refs[:6]
        passed = refs[:passing]
        pooled_ref, small, *passed_on = refs[passing : 2 + 2 * passing]
        rows_refs, pieces = pieces, refs[2 + 2 * passing : -3]
        pack_small(rows, heads, size, *raw, small)
        field, taps, wide = refs[-3:]
        for source, out in zip(passed, passed_on):
            out[...] = source[...]
        for source, norm in zip(rows_refs, pieces):
            normal, _ = normal_rows(source[...].astype(f_type))
            norm[...] = (normal * vector(gain) + vector(shift)).astype(b_type)
    width = heads * size
    clear_border(field)
    load_taps(taps, small, heads, size)
    fill_field(
        field, dot_nt(to_grid(seat_of(place, half), pieces), weights[0 : 3 * width, :])
    )
    convolve(field, taps, wide, False)
    filled = (iota((grid_rows, 1), 0) & 7) < 7
    pooled_ref[...] = jnp.where(
        filled, wide[...].reshape(grid_rows, 3 * width), 0.0
    ).astype(b_type)


def pool_forward(rows, heads, size, place, pieces, weights, small, norm=(), passed=(), after=()):
    width = heads * size
    half = len(pieces)
    model = pieces[0].shape[1]
    far = not norm
    return call(
        functools.partial(pool_forward_kernel, rows, heads, size, half, far, len(passed)),
        "pool_forward",
        6,
        (((grid_rows, 3 * width), b_type),)
        + (
            (((4 * width, model), b_type),)
            if far
            else (((rows.weights, 128), f_type),)
            + tuple((piece.shape, b_type) for piece in (*passed, *pieces))
        ),
        (place,),
        (*pieces, *norm, *weights, *small, *passed),
        scratch=(
            pltpu.VMEM((3, 10, 9, 8, 3 * width), f_type),
            pltpu.VMEM((32, 3 * width), f_type),
            pltpu.VMEM((8, 7, 8, 3 * width), f_type),
        ),
        after=after,
    )


def attend_kernel(rows, heads, size, half, far, place, groups, *refs):
    refs = list(refs)
    small, mem, pooled, weights = refs[:4]
    del refs[:4]
    base = refs.pop(0) if far else None
    if far:
        mine_ref, other_ref = refs.pop(0), refs.pop(0)
    else:
        branch_ref = refs.pop(0)
    probs_ref, head_ref, query_wide, key_wide, mem_wide, head_wide = refs
    width = heads * size
    scale = size ** (-0.5)
    seat = seat_of(place, half)
    w_proj = weight_views((weights,), width)[1] if far else weights
    rest = 128 - size
    ones = (iota((grid_rows, rest), 1) == 0).astype(f_type)
    query_wide[:, size:128] = ones.astype(b_type)
    key_wide[:, size:128] = (ones * own_bias((grid_rows, rest), 0)).astype(b_type)
    first = (iota((rest, grid_rows), 0) == 0).astype(f_type)
    limit = 4 >> groups[clip_of(place, half)]
    mem_wide[size:128, :] = (first * mem_bias((rest, grid_rows), 1, limit)).astype(b_type)
    keys_at = key_places()
    key_wide[:, 128:320] = keys_at
    key_wide[:, 320:512] = keys_at
    expand = table_matrix()
    mask = query_mask() * (1.0 / scale)
    for head in range(heads):
        at = 3 * head * size
        lanes = slice(head * size, (head + 1) * size)
        queries = pooled[:, at : at + size]
        values = pooled[:, at + 2 * size : at + 3 * size]
        start = rows.table + 48 * head
        table_high, table_low = split(small[start : start + 41, 0:size])
        rel = dot_nt(queries, dot(expand, table_high).astype(b_type)) + dot_nt(
            queries, dot(expand, table_low).astype(b_type)
        )
        high, low = split(rel * mask)
        query_wide[:, 0:size] = queries
        query_wide[:, 128:320] = high
        query_wide[:, 320:512] = low
        key_wide[:, 0:size] = pooled[:, at + size : at + 2 * size]
        mem_wide[0:size, :] = mem[0, lanes, :]
        own = dot_nt(query_wide[...], key_wide[...])
        far_scores = dot(query_wide[:, 0:128], mem_wide[...])
        top = jnp.maximum(
            jnp.max(own, axis=-1, keepdims=True), jnp.max(far_scores, axis=-1, keepdims=True)
        )
        own = jnp.exp((own - top) * scale)
        far_scores = jnp.exp((far_scores - top) * scale)
        total = jnp.sum(own, axis=-1, keepdims=True) + jnp.sum(far_scores, axis=-1, keepdims=True)
        inverse = 1.0 / total
        own = own * inverse
        far_scores = far_scores * inverse
        probs_ref[head, 0] = own
        probs_ref[head, 1] = far_scores
        attended = dot(own.astype(b_type), values) + dot_nt(
            far_scores.astype(b_type), mem[1, lanes, :]
        )
        head_wide[:, lanes] = attended + queries.astype(f_type)
    head_ref[...] = head_wide[...].astype(b_type)
    count = base.shape[1] if far else branch_ref.shape[1]
    for step in range(half):
        head_out = dot(gather_matrix((seat ^ step) * count, count), head_ref[...]).astype(b_type)
        part = dot(head_out, w_proj[...])
        if not far:
            branch_ref[step] = part
        elif step == 0:
            mine_ref[...] = part + base[0]
        else:
            other_ref[step - 1] = (part + base[step]).astype(b_type)


def attend(rows, heads, size, half, place, groups, small, mem, pooled, weights, base=None, after=()):
    width = heads * size
    model = weights.shape[1]
    count = clip_rows // half
    far = base is not None
    branch = (
        (((count, model), f_type), ((half - 1, count, model), b_type))
        if far
        else (((half, count, model), f_type),)
    )
    return call(
        functools.partial(attend_kernel, rows, heads, size, half, far),
        "attend",
        10,
        branch
        + (((heads, 2, grid_rows, grid_rows), f_type), ((grid_rows, width), b_type)),
        (place, groups),
        (small, mem, pooled, weights) + ((base,) if far else ()),
        scratch=(
            pltpu.VMEM((grid_rows, 512), b_type),
            pltpu.VMEM((grid_rows, 512), b_type),
            pltpu.VMEM((128, grid_rows), b_type),
            pltpu.VMEM((grid_rows, width), f_type),
        ),
        after=after,
    )


def scores_back_kernel(rows, heads, size, half, parts, *refs):
    place = refs[0]
    pieces = refs[1 : 1 + half]
    weights = refs[1 + half : 1 + half + parts]
    (
        small, mem, pooled_ref, probs_ref, head_ref,
        d_pooled, d_mem_ref, d_table_ref, d_proj_ref,
        d_head_ref, d_low_ref, probs_low, d_scores,
    ) = refs[1 + half + parts :]
    width = heads * size
    scale = size ** (-0.5)
    w_proj = weight_views(weights, width)[1]
    d_branch = to_grid(seat_of(place, half), pieces)
    d_head = dot_nt(d_branch, w_proj[...])
    d_head_ref[...] = d_head
    d_low_ref[...] = d_head.astype(b_type)
    expand = table_matrix()
    keys_at = key_matrix()
    mask = query_mask()
    for head in range(heads):
        at = 3 * head * size
        lanes = slice(head * size, (head + 1) * size)
        queries = pooled_ref[:, at : at + size]
        keys = pooled_ref[:, at + size : at + 2 * size]
        values = pooled_ref[:, at + 2 * size : at + 3 * size]
        mem_keys = mem[0, lanes, :]
        mem_values = mem[1, lanes, :]

        d_att = d_low_ref[:, lanes]
        own = probs_ref[head, 0]
        far_probs = probs_ref[head, 1]
        d_own = dot_nt(d_att, values)
        d_far = dot(d_att, mem_values)
        inner = jnp.sum(own * d_own, axis=-1, keepdims=True) + jnp.sum(
            far_probs * d_far, axis=-1, keepdims=True
        )
        d_scores[0] = (own * (d_own - inner)).astype(b_type)
        d_scores[1] = (far_probs * (d_far - inner)).astype(b_type)
        probs_low[0] = own.astype(b_type)
        probs_low[1] = far_probs.astype(b_type)
        d_query = (dot(d_scores[0], keys) + dot_nt(d_scores[1], mem_keys)) * scale
        start = rows.table + 48 * head
        table_high, table_low = split(small[start : start + 41, 0:size])
        rel_high, rel_low = split(dot_nt(d_scores[0], keys_at) * mask)
        wide_high = dot(expand, table_high).astype(b_type)
        wide_low = dot(expand, table_low).astype(b_type)
        d_rel = dot(rel_high, wide_high) + dot(rel_low, wide_high) + dot(rel_high, wide_low)
        d_pooled[:, at : at + size] = d_query + d_head_ref[:, lanes] + d_rel
        queries_t = jnp.transpose(queries.astype(f_type)).astype(b_type)
        d_att_t = jnp.transpose(d_head_ref[:, lanes]).astype(b_type)
        wide_high, wide_low = split(dot(queries_t, rel_high) + dot(queries_t, rel_low))
        d_table = dot(wide_high, expand) + dot(wide_low, expand)
        d_table_ref[48 * head : 48 * head + 41, 0:size] = jnp.transpose(d_table)
        d_pooled[:, at + size : at + 2 * size] = jnp.transpose(dot(queries_t, d_scores[0])) * scale
        d_mem_ref[0, lanes, :] = (dot(queries_t, d_scores[1]) * scale).astype(b_type)
        d_pooled[:, at + 2 * size : at + 3 * size] = jnp.transpose(dot(d_att_t, probs_low[0]))
        d_mem_ref[1, lanes, :] = dot(d_att_t, probs_low[1]).astype(b_type)
    head_t = jnp.transpose(head_ref[...].astype(f_type)).astype(b_type)
    d_proj_ref[...] = dot(head_t, d_branch).astype(b_type)


def scores_back(rows, heads, size, place, pieces, weights, small, mem, pooled, probs, head, after=()):
    width = heads * size
    return call(
        functools.partial(scores_back_kernel, rows, heads, size, len(pieces), len(weights)),
        "scores_back",
        13,
        (
            ((grid_rows, 3 * width), f_type),
            ((2, width, slot_rows), b_type),
            ((48 * heads, 128), f_type),
            ((width, pieces[0].shape[1]), b_type),
        ),
        (place,),
        (*pieces, *weights, small, mem, pooled, probs, head),
        scratch=(
            pltpu.VMEM((grid_rows, width), f_type),
            pltpu.VMEM((grid_rows, width), b_type),
            pltpu.VMEM((2, grid_rows, grid_rows), b_type),
            pltpu.VMEM((2, grid_rows, grid_rows), b_type),
        ),
        after=after,
    )


def pool_back_kernel(rows, heads, size, half, parts, last, *refs):
    place = refs[0]
    pieces = refs[1 : 1 + half]
    weights = refs[1 + half : 1 + half + parts]
    refs = list(refs[1 + half + parts :])
    small, d_pooled, d_table, d_proj, d_bias = refs[:5]
    del refs[:5]
    if last:
        base, sums_early = refs[:2]
        inputs = refs[2 : 2 + half]
        mine_ref, other_ref, sums_ref = refs[2 + half : 5 + half]
        del refs[: 5 + half]
    else:
        norm_ref = refs.pop(0)
    keep_ref, send_ref, field, grads, taps, wide, packed, d_taps, small_grads = refs
    width = heads * size
    seat = seat_of(place, half)
    w_qkv = weight_views(weights, width)[0]
    clear_border(field)
    clear_border(grads)
    load_taps(taps, small, heads, size)
    tokens = to_grid(seat, pieces)
    fill_field(field, dot_nt(tokens, w_qkv[...]))
    fill_field(grads, d_pooled[...])
    convolve(grads, taps, wide, True)
    d_qkv = wide[...].reshape(grid_rows, 3 * width)
    low = d_qkv.astype(b_type)
    count = pieces[0].shape[0]
    gains, shifts = [], []
    for step in range(half):
        part = dot(gather_matrix((seat ^ step) * count, count), low).astype(b_type)
        part = dot(part, w_qkv[...])
        if not last:
            norm_ref[step] = part
            continue
        part = part + base[step]
        if step == 0:
            mine_ref[...] = part
        else:
            other_ref[step - 1] = part.astype(b_type)
        normal, _ = normal_rows(inputs[step][...].astype(f_type))
        gains.append(column_sum(part * normal))
        shifts.append(column_sum(part))
    if last:
        sums_ref[0:32, :] = sums_early[...]
        put_row(sums_ref, 32, sum(gains[1:], gains[0]))
        put_row(sums_ref, 40, sum(shifts[1:], shifts[0]))
    side = 2 * width
    g_qkv = dot(jnp.transpose(d_qkv).astype(b_type), tokens).astype(b_type)
    packed[0, 0:side, :] = g_qkv[0:side]
    packed[1, 0:width, :] = g_qkv[side : 3 * width]
    packed[1, width:side, :] = d_proj[...]
    tap_grads(field, grads, d_taps)
    small_grads[...] = jnp.zeros(small_grads.shape, f_type)
    for index in range(3 * heads):
        small_grads[32 * index : 32 * index + 27, 0:size] = d_taps[
            0:27, index * size : (index + 1) * size
        ]
    for head in range(heads):
        start = rows.table + 48 * head
        small_grads[start : start + 41, 0:size] = d_table[48 * head : 48 * head + 41, 0:size]
    small_grads[rows.bias : rows.bias + rows.units, :] = d_bias[0 : rows.units, :]
    packed[:, side:, :] = jnp.zeros((2, rows.extra, packed.shape[2]), b_type)
    for line in range(2 * rows.width):
        column = 128 * (line % rows.width)
        packed[line // rows.width, side : side + 32, column : column + 128] = small_grads[
            32 * line : 32 * line + 32, :
        ].astype(b_type)
    core = core_of(place)
    keep_ref[...] = packed[core]
    send_ref[...] = packed[1 - core]


def pool_back(rows, heads, size, place, pieces, weights, small, d_pooled, d_table, d_proj, d_bias,
              late=(), after=()):
    width = heads * size
    half = len(pieces)
    count, model = pieces[0].shape
    last = bool(late)
    norm = (
        (((count, model), f_type), ((half - 1, count, model), b_type), ((48, 128), f_type))
        if last
        else (((half, count, model), f_type),)
    )
    return call(
        functools.partial(pool_back_kernel, rows, heads, size, half, len(weights), last),
        "pool_back",
        9,
        norm
        + (
            ((2 * width + rows.extra, model), b_type),
            ((2 * width + rows.extra, model), b_type),
        ),
        (place,),
        (*pieces, *weights, small, d_pooled, d_table, d_proj, d_bias, *late),
        scratch=(
            pltpu.VMEM((3, 10, 9, 8, 3 * width), f_type),
            pltpu.VMEM((3, 10, 9, 8, 3 * width), f_type),
            pltpu.VMEM((32, 3 * width), f_type),
            pltpu.VMEM((8, 7, 8, 3 * width), f_type),
            pltpu.VMEM((2, 2 * width + rows.extra, model), b_type),
            pltpu.VMEM((32, 3 * width), f_type),
            pltpu.VMEM((rows.used, 128), f_type),
        ),
        after=after,
    )


def frame_of(token):
    return (token * 669) >> 15


def tap_matrix(group):
    frame = frame_of(iota((8, clip_rows), 1))
    return one_hot((frame & ((2 << group) - 1)) == iota((8, clip_rows), 0))


def slot_matrix(which, group):
    token = iota((clip_rows, slot_rows), 0)
    slot = iota((clip_rows, slot_rows), 1)
    frame = frame_of(token)
    line = (slot * 586) >> 15
    return one_hot(
        ((line >> 2) == which)
        & ((line & 3) == (frame >> (group + 1)))
        & (slot - 56 * line == token - 49 * frame)
    )


def compress_kernel(half, place, rows_ref, groups, *refs):
    banks, taps_ref = refs[:4], refs[4]
    outs, products, factors = refs[-4:-2], refs[-2], refs[-1]
    heads, _, _, size = taps_ref.shape
    width = heads * size
    for other in range(2):
        group = groups[clip_of(place, half) ^ other]
        spread = tap_matrix(group)
        for kind in range(2):
            for head in range(heads):
                high, low = split(taps_ref[head, kind])
                factors[kind, head * size : (head + 1) * size, :] = dot_tn(high, spread) + dot_tn(
                    low, spread
                )
        total = None
        for which in range(2):
            for kind in range(2):
                bank = banks[2 * other + which][0, kind].astype(f_type)
                high, low = split(bank * factors[kind])
                products[2 * kind * width : (2 * kind + 1) * width, :] = high
                products[(2 * kind + 1) * width : (2 * kind + 2) * width, :] = low
            part = dot(products[...], slot_matrix(which, group))
            total = part if total is None else total + part
        for kind in range(2):
            start = 2 * kind * width
            outs[other][kind] = (
                total[start : start + width] + total[start + width : start + 2 * width]
            ).astype(b_type)


def bank_spec(width, half, other, which):
    def where(step, place, rows_ref, groups):
        return rows_ref[clip_of(place, half) ^ other, which], 0, 0, 0

    return pl.BlockSpec((1, 2, width, clip_rows), where)


def bank_specs(width, half):
    return [bank_spec(width, half, other, which) for other in range(2) for which in range(2)]


def whole_spec(shape):
    return pl.BlockSpec(shape, lambda *_: (0,) * len(shape))


def compress(half, scalars, bank, taps, after=()):
    width = bank.shape[2]
    shape = (2, width, slot_rows)
    return pl.pallas_call(
        functools.partial(compress_kernel, half),
        out_shape=(jax.ShapeDtypeStruct(shape, b_type),) * 2,
        grid_spec=pltpu.PrefetchScalarGridSpec(
            num_scalar_prefetch=3,
            grid=(1,),
            in_specs=bank_specs(width, half)
            + [whole_spec(taps.shape)]
            + [pl.BlockSpec(memory_space=pl.ANY)] * len(after),
            out_specs=(whole_spec(shape),) * 2,
            scratch_shapes=[
                pltpu.VMEM((4 * width, clip_rows), b_type),
                pltpu.VMEM((2, width, clip_rows), f_type),
            ],
        ),
        compiler_params=pltpu.CompilerParams(vmem_limit_bytes=vmem_bytes),
        cost_estimate=pl.CostEstimate(
            flops=5 * 10**10, bytes_accessed=15 * 10**7, transcendentals=0
        ),
        name="compress",
    )(*scalars, *([bank] * 4), taps, *after)


def compress_back_kernel(rows, heads, size, half, place, rows_ref, groups, *refs):
    banks, grads, out_ref, products = refs[:4], refs[4:6], refs[-2], refs[-1]
    width = grads[0].shape[1]
    total = None
    for other in range(2):
        group = groups[clip_of(place, half) ^ other]
        grad = grads[other][...].reshape(2 * width, slot_rows)
        taps = tap_matrix(group)
        for which in range(2):
            spread = dot_nt(grad, slot_matrix(which, group))
            for kind in range(2):
                bank = banks[2 * other + which][0, kind].astype(f_type)
                high, low = split(bank * spread[kind * width : (kind + 1) * width])
                products[2 * kind * width : (2 * kind + 1) * width, :] = high
                products[(2 * kind + 1) * width : (2 * kind + 2) * width, :] = low
            part = dot_nt(taps, products[...])
            total = part if total is None else total + part
    out_ref[...] = jnp.zeros(out_ref.shape, f_type)
    for head in range(heads):
        for part in range(2):
            start = 8 * (2 * head + part)
            at = 2 * part * width + head * size
            out_ref[start : start + 8, 0:size] = (
                total[:, at : at + size] + total[:, at + width : at + width + size]
            )


def compress_back(rows, heads, size, half, scalars, bank, grad_here, grad_other, after=()):
    width = bank.shape[2]
    return pl.pallas_call(
        functools.partial(compress_back_kernel, rows, heads, size, half),
        out_shape=jax.ShapeDtypeStruct((16 * heads, 128), f_type),
        grid_spec=pltpu.PrefetchScalarGridSpec(
            num_scalar_prefetch=3,
            grid=(1,),
            in_specs=bank_specs(width, half)
            + [whole_spec((2, width, slot_rows))] * 2
            + [pl.BlockSpec(memory_space=pl.ANY)] * len(after),
            out_specs=whole_spec((16 * heads, 128)),
            scratch_shapes=[pltpu.VMEM((4 * width, clip_rows), b_type)],
        ),
        compiler_params=pltpu.CompilerParams(vmem_limit_bytes=vmem_bytes),
        cost_estimate=pl.CostEstimate(
            flops=5 * 10**10, bytes_accessed=15 * 10**7, transcendentals=0
        ),
        name="compress_back",
    )(*scalars, *([bank] * 4), grad_here, grad_other, *after)


def normal_rows(values):
    centered = values - jnp.mean(values, axis=-1, keepdims=True)
    inverse = lax.rsqrt(jnp.mean(centered * centered, axis=-1, keepdims=True) + eps_norm)
    return centered * inverse, inverse


def norm_back(normal, inverse, grad, gain):
    scaled = grad * gain
    return inverse * (
        scaled
        - jnp.mean(scaled, axis=-1, keepdims=True)
        - normal * jnp.mean(scaled * normal, axis=-1, keepdims=True)
    )


def column_sum(values):
    return jnp.sum(values, axis=0, keepdims=True)


def add_pieces(mine, others):
    total = mine[...]
    for other in others:
        total = total + other[0].astype(f_type)
    return total


def second_norm_kernel(half, rows_ref, mine, *refs):
    others = refs[: half - 1]
    bias, gain, shift, mid_ref, out_ref = refs[half - 1 :]
    midway = rows_ref[...].astype(f_type) + (add_pieces(mine, others) + vector(bias))
    mid_ref[...] = midway
    normal, _ = normal_rows(midway)
    out_ref[...] = (normal * vector(gain) + vector(shift)).astype(b_type)


def second_back_kernel(half, mid_ref, mine, *refs):
    others = refs[: half - 1]
    top_ref, gain, d_mid_ref, d_low_ref, sums_ref = refs[half - 1 :]
    normal, inverse = normal_rows(mid_ref[...])
    grad = add_pieces(mine, others)
    top = top_ref[...].astype(f_type)
    d_mid = top + norm_back(normal, inverse, grad, vector(gain))
    d_mid_ref[...] = d_mid
    d_low = d_mid.astype(b_type)
    d_low_ref[...] = d_low
    put_row(sums_ref, 0, column_sum(d_low.astype(f_type)))
    put_row(sums_ref, 8, column_sum(grad * normal))
    put_row(sums_ref, 16, column_sum(grad))
    put_row(sums_ref, 24, column_sum(top))


def first_back_kernel(half, rows_ref, d_mid_ref, gain, mine, *refs):
    others = refs[: half - 1]
    refs = refs[half - 1 :]
    mid_ref, down_bias, mlp_mine = refs[:3]
    mlp_others = refs[3 : 2 + half]
    sums, comp, out_ref, y_ref, late = refs[2 + half :]
    late[0:48, :] = sums[...]
    late[48:, :] = comp[...]
    normal, inverse = normal_rows(rows_ref[...].astype(f_type))
    grad = add_pieces(mine, others)
    out_ref[...] = d_mid_ref[...] + norm_back(normal, inverse, grad, vector(gain))
    y_ref[...] = (mid_ref[...] + add_pieces(mlp_mine, mlp_others) + vector(down_bias)).astype(b_type)


def close_kernel(rows, heads, size, place, *refs):
    halves, late = refs[:2], refs[2]
    w_qkv, w_proj, pool, table, bias, comp, whole, small = refs[3:]
    width = heads * size
    side = 2 * width
    core = core_of(place)
    for step in range(2):
        whole[core ^ step] = halves[step][...]
    w_qkv[0:side, :] = whole[0, 0:side, :].astype(f_type)
    w_qkv[side:, :] = whole[1, 0:width, :].astype(f_type)
    w_proj[...] = whole[1, width:side, :].astype(f_type)
    for line in range(2 * rows.width):
        column = 128 * (line % rows.width)
        small[32 * line : 32 * line + 32, :] = whole[
            line // rows.width, side : side + 32, column : column + 128
        ].astype(f_type)
    for head in range(heads):
        for part in range(3):
            start = 32 * (3 * head + part)
            for tap in range(27):
                pool[part, tap, head : head + 1, :] = small[start + tap : start + tap + 1, 0:size]
        start = rows.table + 48 * head
        for slot in range(41):
            table[slot, head : head + 1, :] = small[start + slot : start + slot + 1, 0:size]
        for part in range(2):
            start = rows.comp + 8 * (2 * head + part)
            comp[head, part] = late[start : start + 8, 0:size]
    bias[...] = small[rows.bias : rows.bias + rows.units, :]


def error_function(values):
    x = jnp.clip(values, -4.0, 4.0)
    y = x * x
    top = -2.72614225801306e-10
    for term in (
        2.77068142495902e-08,
        -2.10102402082508e-06,
        -5.69250639462346e-05,
        -7.34990630326855e-04,
        -2.95459980854025e-03,
        -1.60960333262415e-02,
    ):
        top = top * y + term
    low = -1.45660718464996e-05
    for term in (
        -2.13374055278905e-04,
        -1.68282697438203e-03,
        -7.37332916720468e-03,
        -1.42647390514189e-02,
    ):
        low = low * y + term
    return x * top / low


def mlp_kernel(rows, half, flip, part, place, *refs):
    pieces, tops = refs[:half], refs[half : 2 * half]
    refs = refs[2 * half :]
    up, down = refs[:2]
    halves = refs[2:4]
    (
        bias, small, y_mine, y_other, d_mine, d_other,
        left_keep, right_keep, left_send, right_send, sums,
        tokens_all, top_all, far, y_all, d_all,
    ) = refs[4:]
    put_halves(far, place, halves)
    ups = halves[0].shape[0]
    count = pieces[0].shape[0]
    tokens = jnp.concatenate([piece[...].astype(f_type) for piece in pieces], axis=0).astype(b_type)
    top = jnp.concatenate([piece[...].astype(f_type) for piece in tops], axis=0).astype(b_type)
    units = down.shape[0]
    y_all[...] = jnp.zeros(y_all.shape, f_type)
    d_all[...] = jnp.zeros(d_all.shape, f_type)
    even = core_of(place) == 0
    for block in range(2):
        first = up if block == 0 else far.at[0:ups]
        second = down if block == 0 else far.at[ups : 2 * ups]
        shift = wide_row(bias, 0, rows.units) if block == 0 else wide_row(small, rows.bias, rows.units)
        for start in range(0, units, part):
            here = slice(start, start + part)
            if flip:
                hidden = dot_nt(tokens, first[here, :]) + shift[:, here]
            else:
                hidden = dot(tokens, first[:, here]) + shift[:, here]
            half_slope = 0.5 * (1.0 + error_function(hidden * (0.5**0.5)))
            slope = half_slope + hidden * jnp.exp(-0.5 * hidden * hidden) * 0.3989422804014327
            act = (hidden * half_slope).astype(b_type)
            d_hid = (dot_nt(top, second[here, :]) * slope).astype(b_type)
            put_row(sums, 8 * block + start // 128, column_sum(d_hid.astype(f_type)))
            y_all[...] += dot(act, second[here, :])
            if flip:
                d_all[...] += dot(d_hid, first[here, :])
            else:
                d_all[...] += dot_nt(d_hid, first[:, here])

            def store(keep, send, here=here, act=act, d_hid=d_hid, block=block):
                keep[0 if flip else 1][block, :, here] = d_hid
                send[0][block, :, here] = act

            @pl.when(even)
            def _():
                store((left_keep, right_keep), (left_send, right_send))

            @pl.when(jnp.logical_not(even))
            def _():
                store((left_send, right_send), (left_keep, right_keep))

        def fixed(keep, send, block=block):
            keep[1 if flip else 0][block] = tokens
            send[1][block] = top

        @pl.when(even)
        def _():
            fixed((left_keep, right_keep), (left_send, right_send))

        @pl.when(jnp.logical_not(even))
        def _():
            fixed((left_send, right_send), (left_keep, right_keep))

    y_mine[...] = y_all[0:count, :]
    d_mine[...] = d_all[0:count, :]
    for step in range(1, half):
        span = slice(step * count, (step + 1) * count)
        y_other[step - 1] = y_all[span, :].astype(b_type)
        d_other[step - 1] = d_all[span, :].astype(b_type)


def mlp(rows, flip, place, pieces, tops, up, down, chunks, bias, small, after=()):
    half = len(pieces)
    count, model = pieces[0].shape
    total = half * count
    units = down.shape[0]
    part = units
    left = ((2, total, units if flip else model), b_type)
    down_left = ((2, total, units), b_type)
    right = ((2, total, model), b_type)
    assert left == down_left
    return call(
        functools.partial(mlp_kernel, rows, half, flip, part),
        "mlp",
        12,
        (
            ((count, model), f_type),
            ((half - 1, count, model), b_type),
            ((count, model), f_type),
            ((half - 1, count, model), b_type),
            left,
            right,
            left,
            right,
            ((16, 128), f_type),
        ),
        (place,),
        (*pieces, *tops, up, down, *chunks, bias, small),
        scratch=(
            pltpu.VMEM((total, model), b_type),
            pltpu.VMEM((total, model), b_type),
            pltpu.VMEM((2 * chunks[0].shape[0], model), b_type),
            pltpu.VMEM((total, model), f_type),
            pltpu.VMEM((total, model), f_type),
        ),
        after=after,
    )


def product_kernel(left, right, out_ref):
    for k in range(2):
        out_ref[k] = lax.dot_general(
            left[k], right[k], (((0,), (0,)), ((), ())), preferred_element_type=f_type
        ).astype(b_type)


def product(left, right, after=()):
    shape = (2, left.shape[2], right.shape[2])
    return call(product_kernel, "product", 4, ((shape, b_type),), (), (left, right), after=after)[0]


def product_cut_kernel(quad, place, left, right, came, *refs):
    outs, total = refs[:-1], refs[-1]
    seat = seat_in(place[1], quad)
    size = outs[0].shape[1]
    for k in range(2):
        total[...] = dot_tn(left[k], right[k])
        for step, out in enumerate(outs):
            rows = pl.ds(aligned((seat ^ step) * size, size), size)
            part = total[rows, :].astype(b_type).astype(f_type)
            out[k] = (part + came[k, rows, :].astype(f_type)).astype(out.dtype)


def pick_kernel(count, eighth, *refs):
    sources, out_ref, sem = refs[:count], refs[-2], refs[-1]
    rows = out_ref.shape[0]
    start = 0
    for source in sources:
        parts = source.shape[0] // rows

        @pl.when((eighth[0] >= start) & (eighth[0] < start + parts))
        def _(source=source, start=start):
            copy = pltpu.make_async_copy(
                source.at[pl.ds(aligned((eighth[0] - start) * rows, rows), rows), :], out_ref, sem
            )
            copy.start()
            copy.wait()

        start += parts


def pick(eighth, sources, after=()):
    rows = sum(item.shape[0] for item in sources) // 8
    return pl.pallas_call(
        functools.partial(pick_kernel, len(sources)),
        out_shape=jax.ShapeDtypeStruct((rows, sources[0].shape[1]), b_type),
        in_specs=[pl.BlockSpec(memory_space=pltpu.SMEM)]
        + [pl.BlockSpec(memory_space=pl.ANY)] * (len(sources) + len(after)),
        out_specs=pl.BlockSpec(memory_space=pltpu.VMEM),
        scratch_shapes=[pltpu.SemaphoreType.DMA],
        cost_estimate=pl.CostEstimate(flops=10**10, bytes_accessed=10**7, transcendentals=0),
        name="pick",
    )(eighth, *sources, *after)


def add_kernel(*refs):
    total = refs[0][...].astype(f_type)
    for item in refs[1:-1]:
        total = total + item[...].astype(f_type)
    refs[-1][...] = total.astype(refs[-1].dtype)


def powers(count):
    return [1 << place for place in range(count.bit_length() - 1)]


def add_wide(values, after=()):
    return call(add_kernel, "add", 1, ((values[0].shape, f_type),), (), values, after=after)[0]


def add_low(values, after=()):
    return call(add_kernel, "add", 1, ((values[0].shape, b_type),), (), values, after=after)[0]


def seat_in(spot, quad):
    low, high = (bit.bit_length() - 1 for bit in quad)
    return ((spot >> low) & 1) + 2 * ((spot >> high) & 1)


def cut_kernel(quad, count, place, *refs):
    values, outs = refs[:count], refs[count:]
    seat = seat_in(place[1], quad)
    size = outs[0].shape[-2]
    for step, out in enumerate(outs):
        rows = pl.ds(aligned((seat ^ step) * size, size), size)
        total = None
        for item in values:
            part = (item[:, rows, :] if len(item.shape) == 3 else item[rows, :]).astype(f_type)
            total = part if total is None else total + part
        out[...] = total.astype(out.dtype)


def add_both_kernel(first, *refs):
    for values, out in ((refs[:first], refs[-2]), (refs[first:-2], refs[-1])):
        total = values[0][...].astype(f_type)
        for item in values[1:]:
            total = total + item[...].astype(f_type)
        out[...] = total.astype(out.dtype)


def add_both(one, two, after=()):
    return call(
        functools.partial(add_both_kernel, len(one)),
        "add_both",
        2,
        ((one[0].shape, b_type), (two[0].shape, b_type)),
        (),
        (*one, *two),
        after=after,
    )


def sum_kernel(*refs):
    mine, came, kept, sent = refs[0], refs[1:-2], refs[-2], refs[-1]
    total = mine[...]
    for item in came:
        total = total + item[...].astype(f_type)
    kept[...] = total[0]
    sent[...] = total[1].astype(b_type)


def sum_pair(values, after=()):
    shape = values[0].shape[1:]
    return call(sum_kernel, "sum", 2, ((shape, f_type), (shape, b_type)), (), values, after=after)


def swap_pairs(count, bit):
    return [(place, place ^ bit) for place in range(count)]


class Team:
    def __init__(self, heads_count, clips_count):
        self.total = heads_count
        self.half = heads_count // 2
        self.clips = clips_count
        self.here = lax.axis_index("head")
        self.clip = self.here // self.half
        self.seat = self.here % self.half
        self.spot = lax.axis_index("clip")
        self.place = jnp.stack([self.here, self.spot])

    def partner(self, values):
        return lax.ppermute(values, "head", swap_pairs(self.total, self.half))

    def seats(self, values, step):
        return lax.ppermute(values, "head", swap_pairs(self.total, step))

    def swap(self, values, bit):
        return lax.ppermute(values, "clip", swap_pairs(self.clips, bit))

    def gather(self, rows):
        return [rows] + [self.seats(rows, step) for step in range(1, self.half)]

    def scatter(self, others):
        return [self.seats(others[step - 1 : step], step) for step in range(1, self.half)]

    def eighth(self):
        return (self.spot & 1) * 4 + self.seat_in((2, 4))

    def share(self, came):
        mine = self.collect(came, (2, 4))
        return [mine, self.swap(mine, 1)]

    def quads(self):
        bit, found = 2, []
        while bit < self.clips:
            found.append((bit, 2 * bit))
            bit *= 4
        return found

    def seat_in(self, quad):
        return seat_in(self.spot, quad)

    def peer(self, values, quad, step):
        return self.swap(values, (step & 1) * quad[0] + (step >> 1) * quad[1])

    def cut(self, values, quad, after=()):
        size = values[0].shape[-2] // 4
        if size % 16 == 0:
            shape = (*values[0].shape[:-2], size, values[0].shape[-1])
            return call(
                functools.partial(cut_kernel, quad, len(values)),
                "cut",
                2,
                ((shape, f_type),) + ((shape, b_type),) * 3,
                (self.place,),
                values,
                after=after,
            )
        seat = self.seat_in(quad)

        def quarter(place):
            total = None
            for item in values:
                part = lax.dynamic_slice_in_dim(item, place * size, size, axis=-2).astype(f_type)
                total = part if total is None else total + part
            return total

        return [quarter(seat)] + [quarter(seat ^ step).astype(b_type) for step in (1, 2, 3)]

    def product_cut(self, left, right, came, after=()):
        quad = self.quads()[0]
        rows, columns = left.shape[2], right.shape[2]
        size = rows // 4
        if size % 16:
            return self.cut([product(left, right, after), came], quad)
        shape = (2, size, columns)
        return call(
            functools.partial(product_cut_kernel, quad),
            "product_cut",
            6,
            ((shape, f_type),) + ((shape, b_type),) * 3,
            (self.place,),
            (left, right, came),
            scratch=(pltpu.VMEM((rows, columns), f_type),),
            after=after,
        )

    def join(self, pieces, quad):
        seat = self.seat_in(quad)
        return jnp.concatenate(
            [lax.select_n((seat ^ place).astype(jnp.int32), *pieces) for place in range(4)], axis=0
        )

    def reduce_further(self, values, start=0, after=()):
        quads = self.quads()
        sent = tuple(values)
        for index in range(start, len(quads) + 1):
            quad = quads[index - 1]
            values = [values[0]] + [self.peer(values[step], quad, step) for step in (1, 2, 3)]
            if index < len(quads):
                values = self.cut(values, quads[index], after)
        return values, sent

    def collect(self, chunk, quad):
        pieces = [chunk] + [self.peer(chunk, quad, step) for step in (1, 2, 3)]
        return self.join(pieces, quad)

    def reduce(self, keep, send, after=()):
        values, sent = [keep, self.swap(send, 1)], ()
        for quad in self.quads():
            values = self.cut(values, quad, after)
            sent = sent or tuple(values)
            values = [values[0]] + [self.peer(values[step], quad, step) for step in (1, 2, 3)]
        return values, sent

    def finish(self, chunk):
        for quad in reversed(self.quads()):
            chunk = self.collect(chunk, quad)
        return chunk, self.swap(chunk, 1)


def add(values):
    total = values[0].astype(f_type)
    for item in values[1:]:
        total = total + item.astype(f_type)
    return total


def on_device(
    heads_total,
    clips_total,
    inputs,
    ln1_gain,
    ln1_bias,
    w_qkv,
    pool_kernel,
    rel_table,
    comp_kernel,
    memory_bank,
    mem_index,
    clip_group,
    w_proj,
    proj_bias,
    ln2_gain,
    ln2_bias,
    w_up,
    up_bias,
    w_down,
    down_bias,
    cotangent,
):
    team = Team(heads_total, clips_total)
    half = team.half
    heads, _, size = rel_table.shape
    count, model = inputs.shape
    units = w_up.shape[1]
    width = heads * size
    rows = Rows(heads, units, model)
    flip = units != model
    lined = [
        item.reshape(model // 128, 128)
        for item in (ln1_gain, ln1_bias, proj_bias, ln2_gain, ln2_bias, down_bias)
    ]
    gain1, shift1, bias_proj, gain2, shift2, bias_down = lined
    bias_up = up_bias.reshape(units // 128, 128)
    w_qkv = w_qkv.T
    if flip:
        w_up = w_up.T
    bank = memory_bank.transpose(0, 1, 3, 2)
    place = team.place
    scalars = (place, mem_index, clip_group)

    given = team.gather(inputs)
    eighth = team.eighth().reshape(1).astype(jnp.int32)
    chunk_a = pick(eighth, (w_qkv, w_proj))
    came_a = team.partner(chunk_a)
    mem_here, mem_there = compress(half, scalars, bank, comp_kernel, after=(chunk_a,))
    mem_far = team.partner(mem_there)
    pooled_here, small, came_a, top, *tokens1 = pool_forward(
        rows,
        heads,
        size,
        place,
        given,
        (w_qkv,),
        (pool_kernel.transpose(1, 2, 0, 3), rel_table.transpose(1, 0, 2), bias_up),
        norm=(gain1, shift1),
        passed=(came_a, cotangent),
        after=(mem_here,),
    )
    small_far = team.partner(small)
    chunks_a = team.share(came_a)
    tops = team.gather(top)
    chunk_b = pick(eighth, (w_up, w_down), after=(pooled_here,))
    came_b = team.partner(chunk_b)
    chunks_b = team.share(came_b)
    branch, probs_here, heads_here = attend(
        rows, heads, size, half, place, clip_group, small, mem_here, pooled_here, w_proj,
        after=(mem_far, chunk_b),
    )
    pooled_far, weights = pool_forward(
        rows, heads, size, place, tokens1, chunks_a, (small_far,), after=(branch,)
    )
    branch, branch_other, probs_far, heads_far = attend(
        rows, heads, size, half, place, clip_group, small_far, mem_far, pooled_far, weights,
        branch, after=(came_b, *tops),
    )
    weights_here, weights_far = (w_qkv, w_proj), (weights,)
    branch_came = team.scatter(branch_other)
    midway, norm2 = call(
        functools.partial(second_norm_kernel, half),
        "second_norm",
        2,
        (((count, model), f_type), ((count, model), b_type)),
        (),
        (inputs, branch, *branch_came, bias_proj, gain2, shift2),
    )
    tokens2 = team.gather(norm2)
    y, y_other, d_norm2, d_norm2_other, left_k, right_k, left_s, right_s, d_bias = mlp(
        rows, flip, place, tokens2, tops, w_up, w_down, chunks_b, bias_up, small_far
    )
    d_norm2_came = team.scatter(d_norm2_other)
    send_m = product(left_s, right_s)
    d_mid, d_branch, sums2 = call(
        functools.partial(second_back_kernel, half),
        "second_back",
        3,
        (((count, model), f_type), ((count, model), b_type), ((32, 128), f_type)),
        (),
        (midway, d_norm2, *d_norm2_came, cotangent, gain2),
        after=(send_m,),
    )
    d_branches = team.gather(d_branch)
    cut_m = team.product_cut(left_k, right_k, team.swap(send_m, 1), after=(d_branch,))
    sums_m, sent_m = team.reduce_further(cut_m, 1)
    y_came = team.scatter(y_other)

    d_pooled, d_mem_far, d_table, d_proj = scores_back(
        rows, heads, size, place, d_branches, weights_far, small_far, mem_far, pooled_far,
        probs_far, heads_far, after=(*sent_m, *y_came),
    )
    d_mem_back = team.partner(d_mem_far)
    d_norm1, keep_f, send_f = pool_back(
        rows, heads, size, place, tokens1, weights_far, small_far, d_pooled, d_table, d_proj,
        d_bias[8:16],
    )
    sum_m, part_m = sum_pair(sums_m, after=(d_norm1,))
    came_m = team.partner(part_m)
    sums_f, sent_f = team.reduce(keep_f, send_f, after=(part_m,))
    d_pooled, d_mem_here, d_table, d_proj = scores_back(
        rows, heads, size, place, d_branches, weights_here, small, mem_here, pooled_here,
        probs_here, heads_here, after=(d_norm1, *sent_f),
    )
    part_f, chunk_m = add_both(sums_f, [sum_m, came_m], after=(d_pooled,))
    came_f = team.partner(part_f)
    d_norm1, d_norm1_other, sums, keep_o, send_o = pool_back(
        rows, heads, size, place, tokens1, weights_here, small, d_pooled, d_table, d_proj,
        d_bias[0:8], late=(d_norm1, sums2, *given), after=(part_f, chunk_m, d_mem_back),
    )
    d_norm1_came = team.scatter(d_norm1_other)
    halves_m = team.finish(chunk_m)
    g_comp = compress_back(
        rows, heads, size, half, scalars, bank, d_mem_here, d_mem_back, after=(keep_o,)
    )
    sums_o, sent_o = team.reduce(keep_o, send_o, after=(g_comp,))
    chunk_o = add([*sums_o, came_f]).astype(b_type)
    halves_o = team.finish(chunk_o)
    grad_inputs, output, late = call(
        functools.partial(first_back_kernel, half),
        "first_back",
        3,
        (((count, model), f_type), ((count, model), b_type), ((rows.late, 128), f_type)),
        (),
        (
            inputs, d_mid, gain1, d_norm1, *d_norm1_came, midway, bias_down, y, *y_came,
            sums, g_comp,
        ),
        after=sent_o,
    )
    late = late + team.swap(late, 1)
    for quad in team.quads():
        late = add([late] + [team.peer(late, quad, step) for step in (1, 2, 3)])
    sums = late[:48]
    sums = add([sums] + [team.seats(sums, step) for step in range(1, team.total)])
    odd = core_of((0, team.spot)) != 0
    g_up = jnp.where(odd, halves_m[1], halves_m[0]).astype(f_type)
    g_down = jnp.where(odd, halves_m[0], halves_m[1]).astype(f_type)
    g_qkv, g_proj, g_pool, g_rel, g_bias, g_comp = call(
        functools.partial(close_kernel, rows, heads, size),
        "close",
        3,
        (
            ((3 * width, model), f_type),
            ((width, model), f_type),
            ((3, 27, heads, size), f_type),
            ((41, heads, size), f_type),
            ((units // 128, 128), f_type),
            ((heads, 2, 8, size), f_type),
        ),
        (place,),
        (*halves_o, late),
        scratch=(
            pltpu.VMEM((2, 2 * width + rows.extra, model), b_type),
            pltpu.VMEM((rows.used, 128), f_type),
        ),
    )
    if flip:
        g_up = g_up.T

    def total(index):
        return sums[8 * index : 8 * index + model // 128].reshape(model)

    return (
        output,
        grad_inputs,
        total(4),
        total(5),
        g_qkv.T,
        g_pool.transpose(2, 0, 1, 3),
        g_rel.transpose(1, 0, 2),
        g_comp,
        g_proj,
        total(0),
        total(1),
        total(2),
        g_up,
        g_bias.reshape(units),
        g_down,
        total(3),
    )


def solution(mesh):
    return jax.shard_map(
        functools.partial(on_device, mesh.shape["head"], mesh.shape["clip"]),
        mesh=mesh,
        in_specs=(
            P(("clip", "head"), None),
            P(),
            P(),
            P(None, "head"),
            P("head", None, None, None),
            P("head", None, None),
            P("head", None, None, None),
            P("clip", None, None, "head"),
            P("clip", None),
            P("clip"),
            P("head", None),
            P(),
            P(),
            P(),
            P(None, "head"),
            P("head"),
            P("head", None),
            P(),
            P(("clip", "head"), None),
        ),
        out_specs=(
            P(("clip", "head"), None),
            P(("clip", "head"), None),
            P(),
            P(),
            P(None, "head"),
            P("head", None, None, None),
            P("head", None, None),
            P("head", None, None, None),
            P("head", None),
            P(),
            P(),
            P(),
            P(None, "head"),
            P("head"),
            P("head", None),
            P(),
        ),
        check_vma=False,
    )
```

```python
import functools

import jax
import jax.numpy as jnp
from jax import lax
from jax.experimental import pallas as pl
from jax.experimental.pallas import tpu as pltpu
from jax.sharding import PartitionSpec as P

f_type = jnp.float32
b_type = jnp.bfloat16
eps_norm = 1e-06
neg_large = -1000000000.0
clip_rows = 392
grid_rows = 448
slot_rows = 448
vmem_bytes = 24 * 1024 * 1024
vmem_whole = 56 * 1024 * 1024


def dot(a, b):
    return jnp.dot(a, b, preferred_element_type=f_type)


def dot_nt(a, b):
    return lax.dot_general(a, b, (((1,), (1,)), ((), ())), preferred_element_type=f_type)


def dot_tn(a, b):
    return lax.dot_general(a, b, (((0,), (0,)), ((), ())), preferred_element_type=f_type)


def iota(shape, axis):
    return lax.broadcasted_iota(jnp.int32, shape, axis)


def one_hot(flag):
    return jnp.where(flag, 1.0, 0.0).astype(b_type)


def split(values):
    high = values.astype(b_type)
    return high, (values - high.astype(f_type)).astype(b_type)


def aligned(start, step):
    return pl.multiple_of(start, step)


def call(kernel, name, cost, results, scalars, arrays, scratch=(), after=(), room=vmem_bytes):
    def body(*refs):
        kept = refs[: len(scalars) + len(arrays)]
        kernel(*kept, *refs[len(kept) + len(after) :])

    return pl.pallas_call(
        body,
        out_shape=tuple(jax.ShapeDtypeStruct(shape, kind) for shape, kind in results),
        in_specs=[pl.BlockSpec(memory_space=pltpu.SMEM)] * len(scalars)
        + [pl.BlockSpec(memory_space=pltpu.VMEM)] * len(arrays)
        + [pl.BlockSpec(memory_space=pl.ANY)] * len(after),
        out_specs=tuple(pl.BlockSpec(memory_space=pltpu.VMEM) for _ in results),
        scratch_shapes=list(scratch),
        compiler_params=pltpu.CompilerParams(vmem_limit_bytes=room),
        cost_estimate=pl.CostEstimate(
            flops=int(cost * 1e10), bytes_accessed=int(cost * 3e7), transcendentals=0
        ),
        name=name,
    )(*scalars, *arrays, *after)


def spread_matrix(start, count):
    row = iota((grid_rows, count), 0)
    place = row & 7
    return one_hot(
        ((row >> 3) * 7 + place - start == iota((grid_rows, count), 1)) & (place < 7)
    )


def gather_matrix(start, count):
    row = iota((count, grid_rows), 1)
    place = row & 7
    return one_hot(
        ((row >> 3) * 7 + place - start == iota((count, grid_rows), 0)) & (place < 7)
    )


def to_grid(seat, pieces):
    total = None
    for step, piece in enumerate(pieces):
        rows = piece.shape[0]
        part = dot(spread_matrix((seat ^ step) * rows, rows), piece[...])
        total = part if total is None else total + part
    return total.astype(b_type)


def row_coords(shape, axis):
    row = iota(shape, axis)
    line = row >> 3
    frame = (line * 37) >> 8
    return frame, line - frame * 7, row & 7


def coord_of(kind, coords):
    frame, line, place = coords
    return jnp.where(kind == 0, frame, jnp.where(kind == 1, line, place))


def query_mask():
    shape = (grid_rows, 192)
    column = iota(shape, 1)
    coord = coord_of(column >> 6, row_coords(shape, 0))
    return jnp.where(((column >> 3) & 7) == coord, 1.0, 0.0)


def key_matrix():
    shape = (192, grid_rows)
    column = iota(shape, 0)
    coord = coord_of(column >> 6, row_coords(shape, 1))
    return one_hot((column & 7) == coord)


def key_places():
    shape = (grid_rows, 192)
    column = iota(shape, 1)
    coord = coord_of(column >> 6, row_coords(shape, 0))
    return one_hot((column & 7) == coord)


def table_slot(column):
    kind = column >> 6
    at_query = (column >> 3) & 7
    at_key = column & 7
    base = jnp.where(kind == 0, 7, jnp.where(kind == 1, 21, 34))
    valid = (kind == 0) | ((at_query < 7) & (at_key < 7))
    return jnp.where(valid, base + at_query - at_key, -1)


def table_matrix():
    return one_hot(table_slot(iota((192, 41), 0)) == iota((192, 41), 1))


def own_bias(shape, axis):
    return jnp.where((iota(shape, axis) & 7) == 7, neg_large, 0.0)


def mem_bias(shape, axis, limit):
    slot = iota(shape, axis)
    line = (slot * 586) >> 15
    return jnp.where((slot - 56 * line < 49) & ((line & 3) < limit), 0.0, neg_large)


def clear_border(field):
    width = field.shape[-1]
    field[:, 0:1] = jnp.zeros((3, 1, 9, 8, width), f_type)
    field[:, 9:10] = jnp.zeros((3, 1, 9, 8, width), f_type)
    field[:, :, 0:1] = jnp.zeros((3, 10, 1, 8, width), f_type)
    field[:, :, 8:9] = jnp.zeros((3, 10, 1, 8, width), f_type)


def fill_field(field, values):
    width = values.shape[-1]
    lines = values.reshape(56, 8, width)
    field[0, 1:9, 1:8] = pltpu.roll(lines, 1, 1).reshape(8, 7, 8, width)
    field[1, 1:9, 1:8] = lines.reshape(8, 7, 8, width)
    field[2, 1:9, 1:8] = pltpu.roll(lines, 7, 1).reshape(8, 7, 8, width)


def convolve(field, taps, result, flip):
    width = field.shape[-1]
    for start in range(0, width, 128):
        lanes = slice(start, min(start + 128, width))

        def frame(t, carry):
            total = jnp.zeros((7, 8, lanes.stop - lanes.start), f_type)
            for dt in range(3):
                for dw in range(3):
                    near = field[dw, t + dt, :, :, lanes]
                    for dh in range(3):
                        tap = dt * 9 + dh * 3 + dw
                        tap = 26 - tap if flip else tap
                        total = total + near[dh : dh + 7] * taps[tap : tap + 1, lanes]
            result[t, :, :, lanes] = total
            return carry

        lax.fori_loop(0, 8, frame, 0, unroll=8)


def tap_grads(field, grads, result):
    width = field.shape[-1]
    for start in range(0, width, 128):
        lanes = slice(start, min(start + 128, width))
        size = lanes.stop - lanes.start

        def frame(t, sums):
            grad = grads[1, t + 1, 1:8, :, lanes]
            sums = list(sums)
            for dt in range(3):
                for dw in range(3):
                    near = field[dw, t + dt, :, :, lanes]
                    for dh in range(3):
                        tap = dt * 9 + dh * 3 + dw
                        sums[tap] = sums[tap] + jnp.sum(near[dh : dh + 7] * grad, axis=0)
            return tuple(sums)

        sums = lax.fori_loop(
            0, 8, frame, tuple(jnp.zeros((8, size), f_type) for _ in range(27)), unroll=8
        )
        for tap in range(27):
            result[tap : tap + 1, lanes] = jnp.sum(sums[tap], axis=0, keepdims=True)


class Rows:
    def __init__(self, heads, units, width):
        self.taps = 0
        self.table = self.taps + 96 * heads
        self.bias = self.table + 48 * heads
        self.weights = self.bias + 8
        self.comp = 48
        self.late = self.comp + 16 * heads
        self.units = units // 128
        self.width = width // 128
        self.extra = 64
        self.used = 32 * self.width * 2
        assert self.weights <= self.used


def wide_row(ref, start, count):
    return jnp.concatenate([ref[start + k : start + k + 1, :] for k in range(count)], axis=1)


def put_row(ref, start, values):
    for k in range(values.shape[1] // 128):
        ref[start + k : start + k + 1, :] = values[:, 128 * k : 128 * k + 128]


def vector(ref):
    return wide_row(ref, 0, ref.shape[0])


def seat_of(place, half):
    return place[0] & (half - 1)


def clip_of(place, half):
    return place[0] >> (half.bit_length() - 1)


def core_of(place):
    return place[1] & 1


def put_halves(whole, place, halves):
    size = halves[0].shape[0]
    for step, item in enumerate(halves):
        whole[pl.ds(aligned((core_of(place) ^ step) * size, size), size), :] = item[...]


def weight_views(refs, width):
    if len(refs) == 2:
        return refs[0], refs[1]
    return refs[0].at[0 : 3 * width], refs[0].at[3 * width : 4 * width]


def pack_small(rows, heads, size, pool, table, bias, small):
    for head in range(heads):
        for part in range(3):
            start = 32 * (3 * head + part)
            for tap in range(27):
                small[start + tap : start + tap + 1, 0:size] = pool[part, tap, head : head + 1, :]
        start = rows.table + 48 * head
        for slot in range(41):
            small[start + slot : start + slot + 1, 0:size] = table[slot, head : head + 1, :]
    small[rows.bias : rows.bias + rows.units, :] = bias[...]


def load_taps(taps, small, heads, size):
    for index in range(3 * heads):
        taps[0:27, index * size : (index + 1) * size] = small[
            32 * index : 32 * index + 27, 0:size
        ]


def pool_forward_kernel(rows, heads, size, half, far, passing, place, *refs):
    refs = list(refs)
    pieces = refs[:half]
    del refs[:half]
    if far:
        halves = refs[:2]
        small, pooled_ref, weights, field, taps, wide = refs[2:]
        put_halves(weights, place, halves)
    else:
        gain, shift, weights, *raw = refs[:6]
        del refs[:6]
        passed = refs[:passing]
        pooled_ref, small, *passed_on = refs[passing : 2 + 2 * passing]
        rows_refs, pieces = pieces, refs[2 + 2 * passing : -3]
        pack_small(rows, heads, size, *raw, small)
        field, taps, wide = refs[-3:]
        for source, out in zip(passed, passed_on):
            out[...] = source[...]
        for source, norm in zip(rows_refs, pieces):
            normal, _ = normal_rows(source[...].astype(f_type))
            norm[...] = (normal * vector(gain) + vector(shift)).astype(b_type)
    width = heads * size
    clear_border(field)
    load_taps(taps, small, heads, size)
    fill_field(
        field, dot_nt(to_grid(seat_of(place, half), pieces), weights[0 : 3 * width, :])
    )
    convolve(field, taps, wide, False)
    filled = (iota((grid_rows, 1), 0) & 7) < 7
    pooled_ref[...] = jnp.where(
        filled, wide[...].reshape(grid_rows, 3 * width), 0.0
    ).astype(b_type)


def pool_forward(rows, heads, size, place, pieces, weights, small, norm=(), passed=(), after=()):
    width = heads * size
    half = len(pieces)
    model = pieces[0].shape[1]
    far = not norm
    return call(
        functools.partial(pool_forward_kernel, rows, heads, size, half, far, len(passed)),
        "pool_forward",
        6,
        (((grid_rows, 3 * width), b_type),)
        + (
            (((4 * width, model), b_type),)
            if far
            else (((rows.weights, 128), f_type),)
            + tuple((piece.shape, b_type) for piece in (*passed, *pieces))
        ),
        (place,),
        (*pieces, *norm, *weights, *small, *passed),
        scratch=(
            pltpu.VMEM((3, 10, 9, 8, 3 * width), f_type),
            pltpu.VMEM((32, 3 * width), f_type),
            pltpu.VMEM((8, 7, 8, 3 * width), f_type),
        ),
        after=after,
        room=vmem_bytes if far else vmem_whole,
    )


def attend_kernel(rows, heads, size, half, far, place, groups, *refs):
    refs = list(refs)
    small, mem, pooled, weights = refs[:4]
    del refs[:4]
    base = refs.pop(0) if far else None
    if far:
        mine_ref, other_ref = refs.pop(0), refs.pop(0)
    else:
        branch_ref = refs.pop(0)
    probs_ref, head_ref, query_wide, key_wide, mem_wide, head_wide = refs
    width = heads * size
    scale = size ** (-0.5)
    seat = seat_of(place, half)
    w_proj = weight_views((weights,), width)[1] if far else weights
    rest = 128 - size
    ones = (iota((grid_rows, rest), 1) == 0).astype(f_type)
    query_wide[:, size:128] = ones.astype(b_type)
    key_wide[:, size:128] = (ones * own_bias((grid_rows, rest), 0)).astype(b_type)
    first = (iota((rest, grid_rows), 0) == 0).astype(f_type)
    limit = 4 >> groups[clip_of(place, half)]
    mem_wide[size:128, :] = (first * mem_bias((rest, grid_rows), 1, limit)).astype(b_type)
    keys_at = key_places()
    key_wide[:, 128:320] = keys_at
    key_wide[:, 320:512] = keys_at
    expand = table_matrix()
    mask = query_mask() * (1.0 / scale)
    for head in range(heads):
        at = 3 * head * size
        lanes = slice(head * size, (head + 1) * size)
        queries = pooled[:, at : at + size]
        values = pooled[:, at + 2 * size : at + 3 * size]
        start = rows.table + 48 * head
        table_high, table_low = split(small[start : start + 41, 0:size])
        rel = dot_nt(queries, dot(expand, table_high).astype(b_type)) + dot_nt(
            queries, dot(expand, table_low).astype(b_type)
        )
        high, low = split(rel * mask)
        query_wide[:, 0:size] = queries
        query_wide[:, 128:320] = high
        query_wide[:, 320:512] = low
        key_wide[:, 0:size] = pooled[:, at + size : at + 2 * size]
        mem_wide[0:size, :] = mem[0, lanes, :]
        own = dot_nt(query_wide[...], key_wide[...])
        far_scores = dot(query_wide[:, 0:128], mem_wide[...])
        top = jnp.maximum(
            jnp.max(own, axis=-1, keepdims=True), jnp.max(far_scores, axis=-1, keepdims=True)
        )
        own = jnp.exp((own - top) * scale)
        far_scores = jnp.exp((far_scores - top) * scale)
        total = jnp.sum(own, axis=-1, keepdims=True) + jnp.sum(far_scores, axis=-1, keepdims=True)
        inverse = 1.0 / total
        own = own * inverse
        far_scores = far_scores * inverse
        probs_ref[head, 0] = own
        probs_ref[head, 1] = far_scores
        attended = dot(own.astype(b_type), values) + dot_nt(
            far_scores.astype(b_type), mem[1, lanes, :]
        )
        head_wide[:, lanes] = attended + queries.astype(f_type)
    head_ref[...] = head_wide[...].astype(b_type)
    count = base.shape[1] if far else branch_ref.shape[1]
    for step in range(half):
        head_out = dot(gather_matrix((seat ^ step) * count, count), head_ref[...]).astype(b_type)
        part = dot(head_out, w_proj[...])
        if not far:
            branch_ref[step] = part
        elif step == 0:
            mine_ref[...] = part + base[0]
        else:
            other_ref[step - 1] = (part + base[step]).astype(b_type)


def attend(rows, heads, size, half, place, groups, small, mem, pooled, weights, base=None, after=()):
    width = heads * size
    model = weights.shape[1]
    count = clip_rows // half
    far = base is not None
    branch = (
        (((count, model), f_type), ((half - 1, count, model), b_type))
        if far
        else (((half, count, model), f_type),)
    )
    return call(
        functools.partial(attend_kernel, rows, heads, size, half, far),
        "attend",
        10,
        branch
        + (((heads, 2, grid_rows, grid_rows), f_type), ((grid_rows, width), b_type)),
        (place, groups),
        (small, mem, pooled, weights) + ((base,) if far else ()),
        scratch=(
            pltpu.VMEM((grid_rows, 512), b_type),
            pltpu.VMEM((grid_rows, 512), b_type),
            pltpu.VMEM((128, grid_rows), b_type),
            pltpu.VMEM((grid_rows, width), f_type),
        ),
        after=after,
    )


def scores_back_kernel(rows, heads, size, half, parts, *refs):
    place = refs[0]
    pieces = refs[1 : 1 + half]
    weights = refs[1 + half : 1 + half + parts]
    (
        small, mem, pooled_ref, probs_ref, head_ref,
        d_pooled, d_mem_ref, d_table_ref, d_proj_ref,
        d_head_ref, d_low_ref, probs_low, d_scores,
    ) = refs[1 + half + parts :]
    width = heads * size
    scale = size ** (-0.5)
    w_proj = weight_views(weights, width)[1]
    d_branch = to_grid(seat_of(place, half), pieces)
    d_head = dot_nt(d_branch, w_proj[...])
    d_head_ref[...] = d_head
    d_low_ref[...] = d_head.astype(b_type)
    expand = table_matrix()
    keys_at = key_matrix()
    mask = query_mask()
    for head in range(heads):
        at = 3 * head * size
        lanes = slice(head * size, (head + 1) * size)
        queries = pooled_ref[:, at : at + size]
        keys = pooled_ref[:, at + size : at + 2 * size]
        values = pooled_ref[:, at + 2 * size : at + 3 * size]
        mem_keys = mem[0, lanes, :]
        mem_values = mem[1, lanes, :]

        d_att = d_low_ref[:, lanes]
        own = probs_ref[head, 0]
        far_probs = probs_ref[head, 1]
        d_own = dot_nt(d_att, values)
        d_far = dot(d_att, mem_values)
        inner = jnp.sum(own * d_own, axis=-1, keepdims=True) + jnp.sum(
            far_probs * d_far, axis=-1, keepdims=True
        )
        d_scores[0] = (own * (d_own - inner)).astype(b_type)
        d_scores[1] = (far_probs * (d_far - inner)).astype(b_type)
        probs_low[0] = own.astype(b_type)
        probs_low[1] = far_probs.astype(b_type)
        d_query = (dot(d_scores[0], keys) + dot_nt(d_scores[1], mem_keys)) * scale
        start = rows.table + 48 * head
        table_high, table_low = split(small[start : start + 41, 0:size])
        rel_high, rel_low = split(dot_nt(d_scores[0], keys_at) * mask)
        wide_high = dot(expand, table_high).astype(b_type)
        wide_low = dot(expand, table_low).astype(b_type)
        d_rel = dot(rel_high, wide_high) + dot(rel_low, wide_high) + dot(rel_high, wide_low)
        d_pooled[:, at : at + size] = d_query + d_head_ref[:, lanes] + d_rel
        queries_t = jnp.transpose(queries.astype(f_type)).astype(b_type)
        d_att_t = jnp.transpose(d_head_ref[:, lanes]).astype(b_type)
        wide_high, wide_low = split(dot(queries_t, rel_high) + dot(queries_t, rel_low))
        d_table = dot(wide_high, expand) + dot(wide_low, expand)
        d_table_ref[48 * head : 48 * head + 41, 0:size] = jnp.transpose(d_table)
        d_pooled[:, at + size : at + 2 * size] = jnp.transpose(dot(queries_t, d_scores[0])) * scale
        d_mem_ref[0, lanes, :] = (dot(queries_t, d_scores[1]) * scale).astype(b_type)
        d_pooled[:, at + 2 * size : at + 3 * size] = jnp.transpose(dot(d_att_t, probs_low[0]))
        d_mem_ref[1, lanes, :] = dot(d_att_t, probs_low[1]).astype(b_type)
    head_t = jnp.transpose(head_ref[...].astype(f_type)).astype(b_type)
    d_proj_ref[...] = dot(head_t, d_branch).astype(b_type)


def scores_back(rows, heads, size, place, pieces, weights, small, mem, pooled, probs, head, after=()):
    width = heads * size
    return call(
        functools.partial(scores_back_kernel, rows, heads, size, len(pieces), len(weights)),
        "scores_back",
        13,
        (
            ((grid_rows, 3 * width), f_type),
            ((2, width, slot_rows), b_type),
            ((48 * heads, 128), f_type),
            ((width, pieces[0].shape[1]), b_type),
        ),
        (place,),
        (*pieces, *weights, small, mem, pooled, probs, head),
        scratch=(
            pltpu.VMEM((grid_rows, width), f_type),
            pltpu.VMEM((grid_rows, width), b_type),
            pltpu.VMEM((2, grid_rows, grid_rows), b_type),
            pltpu.VMEM((2, grid_rows, grid_rows), b_type),
        ),
        after=after,
    )


def pool_back_kernel(rows, heads, size, half, parts, last, *refs):
    place = refs[0]
    pieces = refs[1 : 1 + half]
    weights = refs[1 + half : 1 + half + parts]
    refs = list(refs[1 + half + parts :])
    small, d_pooled, d_table, d_proj, d_bias = refs[:5]
    del refs[:5]
    if last:
        base, sums_early = refs[:2]
        inputs = refs[2 : 2 + half]
        mine_ref, other_ref, sums_ref = refs[2 + half : 5 + half]
        del refs[: 5 + half]
    else:
        norm_ref = refs.pop(0)
    keep_ref, send_ref, field, grads, taps, wide, packed, d_taps, small_grads = refs
    width = heads * size
    seat = seat_of(place, half)
    w_qkv = weight_views(weights, width)[0]
    clear_border(field)
    clear_border(grads)
    load_taps(taps, small, heads, size)
    tokens = to_grid(seat, pieces)
    fill_field(field, dot_nt(tokens, w_qkv[...]))
    fill_field(grads, d_pooled[...])
    convolve(grads, taps, wide, True)
    d_qkv = wide[...].reshape(grid_rows, 3 * width)
    low = d_qkv.astype(b_type)
    count = pieces[0].shape[0]
    gains, shifts = [], []
    for step in range(half):
        part = dot(gather_matrix((seat ^ step) * count, count), low).astype(b_type)
        part = dot(part, w_qkv[...])
        if not last:
            norm_ref[step] = part
            continue
        part = part + base[step]
        if step == 0:
            mine_ref[...] = part
        else:
            other_ref[step - 1] = part.astype(b_type)
        normal, _ = normal_rows(inputs[step][...].astype(f_type))
        gains.append(column_sum(part * normal))
        shifts.append(column_sum(part))
    if last:
        sums_ref[0:32, :] = sums_early[...]
        put_row(sums_ref, 32, sum(gains[1:], gains[0]))
        put_row(sums_ref, 40, sum(shifts[1:], shifts[0]))
    side = 2 * width
    g_qkv = dot(jnp.transpose(d_qkv).astype(b_type), tokens).astype(b_type)
    packed[0, 0:side, :] = g_qkv[0:side]
    packed[1, 0:width, :] = g_qkv[side : 3 * width]
    packed[1, width:side, :] = d_proj[...]
    tap_grads(field, grads, d_taps)
    small_grads[...] = jnp.zeros(small_grads.shape, f_type)
    for index in range(3 * heads):
        small_grads[32 * index : 32 * index + 27, 0:size] = d_taps[
            0:27, index * size : (index + 1) * size
        ]
    for head in range(heads):
        start = rows.table + 48 * head
        small_grads[start : start + 41, 0:size] = d_table[48 * head : 48 * head + 41, 0:size]
    small_grads[rows.bias : rows.bias + rows.units, :] = d_bias[0 : rows.units, :]
    packed[:, side:, :] = jnp.zeros((2, rows.extra, packed.shape[2]), b_type)
    for line in range(2 * rows.width):
        column = 128 * (line % rows.width)
        packed[line // rows.width, side : side + 32, column : column + 128] = small_grads[
            32 * line : 32 * line + 32, :
        ].astype(b_type)
    core = core_of(place)
    keep_ref[...] = packed[core]
    send_ref[...] = packed[1 - core]


def pool_back(rows, heads, size, place, pieces, weights, small, d_pooled, d_table, d_proj, d_bias,
              late=(), after=()):
    width = heads * size
    half = len(pieces)
    count, model = pieces[0].shape
    last = bool(late)
    norm = (
        (((count, model), f_type), ((half - 1, count, model), b_type), ((48, 128), f_type))
        if last
        else (((half, count, model), f_type),)
    )
    return call(
        functools.partial(pool_back_kernel, rows, heads, size, half, len(weights), last),
        "pool_back",
        9,
        norm
        + (
            ((2 * width + rows.extra, model), b_type),
            ((2 * width + rows.extra, model), b_type),
        ),
        (place,),
        (*pieces, *weights, small, d_pooled, d_table, d_proj, d_bias, *late),
        scratch=(
            pltpu.VMEM((3, 10, 9, 8, 3 * width), f_type),
            pltpu.VMEM((3, 10, 9, 8, 3 * width), f_type),
            pltpu.VMEM((32, 3 * width), f_type),
            pltpu.VMEM((8, 7, 8, 3 * width), f_type),
            pltpu.VMEM((2, 2 * width + rows.extra, model), b_type),
            pltpu.VMEM((32, 3 * width), f_type),
            pltpu.VMEM((rows.used, 128), f_type),
        ),
        after=after,
    )


def frame_of(token):
    return (token * 669) >> 15


def tap_matrix(group):
    frame = frame_of(iota((8, clip_rows), 1))
    return one_hot((frame & ((2 << group) - 1)) == iota((8, clip_rows), 0))


def slot_matrix(which, group):
    token = iota((clip_rows, slot_rows), 0)
    slot = iota((clip_rows, slot_rows), 1)
    frame = frame_of(token)
    line = (slot * 586) >> 15
    return one_hot(
        ((line >> 2) == which)
        & ((line & 3) == (frame >> (group + 1)))
        & (slot - 56 * line == token - 49 * frame)
    )


def compress_kernel(half, place, rows_ref, groups, *refs):
    banks, taps_ref = refs[:4], refs[4]
    outs, products, factors = refs[-4:-2], refs[-2], refs[-1]
    heads, _, _, size = taps_ref.shape
    width = heads * size
    for other in range(2):
        group = groups[clip_of(place, half) ^ other]
        spread = tap_matrix(group)
        for kind in range(2):
            for head in range(heads):
                high, low = split(taps_ref[head, kind])
                factors[kind, head * size : (head + 1) * size, :] = dot_tn(high, spread) + dot_tn(
                    low, spread
                )
        total = None
        for which in range(2):
            for kind in range(2):
                bank = banks[2 * other + which][0, kind].astype(f_type)
                high, low = split(bank * factors[kind])
                products[2 * kind * width : (2 * kind + 1) * width, :] = high
                products[(2 * kind + 1) * width : (2 * kind + 2) * width, :] = low
            part = dot(products[...], slot_matrix(which, group))
            total = part if total is None else total + part
        for kind in range(2):
            start = 2 * kind * width
            outs[other][kind] = (
                total[start : start + width] + total[start + width : start + 2 * width]
            ).astype(b_type)


def bank_spec(width, half, other, which):
    def where(step, place, rows_ref, groups):
        return rows_ref[clip_of(place, half) ^ other, which], 0, 0, 0

    return pl.BlockSpec((1, 2, width, clip_rows), where)


def bank_specs(width, half):
    return [bank_spec(width, half, other, which) for other in range(2) for which in range(2)]


def whole_spec(shape):
    return pl.BlockSpec(shape, lambda *_: (0,) * len(shape))


def compress(half, scalars, bank, taps, after=()):
    width = bank.shape[2]
    shape = (2, width, slot_rows)
    return pl.pallas_call(
        functools.partial(compress_kernel, half),
        out_shape=(jax.ShapeDtypeStruct(shape, b_type),) * 2,
        grid_spec=pltpu.PrefetchScalarGridSpec(
            num_scalar_prefetch=3,
            grid=(1,),
            in_specs=bank_specs(width, half)
            + [whole_spec(taps.shape)]
            + [pl.BlockSpec(memory_space=pl.ANY)] * len(after),
            out_specs=(whole_spec(shape),) * 2,
            scratch_shapes=[
                pltpu.VMEM((4 * width, clip_rows), b_type),
                pltpu.VMEM((2, width, clip_rows), f_type),
            ],
        ),
        compiler_params=pltpu.CompilerParams(vmem_limit_bytes=vmem_whole),
        cost_estimate=pl.CostEstimate(
            flops=5 * 10**10, bytes_accessed=15 * 10**7, transcendentals=0
        ),
        name="compress",
    )(*scalars, *([bank] * 4), taps, *after)


def compress_back_kernel(rows, heads, size, half, place, rows_ref, groups, *refs):
    banks, grads, out_ref, products = refs[:4], refs[4:6], refs[-2], refs[-1]
    width = grads[0].shape[1]
    total = None
    for other in range(2):
        group = groups[clip_of(place, half) ^ other]
        grad = grads[other][...].reshape(2 * width, slot_rows)
        taps = tap_matrix(group)
        for which in range(2):
            spread = dot_nt(grad, slot_matrix(which, group))
            for kind in range(2):
                bank = banks[2 * other + which][0, kind].astype(f_type)
                high, low = split(bank * spread[kind * width : (kind + 1) * width])
                products[2 * kind * width : (2 * kind + 1) * width, :] = high
                products[(2 * kind + 1) * width : (2 * kind + 2) * width, :] = low
            part = dot_nt(taps, products[...])
            total = part if total is None else total + part
    out_ref[...] = jnp.zeros(out_ref.shape, f_type)
    for head in range(heads):
        for part in range(2):
            start = 8 * (2 * head + part)
            at = 2 * part * width + head * size
            out_ref[start : start + 8, 0:size] = (
                total[:, at : at + size] + total[:, at + width : at + width + size]
            )


def compress_back(rows, heads, size, half, scalars, bank, grad_here, grad_other, after=()):
    width = bank.shape[2]
    return pl.pallas_call(
        functools.partial(compress_back_kernel, rows, heads, size, half),
        out_shape=jax.ShapeDtypeStruct((16 * heads, 128), f_type),
        grid_spec=pltpu.PrefetchScalarGridSpec(
            num_scalar_prefetch=3,
            grid=(1,),
            in_specs=bank_specs(width, half)
            + [whole_spec((2, width, slot_rows))] * 2
            + [pl.BlockSpec(memory_space=pl.ANY)] * len(after),
            out_specs=whole_spec((16 * heads, 128)),
            scratch_shapes=[pltpu.VMEM((4 * width, clip_rows), b_type)],
        ),
        compiler_params=pltpu.CompilerParams(vmem_limit_bytes=vmem_bytes),
        cost_estimate=pl.CostEstimate(
            flops=5 * 10**10, bytes_accessed=15 * 10**7, transcendentals=0
        ),
        name="compress_back",
    )(*scalars, *([bank] * 4), grad_here, grad_other, *after)


def normal_rows(values):
    centered = values - jnp.mean(values, axis=-1, keepdims=True)
    inverse = lax.rsqrt(jnp.mean(centered * centered, axis=-1, keepdims=True) + eps_norm)
    return centered * inverse, inverse


def norm_back(normal, inverse, grad, gain):
    scaled = grad * gain
    return inverse * (
        scaled
        - jnp.mean(scaled, axis=-1, keepdims=True)
        - normal * jnp.mean(scaled * normal, axis=-1, keepdims=True)
    )


def column_sum(values):
    return jnp.sum(values, axis=0, keepdims=True)


def add_pieces(mine, others):
    total = mine[...]
    for other in others:
        total = total + other[0].astype(f_type)
    return total


def second_norm_kernel(half, rows_ref, mine, *refs):
    others = refs[: half - 1]
    bias, gain, shift, mid_ref, out_ref = refs[half - 1 :]
    midway = rows_ref[...].astype(f_type) + (add_pieces(mine, others) + vector(bias))
    mid_ref[...] = midway
    normal, _ = normal_rows(midway)
    out_ref[...] = (normal * vector(gain) + vector(shift)).astype(b_type)


def second_back_kernel(half, mid_ref, mine, *refs):
    others = refs[: half - 1]
    top_ref, gain, d_mid_ref, d_low_ref, sums_ref = refs[half - 1 :]
    normal, inverse = normal_rows(mid_ref[...])
    grad = add_pieces(mine, others)
    top = top_ref[...].astype(f_type)
    d_mid = top + norm_back(normal, inverse, grad, vector(gain))
    d_mid_ref[...] = d_mid
    d_low = d_mid.astype(b_type)
    d_low_ref[...] = d_low
    put_row(sums_ref, 0, column_sum(d_low.astype(f_type)))
    put_row(sums_ref, 8, column_sum(grad * normal))
    put_row(sums_ref, 16, column_sum(grad))
    put_row(sums_ref, 24, column_sum(top))


def first_back_kernel(half, rows_ref, d_mid_ref, gain, mine, *refs):
    others = refs[: half - 1]
    refs = refs[half - 1 :]
    mid_ref, down_bias, mlp_mine = refs[:3]
    mlp_others = refs[3 : 2 + half]
    sums, comp, out_ref, y_ref, late = refs[2 + half :]
    late[0:48, :] = sums[...]
    late[48:, :] = comp[...]
    normal, inverse = normal_rows(rows_ref[...].astype(f_type))
    grad = add_pieces(mine, others)
    out_ref[...] = d_mid_ref[...] + norm_back(normal, inverse, grad, vector(gain))
    y_ref[...] = (mid_ref[...] + add_pieces(mlp_mine, mlp_others) + vector(down_bias)).astype(b_type)


def close_kernel(rows, heads, size, place, *refs):
    halves, late = refs[:2], refs[2]
    w_qkv, w_proj, pool, table, bias, comp, whole, small = refs[3:]
    width = heads * size
    side = 2 * width
    core = core_of(place)
    for step in range(2):
        whole[core ^ step] = halves[step][...]
    w_qkv[0:side, :] = whole[0, 0:side, :].astype(f_type)
    w_qkv[side:, :] = whole[1, 0:width, :].astype(f_type)
    w_proj[...] = whole[1, width:side, :].astype(f_type)
    for line in range(2 * rows.width):
        column = 128 * (line % rows.width)
        small[32 * line : 32 * line + 32, :] = whole[
            line // rows.width, side : side + 32, column : column + 128
        ].astype(f_type)
    for head in range(heads):
        for part in range(3):
            start = 32 * (3 * head + part)
            for tap in range(27):
                pool[part, tap, head : head + 1, :] = small[start + tap : start + tap + 1, 0:size]
        start = rows.table + 48 * head
        for slot in range(41):
            table[slot, head : head + 1, :] = small[start + slot : start + slot + 1, 0:size]
        for part in range(2):
            start = rows.comp + 8 * (2 * head + part)
            comp[head, part] = late[start : start + 8, 0:size]
    bias[...] = small[rows.bias : rows.bias + rows.units, :]


def error_function(values):
    x = jnp.clip(values, -4.0, 4.0)
    y = x * x
    top = -2.72614225801306e-10
    for term in (
        2.77068142495902e-08,
        -2.10102402082508e-06,
        -5.69250639462346e-05,
        -7.34990630326855e-04,
        -2.95459980854025e-03,
        -1.60960333262415e-02,
    ):
        top = top * y + term
    low = -1.45660718464996e-05
    for term in (
        -2.13374055278905e-04,
        -1.68282697438203e-03,
        -7.37332916720468e-03,
        -1.42647390514189e-02,
    ):
        low = low * y + term
    return x * top / low


def mlp_kernel(rows, half, flip, part, place, *refs):
    pieces, tops = refs[:half], refs[half : 2 * half]
    refs = refs[2 * half :]
    up, down = refs[:2]
    halves = refs[2:4]
    (
        bias, small, y_mine, y_other, d_mine, d_other,
        left_keep, right_keep, left_send, right_send, sums,
        tokens_all, top_all, far, y_all, d_all,
    ) = refs[4:]
    put_halves(far, place, halves)
    ups = halves[0].shape[0]
    count = pieces[0].shape[0]
    tokens = jnp.concatenate([piece[...].astype(f_type) for piece in pieces], axis=0).astype(b_type)
    top = jnp.concatenate([piece[...].astype(f_type) for piece in tops], axis=0).astype(b_type)
    units = down.shape[0]
    y_all[...] = jnp.zeros(y_all.shape, f_type)
    d_all[...] = jnp.zeros(d_all.shape, f_type)
    even = core_of(place) == 0
    for block in range(2):
        first = up if block == 0 else far.at[0:ups]
        second = down if block == 0 else far.at[ups : 2 * ups]
        shift = wide_row(bias, 0, rows.units) if block == 0 else wide_row(small, rows.bias, rows.units)
        for start in range(0, units, part):
            here = slice(start, start + part)
            if flip:
                hidden = dot_nt(tokens, first[here, :]) + shift[:, here]
            else:
                hidden = dot(tokens, first[:, here]) + shift[:, here]
            half_slope = 0.5 * (1.0 + error_function(hidden * (0.5**0.5)))
            slope = half_slope + hidden * jnp.exp(-0.5 * hidden * hidden) * 0.3989422804014327
            act = (hidden * half_slope).astype(b_type)
            d_hid = (dot_nt(top, second[here, :]) * slope).astype(b_type)
            put_row(sums, 8 * block + start // 128, column_sum(d_hid.astype(f_type)))
            y_all[...] += dot(act, second[here, :])
            if flip:
                d_all[...] += dot(d_hid, first[here, :])
            else:
                d_all[...] += dot_nt(d_hid, first[:, here])

            def store(keep, send, here=here, act=act, d_hid=d_hid, block=block):
                keep[0 if flip else 1][block, :, here] = d_hid
                send[0][block, :, here] = act

            @pl.when(even)
            def _():
                store((left_keep, right_keep), (left_send, right_send))

            @pl.when(jnp.logical_not(even))
            def _():
                store((left_send, right_send), (left_keep, right_keep))

        def fixed(keep, send, block=block):
            keep[1 if flip else 0][block] = tokens
            send[1][block] = top

        @pl.when(even)
        def _():
            fixed((left_keep, right_keep), (left_send, right_send))

        @pl.when(jnp.logical_not(even))
        def _():
            fixed((left_send, right_send), (left_keep, right_keep))

    y_mine[...] = y_all[0:count, :]
    d_mine[...] = d_all[0:count, :]
    for step in range(1, half):
        span = slice(step * count, (step + 1) * count)
        y_other[step - 1] = y_all[span, :].astype(b_type)
        d_other[step - 1] = d_all[span, :].astype(b_type)


def mlp(rows, flip, place, pieces, tops, up, down, chunks, bias, small, after=()):
    half = len(pieces)
    count, model = pieces[0].shape
    total = half * count
    units = down.shape[0]
    part = units
    left = ((2, total, units if flip else model), b_type)
    down_left = ((2, total, units), b_type)
    right = ((2, total, model), b_type)
    assert left == down_left
    return call(
        functools.partial(mlp_kernel, rows, half, flip, part),
        "mlp",
        12,
        (
            ((count, model), f_type),
            ((half - 1, count, model), b_type),
            ((count, model), f_type),
            ((half - 1, count, model), b_type),
            left,
            right,
            left,
            right,
            ((16, 128), f_type),
        ),
        (place,),
        (*pieces, *tops, up, down, *chunks, bias, small),
        scratch=(
            pltpu.VMEM((total, model), b_type),
            pltpu.VMEM((total, model), b_type),
            pltpu.VMEM((2 * chunks[0].shape[0], model), b_type),
            pltpu.VMEM((total, model), f_type),
            pltpu.VMEM((total, model), f_type),
        ),
        after=after,
    )


def product_kernel(left, right, out_ref):
    for k in range(2):
        out_ref[k] = lax.dot_general(
            left[k], right[k], (((0,), (0,)), ((), ())), preferred_element_type=f_type
        ).astype(b_type)


def product(left, right, after=()):
    shape = (2, left.shape[2], right.shape[2])
    return call(product_kernel, "product", 4, ((shape, b_type),), (), (left, right), after=after)[0]


def product_cut_kernel(quad, place, left, right, came, *refs):
    outs, total = refs[:-1], refs[-1]
    seat = seat_in(place[1], quad)
    size = outs[0].shape[1]
    for k in range(2):
        total[...] = dot_tn(left[k], right[k])
        for step, out in enumerate(outs):
            rows = pl.ds(aligned((seat ^ step) * size, size), size)
            part = total[rows, :].astype(b_type).astype(f_type)
            out[k] = (part + came[k, rows, :].astype(f_type)).astype(out.dtype)


def pick_kernel(count, eighth, *refs):
    sources, out_ref, sem = refs[:count], refs[-2], refs[-1]
    rows = out_ref.shape[0]
    start = 0
    for source in sources:
        parts = source.shape[0] // rows

        @pl.when((eighth[0] >= start) & (eighth[0] < start + parts))
        def _(source=source, start=start):
            copy = pltpu.make_async_copy(
                source.at[pl.ds(aligned((eighth[0] - start) * rows, rows), rows), :], out_ref, sem
            )
            copy.start()
            copy.wait()

        start += parts


def pick(eighth, sources, after=()):
    rows = sum(item.shape[0] for item in sources) // 8
    return pl.pallas_call(
        functools.partial(pick_kernel, len(sources)),
        out_shape=jax.ShapeDtypeStruct((rows, sources[0].shape[1]), b_type),
        in_specs=[pl.BlockSpec(memory_space=pltpu.SMEM)]
        + [pl.BlockSpec(memory_space=pl.ANY)] * (len(sources) + len(after)),
        out_specs=pl.BlockSpec(memory_space=pltpu.VMEM),
        scratch_shapes=[pltpu.SemaphoreType.DMA],
        cost_estimate=pl.CostEstimate(flops=10**10, bytes_accessed=10**7, transcendentals=0),
        name="pick",
    )(eighth, *sources, *after)


def add_kernel(*refs):
    total = refs[0][...].astype(f_type)
    for item in refs[1:-1]:
        total = total + item[...].astype(f_type)
    refs[-1][...] = total.astype(refs[-1].dtype)


def powers(count):
    return [1 << place for place in range(count.bit_length() - 1)]


def add_wide(values, after=()):
    return call(add_kernel, "add", 1, ((values[0].shape, f_type),), (), values, after=after)[0]


def add_low(values, after=()):
    return call(add_kernel, "add", 1, ((values[0].shape, b_type),), (), values, after=after)[0]


def seat_in(spot, quad):
    low, high = (bit.bit_length() - 1 for bit in quad)
    return ((spot >> low) & 1) + 2 * ((spot >> high) & 1)


def cut_kernel(quad, count, place, *refs):
    values, outs = refs[:count], refs[count:]
    seat = seat_in(place[1], quad)
    size = outs[0].shape[-2]
    for step, out in enumerate(outs):
        rows = pl.ds(aligned((seat ^ step) * size, size), size)
        total = None
        for item in values:
            part = (item[:, rows, :] if len(item.shape) == 3 else item[rows, :]).astype(f_type)
            total = part if total is None else total + part
        out[...] = total.astype(out.dtype)


def add_both_kernel(first, *refs):
    for values, out in ((refs[:first], refs[-2]), (refs[first:-2], refs[-1])):
        total = values[0][...].astype(f_type)
        for item in values[1:]:
            total = total + item[...].astype(f_type)
        out[...] = total.astype(out.dtype)


def add_both(one, two, after=()):
    return call(
        functools.partial(add_both_kernel, len(one)),
        "add_both",
        2,
        ((one[0].shape, b_type), (two[0].shape, b_type)),
        (),
        (*one, *two),
        after=after,
    )


def sum_kernel(*refs):
    mine, came, kept, sent = refs[0], refs[1:-2], refs[-2], refs[-1]
    total = mine[...]
    for item in came:
        total = total + item[...].astype(f_type)
    kept[...] = total[0]
    sent[...] = total[1].astype(b_type)


def sum_pair(values, after=()):
    shape = values[0].shape[1:]
    return call(sum_kernel, "sum", 2, ((shape, f_type), (shape, b_type)), (), values, after=after)


def swap_pairs(count, bit):
    return [(place, place ^ bit) for place in range(count)]


class Team:
    def __init__(self, heads_count, clips_count):
        self.total = heads_count
        self.half = heads_count // 2
        self.clips = clips_count
        self.here = lax.axis_index("head")
        self.clip = self.here // self.half
        self.seat = self.here % self.half
        self.spot = lax.axis_index("clip")
        self.place = jnp.stack([self.here, self.spot])

    def partner(self, values):
        return lax.ppermute(values, "head", swap_pairs(self.total, self.half))

    def seats(self, values, step):
        return lax.ppermute(values, "head", swap_pairs(self.total, step))

    def swap(self, values, bit):
        return lax.ppermute(values, "clip", swap_pairs(self.clips, bit))

    def gather(self, rows):
        return [rows] + [self.seats(rows, step) for step in range(1, self.half)]

    def scatter(self, others):
        return [self.seats(others[step - 1 : step], step) for step in range(1, self.half)]

    def eighth(self):
        return (self.spot & 1) * 4 + self.seat_in((2, 4))

    def share(self, came):
        mine = self.collect(came, (2, 4))
        return [mine, self.swap(mine, 1)]

    def quads(self):
        bit, found = 2, []
        while bit < self.clips:
            found.append((bit, 2 * bit))
            bit *= 4
        return found

    def seat_in(self, quad):
        return seat_in(self.spot, quad)

    def peer(self, values, quad, step):
        return self.swap(values, (step & 1) * quad[0] + (step >> 1) * quad[1])

    def cut(self, values, quad, after=()):
        size = values[0].shape[-2] // 4
        if size % 16 == 0:
            shape = (*values[0].shape[:-2], size, values[0].shape[-1])
            return call(
                functools.partial(cut_kernel, quad, len(values)),
                "cut",
                2,
                ((shape, f_type),) + ((shape, b_type),) * 3,
                (self.place,),
                values,
                after=after,
            )
        seat = self.seat_in(quad)

        def quarter(place):
            total = None
            for item in values:
                part = lax.dynamic_slice_in_dim(item, place * size, size, axis=-2).astype(f_type)
                total = part if total is None else total + part
            return total

        return [quarter(seat)] + [quarter(seat ^ step).astype(b_type) for step in (1, 2, 3)]

    def product_cut(self, left, right, came, after=()):
        quad = self.quads()[0]
        rows, columns = left.shape[2], right.shape[2]
        size = rows // 4
        if size % 16:
            return self.cut([product(left, right, after), came], quad)
        shape = (2, size, columns)
        return call(
            functools.partial(product_cut_kernel, quad),
            "product_cut",
            6,
            ((shape, f_type),) + ((shape, b_type),) * 3,
            (self.place,),
            (left, right, came),
            scratch=(pltpu.VMEM((rows, columns), f_type),),
            after=after,
        )

    def join(self, pieces, quad):
        seat = self.seat_in(quad)
        return jnp.concatenate(
            [lax.select_n((seat ^ place).astype(jnp.int32), *pieces) for place in range(4)], axis=0
        )

    def reduce_further(self, values, start=0, after=()):
        quads = self.quads()
        sent = tuple(values)
        for index in range(start, len(quads) + 1):
            quad = quads[index - 1]
            values = [values[0]] + [self.peer(values[step], quad, step) for step in (1, 2, 3)]
            if index < len(quads):
                values = self.cut(values, quads[index], after)
        return values, sent

    def collect(self, chunk, quad):
        pieces = [chunk] + [self.peer(chunk, quad, step) for step in (1, 2, 3)]
        return self.join(pieces, quad)

    def reduce(self, keep, send, after=()):
        values, sent = [keep, self.swap(send, 1)], ()
        for quad in self.quads():
            values = self.cut(values, quad, after)
            sent = sent or tuple(values)
            values = [values[0]] + [self.peer(values[step], quad, step) for step in (1, 2, 3)]
        return values, sent

    def finish(self, chunk):
        for quad in reversed(self.quads()):
            chunk = self.collect(chunk, quad)
        return chunk, self.swap(chunk, 1)


def add(values):
    total = values[0].astype(f_type)
    for item in values[1:]:
        total = total + item.astype(f_type)
    return total


def on_device(
    heads_total,
    clips_total,
    inputs,
    ln1_gain,
    ln1_bias,
    w_qkv,
    pool_kernel,
    rel_table,
    comp_kernel,
    memory_bank,
    mem_index,
    clip_group,
    w_proj,
    proj_bias,
    ln2_gain,
    ln2_bias,
    w_up,
    up_bias,
    w_down,
    down_bias,
    cotangent,
):
    team = Team(heads_total, clips_total)
    half = team.half
    heads, _, size = rel_table.shape
    count, model = inputs.shape
    units = w_up.shape[1]
    width = heads * size
    rows = Rows(heads, units, model)
    flip = units != model
    lined = [
        item.reshape(model // 128, 128)
        for item in (ln1_gain, ln1_bias, proj_bias, ln2_gain, ln2_bias, down_bias)
    ]
    gain1, shift1, bias_proj, gain2, shift2, bias_down = lined
    bias_up = up_bias.reshape(units // 128, 128)
    w_qkv = w_qkv.T
    if flip:
        w_up = w_up.T
    bank = memory_bank.transpose(0, 1, 3, 2)
    place = team.place
    scalars = (place, mem_index, clip_group)

    given = team.gather(inputs)
    eighth = team.eighth().reshape(1).astype(jnp.int32)
    chunk_a = pick(eighth, (w_qkv, w_proj))
    came_a = team.partner(chunk_a)
    mem_here, mem_there = compress(half, scalars, bank, comp_kernel, after=(chunk_a,))
    mem_far = team.partner(mem_there)
    pooled_here, small, came_a, top, *tokens1 = pool_forward(
        rows,
        heads,
        size,
        place,
        given,
        (w_qkv,),
        (pool_kernel.transpose(1, 2, 0, 3), rel_table.transpose(1, 0, 2), bias_up),
        norm=(gain1, shift1),
        passed=(came_a, cotangent),
        after=(mem_here,),
    )
    small_far = team.partner(small)
    chunks_a = team.share(came_a)
    tops = team.gather(top)
    chunk_b = pick(eighth, (w_up, w_down), after=(pooled_here,))
    came_b = team.partner(chunk_b)
    chunks_b = team.share(came_b)
    branch, probs_here, heads_here = attend(
        rows, heads, size, half, place, clip_group, small, mem_here, pooled_here, w_proj,
        after=(mem_far, chunk_b),
    )
    pooled_far, weights = pool_forward(
        rows, heads, size, place, tokens1, chunks_a, (small_far,), after=(branch,)
    )
    branch, branch_other, probs_far, heads_far = attend(
        rows, heads, size, half, place, clip_group, small_far, mem_far, pooled_far, weights,
        branch, after=(came_b, *tops),
    )
    weights_here, weights_far = (w_qkv, w_proj), (weights,)
    branch_came = team.scatter(branch_other)
    midway, norm2 = call(
        functools.partial(second_norm_kernel, half),
        "second_norm",
        2,
        (((count, model), f_type), ((count, model), b_type)),
        (),
        (inputs, branch, *branch_came, bias_proj, gain2, shift2),
    )
    tokens2 = team.gather(norm2)
    y, y_other, d_norm2, d_norm2_other, left_k, right_k, left_s, right_s, d_bias = mlp(
        rows, flip, place, tokens2, tops, w_up, w_down, chunks_b, bias_up, small_far
    )
    d_norm2_came = team.scatter(d_norm2_other)
    send_m = product(left_s, right_s)
    d_mid, d_branch, sums2 = call(
        functools.partial(second_back_kernel, half),
        "second_back",
        3,
        (((count, model), f_type), ((count, model), b_type), ((32, 128), f_type)),
        (),
        (midway, d_norm2, *d_norm2_came, cotangent, gain2),
        after=(send_m,),
    )
    d_branches = team.gather(d_branch)
    cut_m = team.product_cut(left_k, right_k, team.swap(send_m, 1), after=(d_branch,))
    sums_m, sent_m = team.reduce_further(cut_m, 1)
    y_came = team.scatter(y_other)

    d_pooled, d_mem_far, d_table, d_proj = scores_back(
        rows, heads, size, place, d_branches, weights_far, small_far, mem_far, pooled_far,
        probs_far, heads_far, after=(*sent_m, *y_came),
    )
    d_mem_back = team.partner(d_mem_far)
    d_norm1, keep_f, send_f = pool_back(
        rows, heads, size, place, tokens1, weights_far, small_far, d_pooled, d_table, d_proj,
        d_bias[8:16],
    )
    d_pooled, d_mem_here, d_table, d_proj = scores_back(
        rows, heads, size, place, d_branches, weights_here, small, mem_here, pooled_here,
        probs_here, heads_here, after=(d_norm1,),
    )
    sum_m, part_m = sum_pair(sums_m, after=(d_pooled,))
    came_m = team.partner(part_m)
    sums_f, sent_f = team.reduce(keep_f, send_f, after=(part_m,))
    d_norm1, d_norm1_other, sums, keep_o, send_o = pool_back(
        rows, heads, size, place, tokens1, weights_here, small, d_pooled, d_table, d_proj,
        d_bias[0:8], late=(d_norm1, sums2, *given), after=(*sent_f, d_mem_back),
    )
    part_f, chunk_m = add_both(sums_f, [sum_m, came_m], after=(keep_o,))
    came_f = team.partner(part_f)
    d_norm1_came = team.scatter(d_norm1_other)
    halves_m = team.finish(chunk_m)
    g_comp = compress_back(
        rows, heads, size, half, scalars, bank, d_mem_here, d_mem_back, after=(keep_o,)
    )
    sums_o, sent_o = team.reduce(keep_o, send_o, after=(g_comp,))
    chunk_o = add([*sums_o, came_f]).astype(b_type)
    halves_o = team.finish(chunk_o)
    grad_inputs, output, late = call(
        functools.partial(first_back_kernel, half),
        "first_back",
        3,
        (((count, model), f_type), ((count, model), b_type), ((rows.late, 128), f_type)),
        (),
        (
            inputs, d_mid, gain1, d_norm1, *d_norm1_came, midway, bias_down, y, *y_came,
            sums, g_comp,
        ),
        after=sent_o,
    )
    late = late + team.swap(late, 1)
    for quad in team.quads():
        late = add([late] + [team.peer(late, quad, step) for step in (1, 2, 3)])
    sums = late[:48]
    sums = add([sums] + [team.seats(sums, step) for step in range(1, team.total)])
    odd = core_of((0, team.spot)) != 0
    g_up = jnp.where(odd, halves_m[1], halves_m[0]).astype(f_type)
    g_down = jnp.where(odd, halves_m[0], halves_m[1]).astype(f_type)
    g_qkv, g_proj, g_pool, g_rel, g_bias, g_comp = call(
        functools.partial(close_kernel, rows, heads, size),
        "close",
        3,
        (
            ((3 * width, model), f_type),
            ((width, model), f_type),
            ((3, 27, heads, size), f_type),
            ((41, heads, size), f_type),
            ((units // 128, 128), f_type),
            ((heads, 2, 8, size), f_type),
        ),
        (place,),
        (*halves_o, late),
        scratch=(
            pltpu.VMEM((2, 2 * width + rows.extra, model), b_type),
            pltpu.VMEM((rows.used, 128), f_type),
        ),
    )
    if flip:
        g_up = g_up.T

    def total(index):
        return sums[8 * index : 8 * index + model // 128].reshape(model)

    return (
        output,
        grad_inputs,
        total(4),
        total(5),
        g_qkv.T,
        g_pool.transpose(2, 0, 1, 3),
        g_rel.transpose(1, 0, 2),
        g_comp,
        g_proj,
        total(0),
        total(1),
        total(2),
        g_up,
        g_bias.reshape(units),
        g_down,
        total(3),
    )


def solution(mesh):
    return jax.shard_map(
        functools.partial(on_device, mesh.shape["head"], mesh.shape["clip"]),
        mesh=mesh,
        in_specs=(
            P(("clip", "head"), None),
            P(),
            P(),
            P(None, "head"),
            P("head", None, None, None),
            P("head", None, None),
            P("head", None, None, None),
            P("clip", None, None, "head"),
            P("clip", None),
            P("clip"),
            P("head", None),
            P(),
            P(),
            P(),
            P(None, "head"),
            P("head"),
            P("head", None),
            P(),
            P(("clip", "head"), None),
        ),
        out_specs=(
            P(("clip", "head"), None),
            P(("clip", "head"), None),
            P(),
            P(),
            P(None, "head"),
            P("head", None, None, None),
            P("head", None, None),
            P("head", None, None, None),
            P("head", None),
            P(),
            P(),
            P(),
            P(None, "head"),
            P("head"),
            P("head", None),
            P(),
        ),
        check_vma=False,
    )
```

```python
import functools

import jax
import jax.numpy as jnp
from jax import lax
from jax.experimental import pallas as pl
from jax.experimental.pallas import tpu as pltpu
from jax.sharding import PartitionSpec as P

f_type = jnp.float32
b_type = jnp.bfloat16
eps_norm = 1e-06
neg_large = -1000000000.0
clip_rows = 392
grid_rows = 448
slot_rows = 448
vmem_bytes = 28 * 1024 * 1024
vmem_whole = 56 * 1024 * 1024


def dot(a, b):
    return jnp.dot(a, b, preferred_element_type=f_type)


def dot_nt(a, b):
    return lax.dot_general(a, b, (((1,), (1,)), ((), ())), preferred_element_type=f_type)


def dot_tn(a, b):
    return lax.dot_general(a, b, (((0,), (0,)), ((), ())), preferred_element_type=f_type)


def iota(shape, axis):
    return lax.broadcasted_iota(jnp.int32, shape, axis)


def one_hot(flag):
    return jnp.where(flag, 1.0, 0.0).astype(b_type)


def split(values):
    high = values.astype(b_type)
    return high, (values - high.astype(f_type)).astype(b_type)


def aligned(start, step):
    return pl.multiple_of(start, step)


def call(kernel, name, cost, results, scalars, arrays, scratch=(), after=(), room=vmem_bytes):
    def body(*refs):
        kept = refs[: len(scalars) + len(arrays)]
        kernel(*kept, *refs[len(kept) + len(after) :])

    return pl.pallas_call(
        body,
        out_shape=tuple(jax.ShapeDtypeStruct(shape, kind) for shape, kind in results),
        in_specs=[pl.BlockSpec(memory_space=pltpu.SMEM)] * len(scalars)
        + [pl.BlockSpec(memory_space=pltpu.VMEM)] * len(arrays)
        + [pl.BlockSpec(memory_space=pl.ANY)] * len(after),
        out_specs=tuple(pl.BlockSpec(memory_space=pltpu.VMEM) for _ in results),
        scratch_shapes=list(scratch),
        compiler_params=pltpu.CompilerParams(vmem_limit_bytes=room),
        cost_estimate=pl.CostEstimate(
            flops=int(cost * 1e10), bytes_accessed=int(cost * 3e7), transcendentals=0
        ),
        name=name,
    )(*scalars, *arrays, *after)


def spread_matrix(start, count):
    row = iota((grid_rows, count), 0)
    place = row & 7
    return one_hot(
        ((row >> 3) * 7 + place - start == iota((grid_rows, count), 1)) & (place < 7)
    )


def gather_matrix(start, count):
    row = iota((count, grid_rows), 1)
    place = row & 7
    return one_hot(
        ((row >> 3) * 7 + place - start == iota((count, grid_rows), 0)) & (place < 7)
    )


def to_grid(seat, pieces):
    total = None
    for step, piece in enumerate(pieces):
        rows = piece.shape[0]
        part = dot(spread_matrix((seat ^ step) * rows, rows), piece[...])
        total = part if total is None else total + part
    return total.astype(b_type)


def row_coords(shape, axis):
    row = iota(shape, axis)
    line = row >> 3
    frame = (line * 37) >> 8
    return frame, line - frame * 7, row & 7


def coord_of(kind, coords):
    frame, line, place = coords
    return jnp.where(kind == 0, frame, jnp.where(kind == 1, line, place))


def query_mask():
    shape = (grid_rows, 192)
    column = iota(shape, 1)
    coord = coord_of(column >> 6, row_coords(shape, 0))
    return jnp.where(((column >> 3) & 7) == coord, 1.0, 0.0)


def key_matrix():
    shape = (192, grid_rows)
    column = iota(shape, 0)
    coord = coord_of(column >> 6, row_coords(shape, 1))
    return one_hot((column & 7) == coord)


def key_places():
    shape = (grid_rows, 192)
    column = iota(shape, 1)
    coord = coord_of(column >> 6, row_coords(shape, 0))
    return one_hot((column & 7) == coord)


def table_slot(column):
    kind = column >> 6
    at_query = (column >> 3) & 7
    at_key = column & 7
    base = jnp.where(kind == 0, 7, jnp.where(kind == 1, 21, 34))
    valid = (kind == 0) | ((at_query < 7) & (at_key < 7))
    return jnp.where(valid, base + at_query - at_key, -1)


def table_matrix():
    return one_hot(table_slot(iota((192, 41), 0)) == iota((192, 41), 1))


def own_bias(shape, axis):
    return jnp.where((iota(shape, axis) & 7) == 7, neg_large, 0.0)


def mem_bias(shape, axis, limit):
    slot = iota(shape, axis)
    line = (slot * 586) >> 15
    return jnp.where((slot - 56 * line < 49) & ((line & 3) < limit), 0.0, neg_large)


def clear_border(field):
    width = field.shape[-1]
    field[:, 0:1] = jnp.zeros((3, 1, 9, 8, width), f_type)
    field[:, 9:10] = jnp.zeros((3, 1, 9, 8, width), f_type)
    field[:, :, 0:1] = jnp.zeros((3, 10, 1, 8, width), f_type)
    field[:, :, 8:9] = jnp.zeros((3, 10, 1, 8, width), f_type)


def fill_field(field, values):
    width = values.shape[-1]
    lines = values.reshape(56, 8, width)
    field[0, 1:9, 1:8] = pltpu.roll(lines, 1, 1).reshape(8, 7, 8, width)
    field[1, 1:9, 1:8] = lines.reshape(8, 7, 8, width)
    field[2, 1:9, 1:8] = pltpu.roll(lines, 7, 1).reshape(8, 7, 8, width)


def convolve(field, taps, result, flip):
    width = field.shape[-1]
    for start in range(0, width, 128):
        lanes = slice(start, min(start + 128, width))

        def frame(t, carry):
            total = jnp.zeros((7, 8, lanes.stop - lanes.start), f_type)
            for dt in range(3):
                for dw in range(3):
                    near = field[dw, t + dt, :, :, lanes]
                    for dh in range(3):
                        tap = dt * 9 + dh * 3 + dw
                        tap = 26 - tap if flip else tap
                        total = total + near[dh : dh + 7] * taps[tap : tap + 1, lanes]
            result[t, :, :, lanes] = total
            return carry

        lax.fori_loop(0, 8, frame, 0, unroll=8)


def tap_grads(field, grads, result):
    width = field.shape[-1]
    for start in range(0, width, 128):
        lanes = slice(start, min(start + 128, width))
        size = lanes.stop - lanes.start

        def frame(t, sums):
            grad = grads[1, t + 1, 1:8, :, lanes]
            sums = list(sums)
            for dt in range(3):
                for dw in range(3):
                    near = field[dw, t + dt, :, :, lanes]
                    for dh in range(3):
                        tap = dt * 9 + dh * 3 + dw
                        sums[tap] = sums[tap] + jnp.sum(near[dh : dh + 7] * grad, axis=0)
            return tuple(sums)

        sums = lax.fori_loop(
            0, 8, frame, tuple(jnp.zeros((8, size), f_type) for _ in range(27)), unroll=8
        )
        for tap in range(27):
            result[tap : tap + 1, lanes] = jnp.sum(sums[tap], axis=0, keepdims=True)


class Rows:
    def __init__(self, heads, units, width):
        self.taps = 0
        self.table = self.taps + 96 * heads
        self.bias = self.table + 48 * heads
        self.weights = self.bias + 8
        self.comp = 48
        self.late = self.comp + 16 * heads
        self.units = units // 128
        self.width = width // 128
        self.extra = 64
        self.used = 32 * self.width * 2
        assert self.weights <= self.used


def wide_row(ref, start, count):
    return jnp.concatenate([ref[start + k : start + k + 1, :] for k in range(count)], axis=1)


def put_row(ref, start, values):
    for k in range(values.shape[1] // 128):
        ref[start + k : start + k + 1, :] = values[:, 128 * k : 128 * k + 128]


def vector(ref):
    return wide_row(ref, 0, ref.shape[0])


def seat_of(place, half):
    return place[0] & (half - 1)


def clip_of(place, half):
    return place[0] >> (half.bit_length() - 1)


def core_of(place):
    return place[1] & 1


def put_halves(whole, place, halves):
    size = halves[0].shape[0]
    for step, item in enumerate(halves):
        whole[pl.ds(aligned((core_of(place) ^ step) * size, size), size), :] = item[...]


def weight_views(refs, width):
    if len(refs) == 2:
        return refs[0], refs[1]
    return refs[0].at[0 : 3 * width], refs[0].at[3 * width : 4 * width]


def pack_small(rows, heads, size, pool, table, bias, small):
    for head in range(heads):
        for part in range(3):
            start = 32 * (3 * head + part)
            for tap in range(27):
                small[start + tap : start + tap + 1, 0:size] = pool[part, tap, head : head + 1, :]
        start = rows.table + 48 * head
        for slot in range(41):
            small[start + slot : start + slot + 1, 0:size] = table[slot, head : head + 1, :]
    small[rows.bias : rows.bias + rows.units, :] = bias[...]


def load_taps(taps, small, heads, size):
    for index in range(3 * heads):
        taps[0:27, index * size : (index + 1) * size] = small[
            32 * index : 32 * index + 27, 0:size
        ]


def pool_forward_kernel(rows, heads, size, half, far, passing, place, *refs):
    refs = list(refs)
    pieces = refs[:half]
    del refs[:half]
    if far:
        halves = refs[:2]
        small, pooled_ref, weights, field, taps, wide = refs[2:]
        put_halves(weights, place, halves)
    else:
        gain, shift, weights, *raw = refs[:6]
        del refs[:6]
        passed = refs[:passing]
        pooled_ref, small, *passed_on = refs[passing : 2 + 2 * passing]
        rows_refs, pieces = pieces, refs[2 + 2 * passing : -3]
        pack_small(rows, heads, size, *raw, small)
        field, taps, wide = refs[-3:]
        for source, out in zip(passed, passed_on):
            out[...] = source[...]
        for source, norm in zip(rows_refs, pieces):
            normal, _ = normal_rows(source[...].astype(f_type))
            norm[...] = (normal * vector(gain) + vector(shift)).astype(b_type)
    width = heads * size
    clear_border(field)
    load_taps(taps, small, heads, size)
    fill_field(
        field, dot_nt(to_grid(seat_of(place, half), pieces), weights[0 : 3 * width, :])
    )
    convolve(field, taps, wide, False)
    filled = (iota((grid_rows, 1), 0) & 7) < 7
    pooled_ref[...] = jnp.where(
        filled, wide[...].reshape(grid_rows, 3 * width), 0.0
    ).astype(b_type)


def pool_forward(rows, heads, size, place, pieces, weights, small, norm=(), passed=(), after=()):
    width = heads * size
    half = len(pieces)
    model = pieces[0].shape[1]
    far = not norm
    return call(
        functools.partial(pool_forward_kernel, rows, heads, size, half, far, len(passed)),
        "pool_forward",
        6,
        (((grid_rows, 3 * width), b_type),)
        + (
            (((4 * width, model), b_type),)
            if far
            else (((rows.weights, 128), f_type),)
            + tuple((piece.shape, b_type) for piece in (*passed, *pieces))
        ),
        (place,),
        (*pieces, *norm, *weights, *small, *passed),
        scratch=(
            pltpu.VMEM((3, 10, 9, 8, 3 * width), f_type),
            pltpu.VMEM((32, 3 * width), f_type),
            pltpu.VMEM((8, 7, 8, 3 * width), f_type),
        ),
        after=after,
        room=vmem_bytes if far else vmem_whole,
    )


def attend_kernel(rows, heads, size, half, far, place, groups, *refs):
    refs = list(refs)
    small, mem, pooled, weights = refs[:4]
    del refs[:4]
    base = refs.pop(0) if far else None
    if far:
        mine_ref, other_ref = refs.pop(0), refs.pop(0)
    else:
        branch_ref = refs.pop(0)
    probs_ref, head_ref, query_wide, key_wide, mem_wide, head_wide = refs
    width = heads * size
    scale = size ** (-0.5)
    seat = seat_of(place, half)
    w_proj = weight_views((weights,), width)[1] if far else weights
    rest = 128 - size
    ones = (iota((grid_rows, rest), 1) == 0).astype(f_type)
    query_wide[:, size:128] = ones.astype(b_type)
    key_wide[:, size:128] = (ones * own_bias((grid_rows, rest), 0)).astype(b_type)
    first = (iota((rest, grid_rows), 0) == 0).astype(f_type)
    limit = 4 >> groups[clip_of(place, half)]
    mem_wide[size:128, :] = (first * mem_bias((rest, grid_rows), 1, limit)).astype(b_type)
    keys_at = key_places()
    key_wide[:, 128:320] = keys_at
    key_wide[:, 320:512] = keys_at
    expand = table_matrix()
    mask = query_mask() * (1.0 / scale)
    for head in range(heads):
        at = 3 * head * size
        lanes = slice(head * size, (head + 1) * size)
        queries = pooled[:, at : at + size]
        values = pooled[:, at + 2 * size : at + 3 * size]
        start = rows.table + 48 * head
        table_high, table_low = split(small[start : start + 41, 0:size])
        rel = dot_nt(queries, dot(expand, table_high).astype(b_type)) + dot_nt(
            queries, dot(expand, table_low).astype(b_type)
        )
        high, low = split(rel * mask)
        query_wide[:, 0:size] = queries
        query_wide[:, 128:320] = high
        query_wide[:, 320:512] = low
        key_wide[:, 0:size] = pooled[:, at + size : at + 2 * size]
        mem_wide[0:size, :] = mem[0, lanes, :]
        own = dot_nt(query_wide[...], key_wide[...])
        far_scores = dot(query_wide[:, 0:128], mem_wide[...])
        top = jnp.maximum(
            jnp.max(own, axis=-1, keepdims=True), jnp.max(far_scores, axis=-1, keepdims=True)
        )
        own = jnp.exp((own - top) * scale)
        far_scores = jnp.exp((far_scores - top) * scale)
        total = jnp.sum(own, axis=-1, keepdims=True) + jnp.sum(far_scores, axis=-1, keepdims=True)
        inverse = 1.0 / total
        own = own * inverse
        far_scores = far_scores * inverse
        probs_ref[head, 0] = own
        probs_ref[head, 1] = far_scores
        attended = dot(own.astype(b_type), values) + dot_nt(
            far_scores.astype(b_type), mem[1, lanes, :]
        )
        head_wide[:, lanes] = attended + queries.astype(f_type)
    head_ref[...] = head_wide[...].astype(b_type)
    count = base.shape[1] if far else branch_ref.shape[1]
    for step in range(half):
        head_out = dot(gather_matrix((seat ^ step) * count, count), head_ref[...]).astype(b_type)
        part = dot(head_out, w_proj[...])
        if not far:
            branch_ref[step] = part
        elif step == 0:
            mine_ref[...] = part + base[0]
        else:
            other_ref[step - 1] = (part + base[step]).astype(b_type)


def attend(rows, heads, size, half, place, groups, small, mem, pooled, weights, base=None, after=()):
    width = heads * size
    model = weights.shape[1]
    count = clip_rows // half
    far = base is not None
    branch = (
        (((count, model), f_type), ((half - 1, count, model), b_type))
        if far
        else (((half, count, model), f_type),)
    )
    return call(
        functools.partial(attend_kernel, rows, heads, size, half, far),
        "attend",
        10,
        branch
        + (((heads, 2, grid_rows, grid_rows), f_type), ((grid_rows, width), b_type)),
        (place, groups),
        (small, mem, pooled, weights) + ((base,) if far else ()),
        scratch=(
            pltpu.VMEM((grid_rows, 512), b_type),
            pltpu.VMEM((grid_rows, 512), b_type),
            pltpu.VMEM((128, grid_rows), b_type),
            pltpu.VMEM((grid_rows, width), f_type),
        ),
        after=after,
    )


def scores_back_kernel(rows, heads, size, half, parts, *refs):
    place = refs[0]
    pieces = refs[1 : 1 + half]
    weights = refs[1 + half : 1 + half + parts]
    (
        small, mem, pooled_ref, probs_ref, head_ref,
        d_pooled, d_mem_ref, d_table_ref, d_proj_ref,
        d_head_ref, d_low_ref, probs_low, d_scores,
    ) = refs[1 + half + parts :]
    width = heads * size
    scale = size ** (-0.5)
    w_proj = weight_views(weights, width)[1]
    d_branch = to_grid(seat_of(place, half), pieces)
    d_head = dot_nt(d_branch, w_proj[...])
    d_head_ref[...] = d_head
    d_low_ref[...] = d_head.astype(b_type)
    expand = table_matrix()
    keys_at = key_matrix()
    mask = query_mask()
    for head in range(heads):
        at = 3 * head * size
        lanes = slice(head * size, (head + 1) * size)
        queries = pooled_ref[:, at : at + size]
        keys = pooled_ref[:, at + size : at + 2 * size]
        values = pooled_ref[:, at + 2 * size : at + 3 * size]
        mem_keys = mem[0, lanes, :]
        mem_values = mem[1, lanes, :]

        d_att = d_low_ref[:, lanes]
        own = probs_ref[head, 0]
        far_probs = probs_ref[head, 1]
        d_own = dot_nt(d_att, values)
        d_far = dot(d_att, mem_values)
        inner = jnp.sum(own * d_own, axis=-1, keepdims=True) + jnp.sum(
            far_probs * d_far, axis=-1, keepdims=True
        )
        d_scores[0] = (own * (d_own - inner)).astype(b_type)
        d_scores[1] = (far_probs * (d_far - inner)).astype(b_type)
        probs_low[0] = own.astype(b_type)
        probs_low[1] = far_probs.astype(b_type)
        d_query = (dot(d_scores[0], keys) + dot_nt(d_scores[1], mem_keys)) * scale
        start = rows.table + 48 * head
        table_high, table_low = split(small[start : start + 41, 0:size])
        rel_high, rel_low = split(dot_nt(d_scores[0], keys_at) * mask)
        wide_high = dot(expand, table_high).astype(b_type)
        wide_low = dot(expand, table_low).astype(b_type)
        d_rel = dot(rel_high, wide_high) + dot(rel_low, wide_high) + dot(rel_high, wide_low)
        d_pooled[:, at : at + size] = d_query + d_head_ref[:, lanes] + d_rel
        queries_t = jnp.transpose(queries.astype(f_type)).astype(b_type)
        d_att_t = jnp.transpose(d_head_ref[:, lanes]).astype(b_type)
        wide_high, wide_low = split(dot(queries_t, rel_high) + dot(queries_t, rel_low))
        d_table = dot(wide_high, expand) + dot(wide_low, expand)
        d_table_ref[48 * head : 48 * head + 41, 0:size] = jnp.transpose(d_table)
        d_pooled[:, at + size : at + 2 * size] = jnp.transpose(dot(queries_t, d_scores[0])) * scale
        d_mem_ref[0, lanes, :] = (dot(queries_t, d_scores[1]) * scale).astype(b_type)
        d_pooled[:, at + 2 * size : at + 3 * size] = jnp.transpose(dot(d_att_t, probs_low[0]))
        d_mem_ref[1, lanes, :] = dot(d_att_t, probs_low[1]).astype(b_type)
    head_t = jnp.transpose(head_ref[...].astype(f_type)).astype(b_type)
    d_proj_ref[...] = dot(head_t, d_branch).astype(b_type)


def scores_back(rows, heads, size, place, pieces, weights, small, mem, pooled, probs, head, after=()):
    width = heads * size
    return call(
        functools.partial(scores_back_kernel, rows, heads, size, len(pieces), len(weights)),
        "scores_back",
        13,
        (
            ((grid_rows, 3 * width), f_type),
            ((2, width, slot_rows), b_type),
            ((48 * heads, 128), f_type),
            ((width, pieces[0].shape[1]), b_type),
        ),
        (place,),
        (*pieces, *weights, small, mem, pooled, probs, head),
        scratch=(
            pltpu.VMEM((grid_rows, width), f_type),
            pltpu.VMEM((grid_rows, width), b_type),
            pltpu.VMEM((2, grid_rows, grid_rows), b_type),
            pltpu.VMEM((2, grid_rows, grid_rows), b_type),
        ),
        after=after,
    )


def pool_back_kernel(rows, heads, size, half, parts, last, *refs):
    place = refs[0]
    pieces = refs[1 : 1 + half]
    weights = refs[1 + half : 1 + half + parts]
    refs = list(refs[1 + half + parts :])
    small, d_pooled, d_table, d_proj, d_bias = refs[:5]
    del refs[:5]
    if last:
        base, sums_early = refs[:2]
        inputs = refs[2 : 2 + half]
        mine_ref, other_ref, sums_ref = refs[2 + half : 5 + half]
        del refs[: 5 + half]
    else:
        norm_ref = refs.pop(0)
    keep_ref, send_ref, field, grads, taps, wide, packed, d_taps, small_grads = refs
    width = heads * size
    seat = seat_of(place, half)
    w_qkv = weight_views(weights, width)[0]
    clear_border(field)
    clear_border(grads)
    load_taps(taps, small, heads, size)
    tokens = to_grid(seat, pieces)
    fill_field(field, dot_nt(tokens, w_qkv[...]))
    fill_field(grads, d_pooled[...])
    convolve(grads, taps, wide, True)
    d_qkv = wide[...].reshape(grid_rows, 3 * width)
    low = d_qkv.astype(b_type)
    count = pieces[0].shape[0]
    gains, shifts = [], []
    for step in range(half):
        part = dot(gather_matrix((seat ^ step) * count, count), low).astype(b_type)
        part = dot(part, w_qkv[...])
        if not last:
            norm_ref[step] = part
            continue
        part = part + base[step]
        if step == 0:
            mine_ref[...] = part
        else:
            other_ref[step - 1] = part.astype(b_type)
        normal, _ = normal_rows(inputs[step][...].astype(f_type))
        gains.append(column_sum(part * normal))
        shifts.append(column_sum(part))
    if last:
        sums_ref[0:32, :] = sums_early[...]
        put_row(sums_ref, 32, sum(gains[1:], gains[0]))
        put_row(sums_ref, 40, sum(shifts[1:], shifts[0]))
    side = 2 * width
    g_qkv = dot(jnp.transpose(d_qkv).astype(b_type), tokens).astype(b_type)
    packed[0, 0:side, :] = g_qkv[0:side]
    packed[1, 0:width, :] = g_qkv[side : 3 * width]
    packed[1, width:side, :] = d_proj[...]
    tap_grads(field, grads, d_taps)
    small_grads[...] = jnp.zeros(small_grads.shape, f_type)
    for index in range(3 * heads):
        small_grads[32 * index : 32 * index + 27, 0:size] = d_taps[
            0:27, index * size : (index + 1) * size
        ]
    for head in range(heads):
        start = rows.table + 48 * head
        small_grads[start : start + 41, 0:size] = d_table[48 * head : 48 * head + 41, 0:size]
    small_grads[rows.bias : rows.bias + rows.units, :] = d_bias[0 : rows.units, :]
    packed[:, side:, :] = jnp.zeros((2, rows.extra, packed.shape[2]), b_type)
    for line in range(2 * rows.width):
        column = 128 * (line % rows.width)
        packed[line // rows.width, side : side + 32, column : column + 128] = small_grads[
            32 * line : 32 * line + 32, :
        ].astype(b_type)
    core = core_of(place)
    keep_ref[...] = packed[core]
    send_ref[...] = packed[1 - core]


def pool_back(rows, heads, size, place, pieces, weights, small, d_pooled, d_table, d_proj, d_bias,
              late=(), after=()):
    width = heads * size
    half = len(pieces)
    count, model = pieces[0].shape
    last = bool(late)
    norm = (
        (((count, model), f_type), ((half - 1, count, model), b_type), ((48, 128), f_type))
        if last
        else (((half, count, model), f_type),)
    )
    return call(
        functools.partial(pool_back_kernel, rows, heads, size, half, len(weights), last),
        "pool_back",
        9,
        norm
        + (
            ((2 * width + rows.extra, model), b_type),
            ((2 * width + rows.extra, model), b_type),
        ),
        (place,),
        (*pieces, *weights, small, d_pooled, d_table, d_proj, d_bias, *late),
        scratch=(
            pltpu.VMEM((3, 10, 9, 8, 3 * width), f_type),
            pltpu.VMEM((3, 10, 9, 8, 3 * width), f_type),
            pltpu.VMEM((32, 3 * width), f_type),
            pltpu.VMEM((8, 7, 8, 3 * width), f_type),
            pltpu.VMEM((2, 2 * width + rows.extra, model), b_type),
            pltpu.VMEM((32, 3 * width), f_type),
            pltpu.VMEM((rows.used, 128), f_type),
        ),
        after=after,
    )


def frame_of(token):
    return (token * 669) >> 15


def tap_matrix(group):
    frame = frame_of(iota((8, clip_rows), 1))
    return one_hot((frame & ((2 << group) - 1)) == iota((8, clip_rows), 0))


def slot_matrix(which, group):
    token = iota((clip_rows, slot_rows), 0)
    slot = iota((clip_rows, slot_rows), 1)
    frame = frame_of(token)
    line = (slot * 586) >> 15
    return one_hot(
        ((line >> 2) == which)
        & ((line & 3) == (frame >> (group + 1)))
        & (slot - 56 * line == token - 49 * frame)
    )


def compress_kernel(half, place, rows_ref, groups, *refs):
    banks, taps_ref = refs[:4], refs[4]
    outs, products, factors = refs[-4:-2], refs[-2], refs[-1]
    heads, _, _, size = taps_ref.shape
    width = heads * size
    for other in range(2):
        group = groups[clip_of(place, half) ^ other]
        spread = tap_matrix(group)
        for kind in range(2):
            for head in range(heads):
                high, low = split(taps_ref[head, kind])
                factors[kind, head * size : (head + 1) * size, :] = dot_tn(high, spread) + dot_tn(
                    low, spread
                )
        total = None
        for which in range(2):
            for kind in range(2):
                bank = banks[2 * other + which][0, kind].astype(f_type)
                high, low = split(bank * factors[kind])
                products[2 * kind * width : (2 * kind + 1) * width, :] = high
                products[(2 * kind + 1) * width : (2 * kind + 2) * width, :] = low
            part = dot(products[...], slot_matrix(which, group))
            total = part if total is None else total + part
        for kind in range(2):
            start = 2 * kind * width
            outs[other][kind] = (
                total[start : start + width] + total[start + width : start + 2 * width]
            ).astype(b_type)


def bank_spec(width, half, other, which):
    def where(step, place, rows_ref, groups):
        return rows_ref[clip_of(place, half) ^ other, which], 0, 0, 0

    return pl.BlockSpec((1, 2, width, clip_rows), where)


def bank_specs(width, half):
    return [bank_spec(width, half, other, which) for other in range(2) for which in range(2)]


def whole_spec(shape):
    return pl.BlockSpec(shape, lambda *_: (0,) * len(shape))


def compress(half, scalars, bank, taps, after=()):
    width = bank.shape[2]
    shape = (2, width, slot_rows)
    return pl.pallas_call(
        functools.partial(compress_kernel, half),
        out_shape=(jax.ShapeDtypeStruct(shape, b_type),) * 2,
        grid_spec=pltpu.PrefetchScalarGridSpec(
            num_scalar_prefetch=3,
            grid=(1,),
            in_specs=bank_specs(width, half)
            + [whole_spec(taps.shape)]
            + [pl.BlockSpec(memory_space=pl.ANY)] * len(after),
            out_specs=(whole_spec(shape),) * 2,
            scratch_shapes=[
                pltpu.VMEM((4 * width, clip_rows), b_type),
                pltpu.VMEM((2, width, clip_rows), f_type),
            ],
        ),
        compiler_params=pltpu.CompilerParams(vmem_limit_bytes=vmem_whole),
        cost_estimate=pl.CostEstimate(
            flops=5 * 10**10, bytes_accessed=15 * 10**7, transcendentals=0
        ),
        name="compress",
    )(*scalars, *([bank] * 4), taps, *after)


def compress_back_kernel(rows, heads, size, half, place, rows_ref, groups, *refs):
    banks, grads, out_ref, products = refs[:4], refs[4:6], refs[-2], refs[-1]
    width = grads[0].shape[1]
    total = None
    for other in range(2):
        group = groups[clip_of(place, half) ^ other]
        grad = grads[other][...].reshape(2 * width, slot_rows)
        taps = tap_matrix(group)
        for which in range(2):
            spread = dot_nt(grad, slot_matrix(which, group))
            for kind in range(2):
                bank = banks[2 * other + which][0, kind].astype(f_type)
                high, low = split(bank * spread[kind * width : (kind + 1) * width])
                products[2 * kind * width : (2 * kind + 1) * width, :] = high
                products[(2 * kind + 1) * width : (2 * kind + 2) * width, :] = low
            part = dot_nt(taps, products[...])
            total = part if total is None else total + part
    out_ref[...] = jnp.zeros(out_ref.shape, f_type)
    for head in range(heads):
        for part in range(2):
            start = 8 * (2 * head + part)
            at = 2 * part * width + head * size
            out_ref[start : start + 8, 0:size] = (
                total[:, at : at + size] + total[:, at + width : at + width + size]
            )


def compress_back(rows, heads, size, half, scalars, bank, grad_here, grad_other, after=()):
    width = bank.shape[2]
    return pl.pallas_call(
        functools.partial(compress_back_kernel, rows, heads, size, half),
        out_shape=jax.ShapeDtypeStruct((16 * heads, 128), f_type),
        grid_spec=pltpu.PrefetchScalarGridSpec(
            num_scalar_prefetch=3,
            grid=(1,),
            in_specs=bank_specs(width, half)
            + [whole_spec((2, width, slot_rows))] * 2
            + [pl.BlockSpec(memory_space=pl.ANY)] * len(after),
            out_specs=whole_spec((16 * heads, 128)),
            scratch_shapes=[pltpu.VMEM((4 * width, clip_rows), b_type)],
        ),
        compiler_params=pltpu.CompilerParams(vmem_limit_bytes=vmem_bytes),
        cost_estimate=pl.CostEstimate(
            flops=5 * 10**10, bytes_accessed=15 * 10**7, transcendentals=0
        ),
        name="compress_back",
    )(*scalars, *([bank] * 4), grad_here, grad_other, *after)


def normal_rows(values):
    centered = values - jnp.mean(values, axis=-1, keepdims=True)
    inverse = lax.rsqrt(jnp.mean(centered * centered, axis=-1, keepdims=True) + eps_norm)
    return centered * inverse, inverse


def norm_back(normal, inverse, grad, gain):
    scaled = grad * gain
    return inverse * (
        scaled
        - jnp.mean(scaled, axis=-1, keepdims=True)
        - normal * jnp.mean(scaled * normal, axis=-1, keepdims=True)
    )


def column_sum(values):
    return jnp.sum(values, axis=0, keepdims=True)


def add_pieces(mine, others):
    total = mine[...]
    for other in others:
        total = total + other[0].astype(f_type)
    return total


def second_norm_kernel(half, rows_ref, mine, *refs):
    others = refs[: half - 1]
    bias, gain, shift, mid_ref, out_ref = refs[half - 1 :]
    midway = rows_ref[...].astype(f_type) + (add_pieces(mine, others) + vector(bias))
    mid_ref[...] = midway
    normal, _ = normal_rows(midway)
    out_ref[...] = (normal * vector(gain) + vector(shift)).astype(b_type)


def second_back_kernel(half, mid_ref, mine, *refs):
    others = refs[: half - 1]
    top_ref, gain, d_mid_ref, d_low_ref, sums_ref = refs[half - 1 :]
    normal, inverse = normal_rows(mid_ref[...])
    grad = add_pieces(mine, others)
    top = top_ref[...].astype(f_type)
    d_mid = top + norm_back(normal, inverse, grad, vector(gain))
    d_mid_ref[...] = d_mid
    d_low = d_mid.astype(b_type)
    d_low_ref[...] = d_low
    put_row(sums_ref, 0, column_sum(d_low.astype(f_type)))
    put_row(sums_ref, 8, column_sum(grad * normal))
    put_row(sums_ref, 16, column_sum(grad))
    put_row(sums_ref, 24, column_sum(top))


def first_back_kernel(half, rows_ref, d_mid_ref, gain, mine, *refs):
    others = refs[: half - 1]
    refs = refs[half - 1 :]
    mid_ref, down_bias, mlp_mine = refs[:3]
    mlp_others = refs[3 : 2 + half]
    sums, comp, out_ref, y_ref, late = refs[2 + half :]
    late[0:48, :] = sums[...]
    late[48:, :] = comp[...]
    normal, inverse = normal_rows(rows_ref[...].astype(f_type))
    grad = add_pieces(mine, others)
    out_ref[...] = d_mid_ref[...] + norm_back(normal, inverse, grad, vector(gain))
    y_ref[...] = (mid_ref[...] + add_pieces(mlp_mine, mlp_others) + vector(down_bias)).astype(b_type)


def close_kernel(rows, heads, size, place, *refs):
    halves, late = refs[:2], refs[2]
    w_qkv, w_proj, pool, table, bias, comp, whole, small = refs[3:]
    width = heads * size
    side = 2 * width
    core = core_of(place)
    for step in range(2):
        whole[core ^ step] = halves[step][...]
    w_qkv[0:side, :] = whole[0, 0:side, :].astype(f_type)
    w_qkv[side:, :] = whole[1, 0:width, :].astype(f_type)
    w_proj[...] = whole[1, width:side, :].astype(f_type)
    for line in range(2 * rows.width):
        column = 128 * (line % rows.width)
        small[32 * line : 32 * line + 32, :] = whole[
            line // rows.width, side : side + 32, column : column + 128
        ].astype(f_type)
    for head in range(heads):
        for part in range(3):
            start = 32 * (3 * head + part)
            for tap in range(27):
                pool[part, tap, head : head + 1, :] = small[start + tap : start + tap + 1, 0:size]
        start = rows.table + 48 * head
        for slot in range(41):
            table[slot, head : head + 1, :] = small[start + slot : start + slot + 1, 0:size]
        for part in range(2):
            start = rows.comp + 8 * (2 * head + part)
            comp[head, part] = late[start : start + 8, 0:size]
    bias[...] = small[rows.bias : rows.bias + rows.units, :]


def error_function(values):
    x = jnp.clip(values, -4.0, 4.0)
    y = x * x
    top = -2.72614225801306e-10
    for term in (
        2.77068142495902e-08,
        -2.10102402082508e-06,
        -5.69250639462346e-05,
        -7.34990630326855e-04,
        -2.95459980854025e-03,
        -1.60960333262415e-02,
    ):
        top = top * y + term
    low = -1.45660718464996e-05
    for term in (
        -2.13374055278905e-04,
        -1.68282697438203e-03,
        -7.37332916720468e-03,
        -1.42647390514189e-02,
    ):
        low = low * y + term
    return x * top / low


def mlp_kernel(rows, half, flip, part, place, *refs):
    pieces, tops = refs[:half], refs[half : 2 * half]
    refs = refs[2 * half :]
    up, down = refs[:2]
    halves = refs[2:4]
    (
        bias, small, y_mine, y_other, d_mine, d_other,
        left_keep, right_keep, left_send, right_send, sums,
        tokens_all, top_all, far, y_all, d_all,
    ) = refs[4:]
    put_halves(far, place, halves)
    ups = halves[0].shape[0]
    count = pieces[0].shape[0]
    tokens = jnp.concatenate([piece[...].astype(f_type) for piece in pieces], axis=0).astype(b_type)
    top = jnp.concatenate([piece[...].astype(f_type) for piece in tops], axis=0).astype(b_type)
    units = down.shape[0]
    y_all[...] = jnp.zeros(y_all.shape, f_type)
    d_all[...] = jnp.zeros(d_all.shape, f_type)
    even = core_of(place) == 0
    for block in range(2):
        first = up if block == 0 else far.at[0:ups]
        second = down if block == 0 else far.at[ups : 2 * ups]
        shift = wide_row(bias, 0, rows.units) if block == 0 else wide_row(small, rows.bias, rows.units)
        for start in range(0, units, part):
            here = slice(start, start + part)
            if flip:
                hidden = dot_nt(tokens, first[here, :]) + shift[:, here]
            else:
                hidden = dot(tokens, first[:, here]) + shift[:, here]
            half_slope = 0.5 * (1.0 + error_function(hidden * (0.5**0.5)))
            slope = half_slope + hidden * jnp.exp(-0.5 * hidden * hidden) * 0.3989422804014327
            act = (hidden * half_slope).astype(b_type)
            d_hid = (dot_nt(top, second[here, :]) * slope).astype(b_type)
            put_row(sums, 8 * block + start // 128, column_sum(d_hid.astype(f_type)))
            y_all[...] += dot(act, second[here, :])
            if flip:
                d_all[...] += dot(d_hid, first[here, :])
            else:
                d_all[...] += dot_nt(d_hid, first[:, here])

            def store(keep, send, here=here, act=act, d_hid=d_hid, block=block):
                keep[0 if flip else 1][block, :, here] = d_hid
                send[0][block, :, here] = act

            @pl.when(even)
            def _():
                store((left_keep, right_keep), (left_send, right_send))

            @pl.when(jnp.logical_not(even))
            def _():
                store((left_send, right_send), (left_keep, right_keep))

        def fixed(keep, send, block=block):
            keep[1 if flip else 0][block] = tokens
            send[1][block] = top

        @pl.when(even)
        def _():
            fixed((left_keep, right_keep), (left_send, right_send))

        @pl.when(jnp.logical_not(even))
        def _():
            fixed((left_send, right_send), (left_keep, right_keep))

    y_mine[...] = y_all[0:count, :]
    d_mine[...] = d_all[0:count, :]
    for step in range(1, half):
        span = slice(step * count, (step + 1) * count)
        y_other[step - 1] = y_all[span, :].astype(b_type)
        d_other[step - 1] = d_all[span, :].astype(b_type)


def mlp(rows, flip, place, pieces, tops, up, down, chunks, bias, small, after=()):
    half = len(pieces)
    count, model = pieces[0].shape
    total = half * count
    units = down.shape[0]
    part = units
    left = ((2, total, units if flip else model), b_type)
    down_left = ((2, total, units), b_type)
    right = ((2, total, model), b_type)
    assert left == down_left
    return call(
        functools.partial(mlp_kernel, rows, half, flip, part),
        "mlp",
        12,
        (
            ((count, model), f_type),
            ((half - 1, count, model), b_type),
            ((count, model), f_type),
            ((half - 1, count, model), b_type),
            left,
            right,
            left,
            right,
            ((16, 128), f_type),
        ),
        (place,),
        (*pieces, *tops, up, down, *chunks, bias, small),
        scratch=(
            pltpu.VMEM((total, model), b_type),
            pltpu.VMEM((total, model), b_type),
            pltpu.VMEM((2 * chunks[0].shape[0], model), b_type),
            pltpu.VMEM((total, model), f_type),
            pltpu.VMEM((total, model), f_type),
        ),
        after=after,
    )


def product_kernel(left, right, out_ref):
    for k in range(2):
        out_ref[k] = lax.dot_general(
            left[k], right[k], (((0,), (0,)), ((), ())), preferred_element_type=f_type
        ).astype(b_type)


def product(left, right, after=()):
    shape = (2, left.shape[2], right.shape[2])
    return call(product_kernel, "product", 4, ((shape, b_type),), (), (left, right), after=after)[0]


def product_cut_kernel(quad, place, left, right, came, *refs):
    outs, total = refs[:-1], refs[-1]
    seat = seat_in(place[1], quad)
    size = outs[0].shape[1]
    for k in range(2):
        total[...] = dot_tn(left[k], right[k])
        for step, out in enumerate(outs):
            rows = pl.ds(aligned((seat ^ step) * size, size), size)
            part = total[rows, :].astype(b_type).astype(f_type)
            out[k] = (part + came[k, rows, :].astype(f_type)).astype(out.dtype)


def pick_kernel(count, eighth, *refs):
    sources, out_ref, sem = refs[:count], refs[-2], refs[-1]
    rows = out_ref.shape[0]
    start = 0
    for source in sources:
        parts = source.shape[0] // rows

        @pl.when((eighth[0] >= start) & (eighth[0] < start + parts))
        def _(source=source, start=start):
            copy = pltpu.make_async_copy(
                source.at[pl.ds(aligned((eighth[0] - start) * rows, rows), rows), :], out_ref, sem
            )
            copy.start()
            copy.wait()

        start += parts


def pick(eighth, sources, after=()):
    rows = sum(item.shape[0] for item in sources) // 8
    return pl.pallas_call(
        functools.partial(pick_kernel, len(sources)),
        out_shape=jax.ShapeDtypeStruct((rows, sources[0].shape[1]), b_type),
        in_specs=[pl.BlockSpec(memory_space=pltpu.SMEM)]
        + [pl.BlockSpec(memory_space=pl.ANY)] * (len(sources) + len(after)),
        out_specs=pl.BlockSpec(memory_space=pltpu.VMEM),
        scratch_shapes=[pltpu.SemaphoreType.DMA],
        cost_estimate=pl.CostEstimate(flops=10**10, bytes_accessed=10**7, transcendentals=0),
        name="pick",
    )(eighth, *sources, *after)


def add_kernel(*refs):
    total = refs[0][...].astype(f_type)
    for item in refs[1:-1]:
        total = total + item[...].astype(f_type)
    refs[-1][...] = total.astype(refs[-1].dtype)


def powers(count):
    return [1 << place for place in range(count.bit_length() - 1)]


def add_wide(values, after=()):
    return call(add_kernel, "add", 1, ((values[0].shape, f_type),), (), values, after=after)[0]


def add_low(values, after=()):
    return call(add_kernel, "add", 1, ((values[0].shape, b_type),), (), values, after=after)[0]


def seat_in(spot, quad):
    low, high = (bit.bit_length() - 1 for bit in quad)
    return ((spot >> low) & 1) + 2 * ((spot >> high) & 1)


def cut_kernel(quad, count, place, *refs):
    values, outs = refs[:count], refs[count:]
    seat = seat_in(place[1], quad)
    size = outs[0].shape[-2]
    for step, out in enumerate(outs):
        rows = pl.ds(aligned((seat ^ step) * size, size), size)
        total = None
        for item in values:
            part = (item[:, rows, :] if len(item.shape) == 3 else item[rows, :]).astype(f_type)
            total = part if total is None else total + part
        out[...] = total.astype(out.dtype)


def add_both_kernel(first, *refs):
    for values, out in ((refs[:first], refs[-2]), (refs[first:-2], refs[-1])):
        total = values[0][...].astype(f_type)
        for item in values[1:]:
            total = total + item[...].astype(f_type)
        out[...] = total.astype(out.dtype)


def add_both(one, two, after=()):
    return call(
        functools.partial(add_both_kernel, len(one)),
        "add_both",
        2,
        ((one[0].shape, b_type), (two[0].shape, b_type)),
        (),
        (*one, *two),
        after=after,
    )


def sum_kernel(*refs):
    mine, came, kept, sent = refs[0], refs[1:-2], refs[-2], refs[-1]
    total = mine[...]
    for item in came:
        total = total + item[...].astype(f_type)
    kept[...] = total[0]
    sent[...] = total[1].astype(b_type)


def sum_pair(values, after=()):
    shape = values[0].shape[1:]
    return call(sum_kernel, "sum", 2, ((shape, f_type), (shape, b_type)), (), values, after=after)


def swap_pairs(count, bit):
    return [(place, place ^ bit) for place in range(count)]


class Team:
    def __init__(self, heads_count, clips_count):
        self.total = heads_count
        self.half = heads_count // 2
        self.clips = clips_count
        self.here = lax.axis_index("head")
        self.clip = self.here // self.half
        self.seat = self.here % self.half
        self.spot = lax.axis_index("clip")
        self.place = jnp.stack([self.here, self.spot])

    def partner(self, values):
        return lax.ppermute(values, "head", swap_pairs(self.total, self.half))

    def seats(self, values, step):
        return lax.ppermute(values, "head", swap_pairs(self.total, step))

    def swap(self, values, bit):
        return lax.ppermute(values, "clip", swap_pairs(self.clips, bit))

    def gather(self, rows):
        return [rows] + [self.seats(rows, step) for step in range(1, self.half)]

    def scatter(self, others):
        return [self.seats(others[step - 1 : step], step) for step in range(1, self.half)]

    def eighth(self):
        return (self.spot & 1) * 4 + self.seat_in((2, 4))

    def share(self, came):
        mine = self.collect(came, (2, 4))
        return [mine, self.swap(mine, 1)]

    def quads(self):
        bit, found = 2, []
        while bit < self.clips:
            found.append((bit, 2 * bit))
            bit *= 4
        return found

    def seat_in(self, quad):
        return seat_in(self.spot, quad)

    def peer(self, values, quad, step):
        return self.swap(values, (step & 1) * quad[0] + (step >> 1) * quad[1])

    def cut(self, values, quad, after=()):
        size = values[0].shape[-2] // 4
        if size % 16 == 0:
            shape = (*values[0].shape[:-2], size, values[0].shape[-1])
            return call(
                functools.partial(cut_kernel, quad, len(values)),
                "cut",
                2,
                ((shape, f_type),) + ((shape, b_type),) * 3,
                (self.place,),
                values,
                after=after,
            )
        seat = self.seat_in(quad)

        def quarter(place):
            total = None
            for item in values:
                part = lax.dynamic_slice_in_dim(item, place * size, size, axis=-2).astype(f_type)
                total = part if total is None else total + part
            return total

        return [quarter(seat)] + [quarter(seat ^ step).astype(b_type) for step in (1, 2, 3)]

    def product_cut(self, left, right, came, after=()):
        quad = self.quads()[0]
        rows, columns = left.shape[2], right.shape[2]
        size = rows // 4
        if size % 16:
            return self.cut([product(left, right, after), came], quad)
        shape = (2, size, columns)
        return call(
            functools.partial(product_cut_kernel, quad),
            "product_cut",
            6,
            ((shape, f_type),) + ((shape, b_type),) * 3,
            (self.place,),
            (left, right, came),
            scratch=(pltpu.VMEM((rows, columns), f_type),),
            after=after,
        )

    def join(self, pieces, quad):
        seat = self.seat_in(quad)
        return jnp.concatenate(
            [lax.select_n((seat ^ place).astype(jnp.int32), *pieces) for place in range(4)], axis=0
        )

    def reduce_further(self, values, start=0, after=()):
        quads = self.quads()
        sent = tuple(values)
        for index in range(start, len(quads) + 1):
            quad = quads[index - 1]
            values = [values[0]] + [self.peer(values[step], quad, step) for step in (1, 2, 3)]
            if index < len(quads):
                values = self.cut(values, quads[index], after)
        return values, sent

    def collect(self, chunk, quad):
        pieces = [chunk] + [self.peer(chunk, quad, step) for step in (1, 2, 3)]
        return self.join(pieces, quad)

    def reduce(self, keep, send, after=()):
        values, sent = [keep, self.swap(send, 1)], ()
        for quad in self.quads():
            values = self.cut(values, quad, after)
            sent = sent or tuple(values)
            values = [values[0]] + [self.peer(values[step], quad, step) for step in (1, 2, 3)]
        return values, sent

    def finish(self, chunk):
        for quad in reversed(self.quads()):
            chunk = self.collect(chunk, quad)
        return chunk, self.swap(chunk, 1)


def add(values):
    total = values[0].astype(f_type)
    for item in values[1:]:
        total = total + item.astype(f_type)
    return total


def on_device(
    heads_total,
    clips_total,
    inputs,
    ln1_gain,
    ln1_bias,
    w_qkv,
    pool_kernel,
    rel_table,
    comp_kernel,
    memory_bank,
    mem_index,
    clip_group,
    w_proj,
    proj_bias,
    ln2_gain,
    ln2_bias,
    w_up,
    up_bias,
    w_down,
    down_bias,
    cotangent,
):
    team = Team(heads_total, clips_total)
    half = team.half
    heads, _, size = rel_table.shape
    count, model = inputs.shape
    units = w_up.shape[1]
    width = heads * size
    rows = Rows(heads, units, model)
    flip = units != model
    lined = [
        item.reshape(model // 128, 128)
        for item in (ln1_gain, ln1_bias, proj_bias, ln2_gain, ln2_bias, down_bias)
    ]
    gain1, shift1, bias_proj, gain2, shift2, bias_down = lined
    bias_up = up_bias.reshape(units // 128, 128)
    w_qkv = w_qkv.T
    if flip:
        w_up = w_up.T
    bank = memory_bank.transpose(0, 1, 3, 2)
    place = team.place
    scalars = (place, mem_index, clip_group)

    given = team.gather(inputs)
    eighth = team.eighth().reshape(1).astype(jnp.int32)
    chunk_a = pick(eighth, (w_qkv, w_proj))
    came_a = team.partner(chunk_a)
    mem_here, mem_there = compress(half, scalars, bank, comp_kernel, after=(chunk_a,))
    mem_far = team.partner(mem_there)
    pooled_here, small, came_a, top, *tokens1 = pool_forward(
        rows,
        heads,
        size,
        place,
        given,
        (w_qkv,),
        (pool_kernel.transpose(1, 2, 0, 3), rel_table.transpose(1, 0, 2), bias_up),
        norm=(gain1, shift1),
        passed=(came_a, cotangent),
        after=(mem_here,),
    )
    small_far = team.partner(small)
    chunks_a = team.share(came_a)
    tops = team.gather(top)
    chunk_b = pick(eighth, (w_up, w_down), after=(pooled_here,))
    came_b = team.partner(chunk_b)
    chunks_b = team.share(came_b)
    branch, probs_here, heads_here = attend(
        rows, heads, size, half, place, clip_group, small, mem_here, pooled_here, w_proj,
        after=(mem_far, chunk_b),
    )
    pooled_far, weights = pool_forward(
        rows, heads, size, place, tokens1, chunks_a, (small_far,), after=(branch,)
    )
    branch, branch_other, probs_far, heads_far = attend(
        rows, heads, size, half, place, clip_group, small_far, mem_far, pooled_far, weights,
        branch, after=(came_b, *tops),
    )
    weights_here, weights_far = (w_qkv, w_proj), (weights,)
    branch_came = team.scatter(branch_other)
    midway, norm2 = call(
        functools.partial(second_norm_kernel, half),
        "second_norm",
        2,
        (((count, model), f_type), ((count, model), b_type)),
        (),
        (inputs, branch, *branch_came, bias_proj, gain2, shift2),
    )
    tokens2 = team.gather(norm2)
    y, y_other, d_norm2, d_norm2_other, left_k, right_k, left_s, right_s, d_bias = mlp(
        rows, flip, place, tokens2, tops, w_up, w_down, chunks_b, bias_up, small_far
    )
    d_norm2_came = team.scatter(d_norm2_other)
    send_m = product(left_s, right_s)
    d_mid, d_branch, sums2 = call(
        functools.partial(second_back_kernel, half),
        "second_back",
        3,
        (((count, model), f_type), ((count, model), b_type), ((32, 128), f_type)),
        (),
        (midway, d_norm2, *d_norm2_came, cotangent, gain2),
        after=(send_m,),
    )
    d_branches = team.gather(d_branch)
    cut_m = team.product_cut(left_k, right_k, team.swap(send_m, 1), after=(d_branch,))
    sums_m, sent_m = team.reduce_further(cut_m, 1)
    y_came = team.scatter(y_other)

    d_pooled, d_mem_far, d_table, d_proj = scores_back(
        rows, heads, size, place, d_branches, weights_far, small_far, mem_far, pooled_far,
        probs_far, heads_far, after=(*sent_m, *y_came),
    )
    d_mem_back = team.partner(d_mem_far)
    d_norm1, keep_f, send_f = pool_back(
        rows, heads, size, place, tokens1, weights_far, small_far, d_pooled, d_table, d_proj,
        d_bias[8:16],
    )
    d_pooled, d_mem_here, d_table, d_proj = scores_back(
        rows, heads, size, place, d_branches, weights_here, small, mem_here, pooled_here,
        probs_here, heads_here, after=(d_norm1,),
    )
    sum_m, part_m = sum_pair(sums_m, after=(d_pooled,))
    came_m = team.partner(part_m)
    sums_f, sent_f = team.reduce(keep_f, send_f, after=(part_m,))
    d_norm1, d_norm1_other, sums, keep_o, send_o = pool_back(
        rows, heads, size, place, tokens1, weights_here, small, d_pooled, d_table, d_proj,
        d_bias[0:8], late=(d_norm1, sums2, *given), after=(*sent_f, d_mem_back),
    )
    part_f, chunk_m = add_both(sums_f, [sum_m, came_m], after=(keep_o,))
    came_f = team.partner(part_f)
    d_norm1_came = team.scatter(d_norm1_other)
    halves_m = team.finish(chunk_m)
    g_comp = compress_back(
        rows, heads, size, half, scalars, bank, d_mem_here, d_mem_back, after=(keep_o,)
    )
    sums_o, sent_o = team.reduce(keep_o, send_o, after=(g_comp,))
    chunk_o = add([*sums_o, came_f]).astype(b_type)
    halves_o = team.finish(chunk_o)
    grad_inputs, output, late = call(
        functools.partial(first_back_kernel, half),
        "first_back",
        3,
        (((count, model), f_type), ((count, model), b_type), ((rows.late, 128), f_type)),
        (),
        (
            inputs, d_mid, gain1, d_norm1, *d_norm1_came, midway, bias_down, y, *y_came,
            sums, g_comp,
        ),
        after=sent_o,
    )
    late = late + team.swap(late, 1)
    for quad in team.quads():
        late = add([late] + [team.peer(late, quad, step) for step in (1, 2, 3)])
    sums = late[:48]
    sums = add([sums] + [team.seats(sums, step) for step in range(1, team.total)])
    odd = core_of((0, team.spot)) != 0
    g_up = jnp.where(odd, halves_m[1], halves_m[0]).astype(f_type)
    g_down = jnp.where(odd, halves_m[0], halves_m[1]).astype(f_type)
    g_qkv, g_proj, g_pool, g_rel, g_bias, g_comp = call(
        functools.partial(close_kernel, rows, heads, size),
        "close",
        3,
        (
            ((3 * width, model), f_type),
            ((width, model), f_type),
            ((3, 27, heads, size), f_type),
            ((41, heads, size), f_type),
            ((units // 128, 128), f_type),
            ((heads, 2, 8, size), f_type),
        ),
        (place,),
        (*halves_o, late),
        scratch=(
            pltpu.VMEM((2, 2 * width + rows.extra, model), b_type),
            pltpu.VMEM((rows.used, 128), f_type),
        ),
    )
    if flip:
        g_up = g_up.T

    def total(index):
        return sums[8 * index : 8 * index + model // 128].reshape(model)

    return (
        output,
        grad_inputs,
        total(4),
        total(5),
        g_qkv.T,
        g_pool.transpose(2, 0, 1, 3),
        g_rel.transpose(1, 0, 2),
        g_comp,
        g_proj,
        total(0),
        total(1),
        total(2),
        g_up,
        g_bias.reshape(units),
        g_down,
        total(3),
    )


def solution(mesh):
    return jax.shard_map(
        functools.partial(on_device, mesh.shape["head"], mesh.shape["clip"]),
        mesh=mesh,
        in_specs=(
            P(("clip", "head"), None),
            P(),
            P(),
            P(None, "head"),
            P("head", None, None, None),
            P("head", None, None),
            P("head", None, None, None),
            P("clip", None, None, "head"),
            P("clip", None),
            P("clip"),
            P("head", None),
            P(),
            P(),
            P(),
            P(None, "head"),
            P("head"),
            P("head", None),
            P(),
            P(("clip", "head"), None),
        ),
        out_specs=(
            P(("clip", "head"), None),
            P(("clip", "head"), None),
            P(),
            P(),
            P(None, "head"),
            P("head", None, None, None),
            P("head", None, None),
            P("head", None, None, None),
            P("head", None),
            P(),
            P(),
            P(),
            P(None, "head"),
            P("head"),
            P("head", None),
            P(),
        ),
        check_vma=False,
    )
```
